128 devices in a mesh: expert: 32 (over z, y, core), shard: 4 (over x).
Axes of the slice: x: 4, y: 4, z: 4, core: 2. Of those that a mesh axis runs over, the one named last changes fastest.
Arguments:
- tokens: bfloat16 [2, 16384, 1024], P(None, ('expert', 'shard')), may hold values from -6 to 6
- cotangent: bfloat16 [2, 16384, 1024], P(None, ('expert', 'shard')), may hold values from -6 to 6
- order: int32 [2, 32, 512], P(None, 'expert'), may hold values from 0 to 511, each once within a row
- lengths: int32 [2, 32, 2], P(None, 'expert'), may hold values from 1 to 448, 512 in all within a row
- routes: int32 [2, 16384, 8], P(None, ('expert', 'shard')), may hold values from 0 to 31, as said below
- gate_weights: float32 [2, 16384, 8], P(None, ('expert', 'shard')), may hold values from 0.06 to 0.2
- capacity: int32 [32], replicated, may hold values from 24 to 48, as said below
- gain_attn: bfloat16 [1024], P('shard'), may hold values from 0.25 to 1.75
- w_query: bfloat16 [1024, 1024], P('shard'), may hold values from -0.1875 to 0.1875
- w_key: bfloat16 [1024, 512], P('shard'), may hold values from -0.1875 to 0.1875
- w_value: bfloat16 [1024, 512], P('shard'), may hold values from -0.1875 to 0.1875
- w_out: bfloat16 [1024, 1024], P('shard'), may hold values from -0.75 to 0.75
- gain_ffn: bfloat16 [1024], P('shard'), may hold values from 0.25 to 1.75
- w_gate: bfloat16 [32, 1024, 512], P('expert', None, 'shard'), may hold values from -0.1875 to 0.1875
- w_up: bfloat16 [32, 1024, 512], P('expert', None, 'shard'), may hold values from -0.1875 to 0.1875
- w_down: bfloat16 [32, 1024, 512], P('expert', None, 'shard'), may hold values from -1 to 1
Outputs:
- block_out: bfloat16 [2, 16384, 1024], P(None, ('expert', 'shard'))
- grad_tokens: bfloat16 [2, 16384, 1024], P(None, ('expert', 'shard'))
- grad_gain_attn: float32 [1024], P('shard')
- grad_query: float32 [1024, 1024], P('shard')
- grad_key: float32 [1024, 512], P('shard')
- grad_value: float32 [1024, 512], P('shard')
- output_weight_gradient: float32 [1024, 1024], P('shard')
- grad_gain_ffn: float32 [1024], P('shard')
- grad_gate: float32 [32, 1024, 512], P('expert', None, 'shard')
- grad_up: float32 [32, 1024, 512], P('expert', None, 'shard')
- grad_down: float32 [32, 1024, 512], P('expert', None, 'shard')
The draws below stay inside these ranges and needn't reach their ends.
Inputs may be any that keep to these rules, and one draw needn't show every extreme that they name: `routes`: each token names 8 different experts; one expert, drawn from the seed, is named by every token and has capacity 48. Pairs of one device beyond an expert's capacity are dropped. Each order[m, g] names every dealt position once.
All inputs are finite; a program needn't handle non-finite values.
Results may differ from the reference program's by a relative error of at most 0.03.
Values may be sent and summed in bfloat16 or wider, within the bound.
No kernel may reach another device: no remote copies, remote signals or barrier semaphores. Data moves between devices by JAX's collectives and lax.ppermute only.
A program may use at most 192 MiB of HBM per device.

```python
import functools
import math
import jax
import jax.numpy as jnp
import numpy as np
from jax import lax

D = 1024
HEADS = 16
KV_HEADS = 8
HEAD = 64
F = 512
SPECIALIST_COUNT = 32
TOPK = 8
TOK = 128
MB = 2
DOCS = 2
CAP = 48
GT = 512
LONGEST = 448
GROUPS = 32
TOKENS = 16384
N_EXPERT = 32
N_SHARD = 4


def expert_ranking(key):
    return jax.random.permutation(key, SPECIALIST_COUNT).astype(jnp.int32)


def draw_routes(key, part):
    specialist_rank_list = expert_ranking(key)
    key = jax.random.fold_in(key, 3)
    noise_perturbation = jax.random.randint(key, (MB, TOKENS, SPECIALIST_COUNT), 0, 65536, dtype=jnp.int32)
    added_reward = jnp.where(specialist_rank_list == 0, 1 << 22, (SPECIALIST_COUNT - specialist_rank_list) * 1024).astype(jnp.int32)
    routing_scores_raw = (noise_perturbation + added_reward[None, None, :]) * 64 + jnp.arange(SPECIALIST_COUNT, dtype=jnp.int32)[None, None, :]
    return lax.top_k(routing_scores_raw, TOPK)[1].astype(jnp.int32)


def draw_capacity(key, part):
    specialist_rank_list = expert_ranking(key)
    key = jax.random.fold_in(key, 5)
    drawn = jax.random.randint(key, (SPECIALIST_COUNT,), CAP // 2, CAP + 1, dtype=jnp.int32)
    return jnp.where(specialist_rank_list == 0, CAP, drawn).astype(jnp.int32)


def block_levels(stream_key, dims, cuts, low, largest):
    factor_of = 1.0
    for position, blocks in cuts:
        steps = jax.random.uniform(jax.random.fold_in(jax.random.fold_in(stream_key, 6), position), (blocks,), jnp.float32, low / len(cuts), largest / len(cuts))
        factor_of = factor_of * jnp.repeat(jnp.exp(steps), dims[position] // blocks).reshape((-1,) + (1,) * (len(dims) - 1 - position))
    return factor_of


def split_up(count, total, reach, slope):
    loads = [(1 << 20) // math.isqrt(rank ** slope) + 1 for rank in range(2, count + 1)]
    rest, given = total - reach - (count - 1), [1] * (count - 1)
    while rest > 0:
        candidates = [i for i in range(count - 1) if given[i] < reach]
        pool, budget = sum([loads[i] for i in candidates]), rest
        for i in candidates:
            more = min(reach - given[i], max(1, budget * loads[i] // pool), rest)
            given[i] = given[i] + more
            rest = rest - more
    return np.array([reach] + given)


def uneven_parts(stream_key, number_of, total, limit, slope):
    if number_of == 2:
        one = jax.random.randint(stream_key, (), max(1, total - limit), min(limit, total - 1) + 1)
        return jnp.stack([one, total - one])
    sizes = jnp.asarray(split_up(number_of, total, limit, slope), jnp.int32)
    pairs = (number_of - 1) // 2
    source_of, sink = sizes[1:1 + 2 * pairs:2], sizes[2:2 + 2 * pairs:2]
    margin = jnp.minimum(source_of - 1, limit - sink)
    moved = jax.random.randint(jax.random.fold_in(stream_key, 1), (pairs,), 0, 1 << 20) % (margin + 1)
    sizes = sizes.at[1:1 + 2 * pairs:2].set(source_of - moved).at[2:2 + 2 * pairs:2].set(sink + moved)
    return sizes[jax.random.permutation(jax.random.fold_in(stream_key, 2), number_of)]


def normal_values(rng, extent, scale, bound, shards=(), kind=jnp.bfloat16):
    values = scale * jax.random.normal(rng, extent, jnp.float32)
    if shards:
        values = values * block_levels(rng, extent, shards, -0.22, 0.18)
    return jnp.clip(values, -bound, bound).astype(kind)


def setup_inputs(seed: int = 0) -> dict:
    splits = jax.random.split(jax.random.key(seed), 17)
    return {
        "tokens": normal_values(splits[0], (MB, TOKENS, D), 1.0, 6.0, ((1, 128),)),
        "cotangent": normal_values(splits[1], (MB, TOKENS, D), 1.0, 6.0, ((1, 128),)),
        "order": jax.vmap(lambda own: jax.random.permutation(own, GT))(jax.random.split(splits[2], MB * GROUPS)).reshape((MB, GROUPS, GT)).astype(jnp.int32),
        "lengths": jax.vmap(lambda own: uneven_parts(own, DOCS, GT, LONGEST, 2))(jax.random.split(splits[3], MB * GROUPS)).reshape((MB, GROUPS, DOCS)).astype(jnp.int32),
        "routes": draw_routes(jax.random.fold_in(splits[16], 71), 0),
        "gate_weights": jnp.clip(jnp.exp(math.log(0.2) - 1.2039728 * jax.random.uniform(splits[5], (MB, TOKENS, TOPK), jnp.float32) ** block_levels(splits[5], (MB, TOKENS, TOPK), ((1, 128),), -0.2, 0.2)), 0.06, 0.2),
        "capacity": draw_capacity(jax.random.fold_in(splits[16], 71), 0),
        "gain_attn": jnp.clip(1.0 + 0.15 * jax.random.normal(splits[7], (D,), jnp.float32), 0.25, 1.75).astype(jnp.bfloat16),
        "w_query": normal_values(splits[8], (D, HEADS * HEAD), D ** -0.5, 0.1875, ((0, 4),)),
        "w_key": normal_values(splits[9], (D, KV_HEADS * HEAD), D ** -0.5, 0.1875, ((0, 4),)),
        "w_value": normal_values(splits[10], (D, KV_HEADS * HEAD), D ** -0.5, 0.1875, ((0, 4),)),
        "w_out": normal_values(splits[11], (HEADS * HEAD, D), (HEADS * HEAD // 16) ** -0.5, 0.75, ((0, 4),)),
        "gain_ffn": jnp.clip(1.0 + 0.15 * jax.random.normal(splits[12], (D,), jnp.float32), 0.25, 1.75).astype(jnp.bfloat16),
        "w_gate": normal_values(splits[13], (SPECIALIST_COUNT, D, F), D ** -0.5, 0.1875, ((0, 32), (2, 4))),
        "w_up": normal_values(splits[14], (SPECIALIST_COUNT, D, F), D ** -0.5, 0.1875, ((0, 32), (2, 4))),
        "w_down": normal_values(splits[15], (SPECIALIST_COUNT, D, F), (F // 16) ** -0.5, 1.0, ((0, 32), (2, 4))),
    }


eps_norm = 1e-05
masked_score = -1e+30

@jax.custom_vjp
def low(v):
    return lax.optimization_barrier(v.astype(jnp.bfloat16)).astype(jnp.float32)

@jax.custom_vjp
def low_back(v):
    return v

def low_keep(v):
    return (low(v), None)

def low_pass(kept, grad):
    return (grad,)

def back_keep(v):
    return (v, None)

def back_low(kept, grad):
    return (low(grad),)
low.defvjp(low_keep, low_pass)
low_back.defvjp(back_keep, back_low)

def precise(left, right):
    return jnp.dot(left, right, precision=lax.Precision.HIGHEST)

def normed(rows, gain):
    return rows * lax.rsqrt(lax.optimization_barrier(jnp.mean(rows * rows, axis=-1, keepdims=True)) + eps_norm) * gain

def document_ids(lengths_row):
    doc_ends = jnp.cumsum(lengths_row).astype(jnp.int32)
    positions = jnp.arange(GT, dtype=jnp.int32)
    return lax.optimization_barrier(jnp.sum((positions[:, None] >= doc_ends[None, :-1]).astype(jnp.int32), axis=1)).astype(jnp.int32)

def inverse_order(order_row):
    return jnp.zeros((GT,), jnp.int32).at[order_row].set(jnp.arange(GT, dtype=jnp.int32))

def take_rows(rows, index_row):
    return rows[index_row]

def attend_group(pieces):
    queries, keys, values, documents = pieces
    share_count = HEADS // KV_HEADS
    grouped_queries = queries.reshape(GT, KV_HEADS, share_count, HEAD)
    grouped_keys = keys.reshape(GT, KV_HEADS, HEAD)
    grouped_values = values.reshape(GT, KV_HEADS, HEAD)
    routing_scores_raw = jnp.einsum('qgrd,kgd->grqk', grouped_queries, grouped_keys, precision=lax.Precision.HIGHEST)
    routing_scores_raw = low_back(routing_scores_raw * HEAD ** (-0.5))
    same_doc = documents[:, None] == documents[None, :]
    routing_scores_raw = jnp.where(same_doc[None, None], routing_scores_raw, masked_score)
    probs = jax.nn.softmax(routing_scores_raw, axis=-1)
    mixed = jnp.einsum('grqk,kgd->qgrd', low(probs), grouped_values, precision=lax.Precision.HIGHEST)
    return mixed.reshape(GT, HEADS * HEAD)

def expert_rows(capacity, w_gate, w_up, w_down, pieces):
    rows, routes_rows, gates_rows = pieces
    chosen = routes_rows.reshape(TOK * TOPK)
    hits = (chosen[:, None] == jnp.arange(SPECIALIST_COUNT, dtype=jnp.int32)[None, :]).astype(jnp.int32)
    ranks = lax.optimization_barrier(jnp.sum(hits * (jnp.cumsum(hits, axis=0).astype(jnp.int32) - 1), axis=1)).astype(jnp.int32)
    limits = lax.optimization_barrier(jnp.sum(hits * capacity[None, :], axis=1)).astype(jnp.int32)
    slots = jnp.where(ranks < limits, chosen * CAP + ranks, SPECIALIST_COUNT * CAP).astype(jnp.int32)
    pair_rows = (jnp.arange(TOK * TOPK, dtype=jnp.int32) // TOPK).astype(jnp.int32)
    owning_experts = jnp.full((SPECIALIST_COUNT * CAP,), TOK, jnp.int32).at[slots].set(pair_rows, mode='drop')
    padded = jnp.concatenate([rows, jnp.zeros((1, D), jnp.float32)], axis=0)
    buffer = low_back(padded[owning_experts].reshape(SPECIALIST_COUNT, CAP, D))
    gate_proj = low_back(jnp.einsum('ecd,edf->ecf', buffer, w_gate, precision=lax.Precision.HIGHEST))
    up_proj = low_back(jnp.einsum('ecd,edf->ecf', buffer, w_up, precision=lax.Precision.HIGHEST))
    hidden = low(jax.nn.silu(gate_proj) * up_proj)
    result = jnp.einsum('ecf,edf->ecd', hidden, w_down, precision=lax.Precision.HIGHEST)
    result = low(low_back(result)).reshape(SPECIALIST_COUNT * CAP, D)
    result = jnp.concatenate([result, jnp.zeros((1, D), jnp.float32)], axis=0)
    picked = result[slots].reshape(TOK, TOPK, D)
    return lax.optimization_barrier(jnp.sum(picked * gates_rows[:, :, None], axis=1))

def forward(order_mb, lengths_mb, routes_mb, gates_mb, capacity, given, gain_attn, w_query, w_key, w_value, w_out, gain_ffn, w_gate, w_up, w_down):
    grouped = given.reshape(GROUPS, GT, D)
    dealt = jax.vmap(take_rows)(grouped, order_mb).reshape(TOKENS, D)
    attn_in = low(normed(dealt, gain_attn))
    queries = low(low_back(precise(attn_in, w_query)))
    keys = low(low_back(precise(attn_in, w_key)))
    values = low(low_back(precise(attn_in, w_value)))
    documents = jax.vmap(document_ids)(lengths_mb)
    mixed = lax.map(jax.checkpoint(attend_group), (queries.reshape(GROUPS, GT, HEADS * HEAD), keys.reshape(GROUPS, GT, KV_HEADS * HEAD), values.reshape(GROUPS, GT, KV_HEADS * HEAD), documents))
    mixed = low(low_back(mixed.reshape(TOKENS, HEADS * HEAD)))
    middle = dealt + low_back(precise(mixed, w_out))
    ffn_in = low(normed(middle, gain_ffn))
    device_count = N_EXPERT * N_SHARD
    expert_part = functools.partial(expert_rows, capacity, w_gate, w_up, w_down)
    mixture = lax.map(jax.checkpoint(expert_part), (ffn_in.reshape(device_count, TOK, D), routes_mb.reshape(device_count, TOK, TOPK), gates_mb.reshape(device_count, TOK, TOPK)))
    total = (middle + mixture.reshape(TOKENS, D)).reshape(GROUPS, GT, D)
    inverse = jax.vmap(inverse_order)(order_mb)
    return jax.vmap(take_rows)(total, inverse).reshape(TOKENS, D)

def reference(tokens, cotangent, order, lengths, routes, gate_weights, capacity, gain_attn, w_query, w_key, w_value, w_out, gain_ffn, w_gate, w_up, w_down):
    params = tuple((weight.astype(jnp.float32) for weight in (gain_attn, w_query, w_key, w_value, w_out, gain_ffn, w_gate, w_up, w_down)))
    totals = tuple((jnp.zeros(weight.shape, jnp.float32) for weight in params))
    outputs = []
    input_grads = []
    for micro_index in range(MB):
        forward_micro = functools.partial(forward, order[micro_index], lengths[micro_index], routes[micro_index], gate_weights[micro_index], capacity)
        result, pullback = jax.vjp(forward_micro, tokens[micro_index].astype(jnp.float32), *params)
        gradients = pullback(cotangent[micro_index].astype(jnp.float32))
        outputs.append(result.astype(jnp.bfloat16))
        input_grads.append(gradients[0].astype(jnp.bfloat16))
        totals = tuple((total + gradient for total, gradient in zip(totals, gradients[1:])))
    return (jnp.stack(outputs), jnp.stack(input_grads), totals[0], totals[1], totals[2], totals[3], totals[4], totals[5], totals[6], totals[7], totals[8])
```

```python
import functools

import jax
import jax.numpy as jnp
from jax import lax
from jax.experimental import pallas as pl
from jax.experimental.pallas import tpu as pltpu
from jax.sharding import PartitionSpec as P

D = 1024
HEADS = 16
KV_HEADS = 8
HEAD = 64
F = 512
EXPERTS = 32
TOPK = 8
CAP = 48
TOK = 128
GT = 512
SHARDS = 4
SLOTS = EXPERTS * CAP
HEADS_HERE = HEADS // SHARDS
KV_HERE = KV_HEADS // SHARDS
QC = HEADS_HERE * HEAD
KC = KV_HERE * HEAD
COLS = QC + 2 * KC
ROWS_HERE = D // SHARDS

EPS = 1e-05
MASKED = -1e30
SCALE = HEAD ** (-0.5)

BF = jnp.bfloat16
F32 = jnp.float32
I32 = jnp.int32

VMEM = pl.BlockSpec(memory_space=pltpu.VMEM)
SMEM = pl.BlockSpec(memory_space=pltpu.SMEM)


def dot(a, b, ca=1, cb=0):
    return lax.dot_general(a, b, (((ca,), (cb,)), ((), ())), preferred_element_type=F32)


def shape(dims, dtype):
    return jax.ShapeDtypeStruct(dims, dtype)


def run(name, body, outs, ins, smem=(), flops=0, size=0, scratch=(), limit=56):
    return pl.pallas_call(
        body,
        out_shape=outs,
        in_specs=[SMEM if i in smem else VMEM for i in range(len(ins))],
        out_specs=[VMEM] * len(outs),
        scratch_shapes=list(scratch),
        compiler_params=pltpu.CompilerParams(vmem_limit_bytes=limit * 1024 * 1024),
        cost_estimate=pl.CostEstimate(flops=flops, bytes_accessed=size, transcendentals=0),
        name=name,
    )(*ins)


def iota(dims, axis):
    return lax.broadcasted_iota(I32, dims, axis)


def rolled_order(order_ref, x):
    rows = [(order_ref[pl.ds((x + k) & 3, 1), :] - TOK * x) & (GT - 1) for k in range(SHARDS)]
    return jnp.concatenate(rows, axis=1)


def given_by_dealt(order_ref, x, rows=GT):
    return jnp.where(iota((rows, GT), 0) == rolled_order(order_ref, x), 1.0, 0.0).astype(BF)


def stack(refs):
    return jnp.concatenate([r[...] for r in refs], axis=0)


def same_documents(x, first_length):
    across = ((iota((GT, GT), 1) + TOK * x) & (GT - 1)) >= first_length
    down = ((iota((GT, GT), 0) + TOK * x) & (GT - 1)) >= first_length
    return jnp.logical_not(jnp.logical_xor(across, down))


def pack_body(place, wq, wk, wv, ga, gf, *outs):
    x = place[0]
    gains = jnp.concatenate([ga[...], gf[...]], axis=1)
    for k in range(SHARDS):
        s = (x - k) & 3
        outs[k][0:ROWS_HERE, 0:QC] = wq[:, pl.ds(pl.multiple_of(s * QC, QC), QC)]
        outs[k][0:ROWS_HERE, QC : QC + KC] = wk[:, pl.ds(pl.multiple_of(s * KC, KC), KC)]
        outs[k][0:ROWS_HERE, QC + KC : COLS] = wv[:, pl.ds(pl.multiple_of(s * KC, KC), KC)]
        outs[k][ROWS_HERE : ROWS_HERE + 16, :] = jnp.broadcast_to(gains, (16, 2 * ROWS_HERE))


def unpack_body(place, p0, p1, p2, p3, w_out, gains_out):
    x = place[0]
    packs = (p0, p1, p2, p3)
    for k in range(SHARDS):
        s = (x + k) & 3
        w_out[pl.ds(pl.multiple_of(s * ROWS_HERE, ROWS_HERE), ROWS_HERE), :] = packs[k][
            0:ROWS_HERE, :
        ]
    rows = [p[ROWS_HERE : ROWS_HERE + 16, :].astype(F32)[0:8] for p in packs]
    for half in range(2):
        for b in range(SHARDS):
            total = jnp.zeros((8, ROWS_HERE), F32)
            for k in range(SHARDS):
                piece = rows[k][:, half * ROWS_HERE : (half + 1) * ROWS_HERE]
                total = jnp.where(((x + k) & 3) == b, piece, total)
            gains_out[half * 8 : half * 8 + 8, b * ROWS_HERE : (b + 1) * ROWS_HERE] = total


def route_body(place, order, c0, c1, c2, c3, routes, gates, cap, c01_ref, chi_ref, clo_ref, d01_ref, slot_ref, dy_ref):
    x = place[0]
    dealt_by_given = given_by_dealt(order, x)[:, 0:TOK]
    dy = dot(dealt_by_given, stack((c0, c1, c2, c3)), 0, 0).astype(BF)
    dy_ref[...] = dy
    named = iota((TOK, EXPERTS), 1)
    hits = jnp.zeros((TOK, EXPERTS), F32)
    weight = jnp.zeros((TOK, EXPERTS), F32)
    for k in range(TOPK):
        hit = routes[:, k : k + 1] == named
        hits = jnp.where(hit, 1.0, hits)
        weight = jnp.where(hit, gates[:, k : k + 1], weight)
    earlier = jnp.where(iota((TOK, TOK), 1) < iota((TOK, TOK), 0), 1.0, 0.0).astype(BF)
    ranks = dot(earlier, hits.astype(BF))
    kept = jnp.logical_and(hits > 0.0, ranks < cap[...].astype(F32))
    place_of = jnp.where(kept, ranks, -1.0).astype(BF)
    first = iota((EXPERTS, SLOTS), 0) * CAP
    slot = iota((EXPERTS, SLOTS), 1)
    spread = jnp.where(jnp.logical_and(slot >= first, slot < first + CAP), 1.0, 0.0).astype(BF)
    within = (iota((TOK, SLOTS), 1) % CAP).astype(F32)
    own = dot(place_of, spread) == within
    c01_ref[...] = jnp.where(own, 1.0, 0.0).astype(BF)
    high = weight.astype(BF)
    low = (weight - high.astype(F32)).astype(BF)
    chi_ref[...] = jnp.where(own, dot(high, spread), 0.0).astype(BF)
    clo_ref[...] = jnp.where(own, dot(low, spread), 0.0).astype(BF)
    within_t = (iota((SLOTS, TOK), 0) % CAP).astype(F32)
    own_t = dot(spread, place_of, 0, 1) == within_t
    d01 = jnp.where(own_t, 1.0, 0.0).astype(BF)
    d01_ref[...] = d01
    gate_t = jnp.where(own_t, dot(spread, high, 0, 1) + dot(spread, low, 0, 1), 0.0)
    gate_of = jnp.sum(gate_t, axis=1, keepdims=True)
    slot_ref[...] = (dot(d01, dy) * gate_of).astype(BF)


def attend_body(
    place, order, t0, t1, t2, t3, w, gains, wo, o0, o1, o2, o3, dealt_ref, xr_ref, qkv_ref, mixed_ref, mass_ref
):
    x, first_length = place[0], place[1]
    deal = given_by_dealt(order, x)
    dealt = dot(deal, stack((t0, t1, t2, t3)), 0, 0)
    dealt_ref[...] = dealt[0:TOK].astype(BF)
    scaled = dealt * lax.rsqrt(jnp.mean(dealt * dealt, axis=-1, keepdims=True) + EPS)
    xr_ref[...] = scaled.astype(BF)
    attn_in = (scaled * gains[0:1, :]).astype(BF)
    qkv = dot(attn_in, w[...]).astype(BF)
    qkv_ref[...] = qkv
    same = same_documents(x, first_length)
    heads = []
    masses = []
    for h in range(HEADS_HERE):
        g = h // (HEADS // KV_HEADS)
        q = qkv[:, h * HEAD : (h + 1) * HEAD]
        k = qkv[:, QC + g * HEAD : QC + (g + 1) * HEAD]
        v = qkv[:, QC + KC + g * HEAD : QC + KC + (g + 1) * HEAD]
        scores = jnp.where(same, dot(q, k, 1, 1) * SCALE, MASKED)
        highest = jnp.max(scores, axis=-1, keepdims=True)
        raised = jnp.exp(scores - highest)
        total = jnp.sum(raised, axis=-1, keepdims=True)
        probs = (raised * (1.0 / total)).astype(BF)
        heads.append(dot(probs, v).astype(BF))
        masses.append(jnp.broadcast_to(highest + jnp.log(total), (GT, 32)))
    mixed = jnp.concatenate(heads, axis=1)
    mixed_ref[...] = mixed
    mass_ref[...] = jnp.concatenate(masses, axis=1)
    part = dot(mixed, wo[...]).astype(BF)
    for k, out in enumerate((o0, o1, o2, o3)):
        out[...] = part[k * TOK : (k + 1) * TOK]


def leave_body(own, r1, r2, r3, dealt, gains, d01, middle_ref, rows_ref):
    middle = dealt[...].astype(F32) + (
        (own[...].astype(F32) + r1[...].astype(F32)) + (r2[...].astype(F32) + r3[...].astype(F32))
    )
    middle_ref[...] = middle
    r = lax.rsqrt(jnp.mean(middle * middle, axis=-1, keepdims=True) + EPS)
    ffn_in = (middle * r * gains[8:9, :]).astype(BF)
    rows_ref[...] = dot(d01[...], ffn_in).astype(BF)


TILE = 256


def expert_body(last, *refs):
    refs = list(refs)
    rows, grads = refs[:2]
    blocks = refs[2:6]
    refs = refs[6:]
    prev = None
    if last:
        prev, refs = refs[0], refs[1:]
    out_ref, back_ref = refs[:2]
    if last:
        own_ref, sends, (wg, wu, wd, acc) = refs[2], refs[3:6], refs[6:]
    else:
        sums_ref, (wg, wu, wd, acc) = refs[2], refs[3:]
    step = pl.program_id(0)

    @pl.when(step == 0)
    def _():
        for k in range(SHARDS):
            at = slice(k * 128, (k + 1) * 128)
            wg[:, at] = blocks[k][0]
            wu[:, at] = blocks[k][1]
            wd[:, at] = blocks[k][2]
        acc[...] = prev[...] if last else jnp.zeros(acc.shape, F32)

    row = rows[...]
    grad = grads[...]
    gate = dot(row, wg[...])
    up = dot(row, wu[...])
    sig = jax.nn.sigmoid(gate)
    silu = gate * sig
    hidden = (silu * up).astype(BF)
    out_ref[...] = dot(hidden, wd[...], 1, 1).astype(BF)
    grad_hidden = dot(grad, wd[...])
    grad_gate = (grad_hidden * up * sig * (1.0 + gate * (1.0 - sig))).astype(BF)
    grad_up = (grad_hidden * silu).astype(BF)
    back_ref[...] = (dot(grad_gate, wg[...], 1, 1) + dot(grad_up, wu[...], 1, 1)).astype(BF)
    acc[0] += dot(row, grad_gate, 0, 0)
    acc[1] += dot(row, grad_up, 0, 0)
    acc[2] += dot(grad, hidden, 0, 0)

    @pl.when(step == pl.num_programs(0) - 1)
    def _():
        if last:
            for j in range(3):
                own_ref[j] = acc[j, :, 0:128]
                for k in range(1, SHARDS):
                    sends[k - 1][j] = acc[j, :, k * 128 : (k + 1) * 128].astype(BF)
        else:
            sums_ref[...] = acc[...]


def expert_call(rows, grads, blocks, prev):
    last = prev is not None
    tiles = SLOTS // TILE
    tile = pl.BlockSpec((TILE, D), lambda i: (i, 0))

    def fixed(dims):
        return pl.BlockSpec(dims, lambda i: (0,) * len(dims), pipeline_mode=pl.Buffered(1))

    ins = [rows, grads, *blocks]
    in_specs = [tile, tile] + [fixed((3, D, 128))] * 4
    outs = [shape((SLOTS, D), BF), shape((SLOTS, D), BF)]
    out_specs = [tile, tile]
    if last:
        ins.append(prev)
        in_specs.append(fixed((3, D, F)))
        outs += [shape((3, D, 128), F32)] + [shape((3, D, 128), BF)] * 3
        out_specs += [fixed((3, D, 128))] * 4
    else:
        outs.append(shape((3, D, F), F32))
        out_specs.append(fixed((3, D, F)))
    return pl.pallas_call(
        functools.partial(expert_body, last),
        grid=(tiles,),
        in_specs=in_specs,
        out_specs=out_specs,
        out_shape=outs,
        scratch_shapes=[pltpu.VMEM((D, F), BF)] * 3 + [pltpu.VMEM((3, D, F), F32)],
        compiler_params=pltpu.CompilerParams(
            vmem_limit_bytes=56 * 1024 * 1024, dimension_semantics=("arbitrary",)
        ),
        cost_estimate=pl.CostEstimate(
            flops=18 * SLOTS * D * F, bytes_accessed=8 * SLOTS * D + 20 * D * F, transcendentals=0
        ),
        name="expert",
    )(*ins)


def returned_body(back, c01, middle, gains, dy, branch_ref, gain_ref):
    upstream = dot(c01[...], back[...])
    mid = middle[...]
    r = lax.rsqrt(jnp.mean(mid * mid, axis=-1, keepdims=True) + EPS)
    scaled = upstream * gains[8:9, :]
    grad = r * scaled - mid * (r * r * r) * jnp.mean(scaled * mid, axis=-1, keepdims=True)
    branch_ref[...] = (dy[...].astype(F32) + grad).astype(BF)
    gain_ref[...] = jnp.broadcast_to(jnp.sum(upstream * mid * r, axis=0, keepdims=True), (8, D))


def block_body(back, chi, clo, middle, out_ref):
    mixture = dot(chi[...], back[...]) + dot(clo[...], back[...])
    out_ref[...] = (middle[...] + mixture).astype(BF)


def place_body(place, order, b0, b1, b2, b3, out_ref):
    deal = given_by_dealt(order, place[0], TOK)
    out_ref[...] = dot(deal, stack((b0, b1, b2, b3))).astype(BF)


def attend_back_body(last, place, order, g0, g1, g2, g3, xr, qkv_ref, mixed, mass, w, wo, *refs):
    x, first_length = place[0], place[1]
    if last:
        prev_w, prev_o, gain0, gain1, *refs = refs
    o0, o1, o2, o3, given_ref, *refs = refs
    deal = given_by_dealt(order, x)
    branch = stack((g0, g1, g2, g3))
    given_ref[...] = dot(deal[0:TOK], branch).astype(BF)
    sum_o = dot(mixed[...], branch, 0, 0)
    grad_mixed = dot(branch, wo[...], 1, 1).astype(BF)
    qkv = qkv_ref[...]
    same = same_documents(x, first_length)
    grad_q, grad_k, grad_v = [], [], []
    for g in range(KV_HERE):
        k = qkv[:, QC + g * HEAD : QC + (g + 1) * HEAD]
        v = qkv[:, QC + KC + g * HEAD : QC + KC + (g + 1) * HEAD]
        sum_k = jnp.zeros((HEAD, GT), F32)
        sum_v = jnp.zeros((HEAD, GT), F32)
        for r in range(HEADS // KV_HEADS):
            h = g * (HEADS // KV_HEADS) + r
            q = qkv[:, h * HEAD : (h + 1) * HEAD]
            gm = grad_mixed[:, h * HEAD : (h + 1) * HEAD]
            scores = jnp.where(same, dot(q, k, 1, 1) * SCALE, MASKED)
            probs = jnp.exp(scores - mass[:, h * 32 : h * 32 + 1])
            grad_probs = dot(gm, v, 1, 1)
            sum_v += dot(gm, probs.astype(BF), 0, 0)
            weighted = probs * grad_probs
            grad_scores = weighted - probs * jnp.sum(weighted, axis=-1, keepdims=True)
            grad_scores = grad_scores.astype(BF)
            grad_q.append((dot(grad_scores, k) * SCALE).astype(BF))
            sum_k += dot(q, grad_scores, 0, 0)
        grad_k.append((sum_k * SCALE).astype(BF))
        grad_v.append(sum_v.astype(BF))
    grad_kv = jnp.concatenate(grad_k + grad_v, axis=0).astype(F32).T.astype(BF)
    grad_qkv = jnp.concatenate(grad_q + [grad_kv], axis=1)
    sum_w = dot(xr[...], grad_qkv, 0, 0)
    part = dot(grad_qkv, w[...], 1, 1).astype(BF)
    part = dot(deal, part).astype(BF)
    for k, out in enumerate((o0, o1, o2, o3)):
        out[...] = part[k * TOK : (k + 1) * TOK]
    if not last:
        sum_w_ref, sum_o_ref = refs
        sum_w_ref[...] = sum_w
        sum_o_ref[...] = sum_o
        return
    keep_ref, send_ref, all_w, all_o = refs
    c = place[2]
    all_w[...] = sum_w + prev_w[...]
    all_o[...] = sum_o + prev_o[...]
    gain = gain0[...] + gain1[...]
    for ref, half in ((keep_ref, c), (send_ref, 1 - c)):
        at = pl.ds(pl.multiple_of(half * 256, 256), 256)
        ref[0:D, :] = all_w[:, at].astype(ref.dtype)
        for j in range(2):
            at = pl.ds(pl.multiple_of(j * 512 + half * 256, 256), 256)
            ref[D + j * 256 : D + (j + 1) * 256, :] = all_o[:, at].astype(ref.dtype)
        tile = jnp.concatenate(
            [gain[0:1, b * 256 : (b + 1) * 256] for b in range(4)] + [jnp.zeros((12, 256), F32)], axis=0
        )
        for j in range(16):
            ref[6 * 256 + j * 16 : 6 * 256 + (j + 1) * 16, :] = tile.astype(ref.dtype)


def tokens_body(tokens, p0, p1, p2, p3, given, gains, out_ref):
    upstream = (p0[...].astype(F32) + p1[...].astype(F32)) + (
        p2[...].astype(F32) + p3[...].astype(F32)
    )
    v = tokens[...].astype(F32)
    r = lax.rsqrt(jnp.mean(v * v, axis=-1, keepdims=True) + EPS)
    scaled = upstream * gains[0:1, :]
    grad = r * scaled - v * (r * r * r) * jnp.mean(scaled * v, axis=-1, keepdims=True)
    out_ref[...] = (given[...].astype(F32) + grad).astype(BF)


BLOCKS = 7


def split_y_body(place, keep, got, own_ref, s1, s2, s3):
    y = place[3]
    for b in range(BLOCKS):
        for k, ref in enumerate((own_ref, s1, s2, s3)):
            at = pl.ds(pl.multiple_of(b * 256 + ((y + k) & 3) * 64, 64), 64)
            ref[b * 64 : (b + 1) * 64, :] = (keep[at, :] + got[at, :].astype(F32)).astype(ref.dtype)


def split_z_body(place, own, r1, r2, r3, own_ref, s1, s2, s3):
    z = place[4]
    for b in range(BLOCKS):
        for k, ref in enumerate((own_ref, s1, s2, s3)):
            at = pl.ds(pl.multiple_of(b * 64 + ((z + k) & 3) * 16, 16), 16)
            total = (own[at, :] + r1[at, :].astype(F32)) + (
                r2[at, :].astype(F32) + r3[at, :].astype(F32)
            )
            ref[b * 16 : (b + 1) * 16, :] = total.astype(ref.dtype)


def split_x_body(place, own, r1, r2, r3, o_ref, own_ref, s1, s2, s3):
    x = place[0]

    def total(at):
        return (own[at, :] + r1[at, :].astype(F32)) + (r2[at, :].astype(F32) + r3[at, :].astype(F32))

    gain = total(slice(96, 112))
    row = iota((16, 256), 0)
    for k, ref in enumerate((own_ref, s1, s2, s3)):
        s = (x + k) & 3
        ref[0:16, :] = total(pl.ds(pl.multiple_of(s * 16, 16), 16)).astype(ref.dtype)
        mine = jnp.sum(jnp.where(row == s, gain, 0.0), axis=0, keepdims=True)
        ref[16:32, :] = jnp.broadcast_to(mine, (16, 256)).astype(ref.dtype)
    o_ref[...] = total(slice(64, 96)).astype(BF)


def join_x_body(place, o, own, r1, r2, r3, out_ref, gain_ref):
    x = place[0]
    gain = jnp.zeros((16, 256), F32)
    for k, ref in enumerate((own, r1, r2, r3)):
        s = (x - k) & 3
        out_ref[pl.ds(pl.multiple_of(s * 16, 16), 16), :] = ref[0:16, :].astype(BF)
        gain += ref[16:32, :].astype(F32)
    out_ref[64:96, :] = o[...]
    gain_ref[...] = gain[0:8]


def join_body(index, place, own, r1, r2, r3, out_ref):
    at = place[index]
    rows = own.shape[0]
    for k, ref in enumerate((own, r1, r2, r3)):
        s = (at + k) & 3
        out_ref[pl.ds(pl.multiple_of(s * rows, rows), rows), :] = ref[...]


def weights_body(place, own, got, wq, wk, wv, gain, q_ref, k_ref, v_ref, o_ref, gain_ref):
    c = place[2]
    scale = gain[...]
    total = jnp.zeros((ROWS_HERE, 1), F32)

    def piece(ref, b):
        return jnp.concatenate(
            [ref[j * 96 + b * 16 : j * 96 + (b + 1) * 16, :] for j in range(16)], axis=0
        ).astype(F32)

    for b in range(6):
        mine, other = piece(own, b), piece(got, b)
        left = jnp.where(c == 0, mine, other)
        right = jnp.where(c == 0, other, mine)
        if b < 4:
            q_ref[:, b * QC : (b + 1) * QC] = left * scale
            k_ref[:, b * KC : (b + 1) * KC] = right[:, 0:KC] * scale
            v_ref[:, b * KC : (b + 1) * KC] = right[:, KC : 2 * KC] * scale
            total += jnp.sum(
                left * wq[:, b * QC : (b + 1) * QC].astype(F32), axis=1, keepdims=True
            )
            total += jnp.sum(
                right[:, 0:KC] * wk[:, b * KC : (b + 1) * KC].astype(F32), axis=1, keepdims=True
            )
            total += jnp.sum(
                right[:, KC : 2 * KC] * wv[:, b * KC : (b + 1) * KC].astype(F32),
                axis=1,
                keepdims=True,
            )
        else:
            o_ref[:, (b - 4) * 512 : (b - 4) * 512 + 256] = left
            o_ref[:, (b - 4) * 512 + 256 : (b - 3) * 512] = right
    gain_ref[...] = total


def from_right(v, k):
    return lax.ppermute(v, "shard", [(i, (i - k) % SHARDS) for i in range(SHARDS)])


def to_right(v, k):
    return lax.ppermute(v, "shard", [(i, (i + k) % SHARDS) for i in range(SHARDS)])


def gather_x(v):
    return [v] + [from_right(v, k) for k in (1, 2, 3)]


def scatter_x(blocks):
    return [blocks[0]] + [to_right(blocks[k], k) for k in (1, 2, 3)]


def along(v, step):
    pairs = []
    for i in range(EXPERTS):
        z, y, c = step(i // 8, (i // 2) % 4, i % 2)
        pairs.append((i, (z % 4) * 8 + (y % 4) * 2 + c % 2))
    return lax.ppermute(v, "expert", pairs)


def swap_core(v):
    return along(v, lambda z, y, c: (z, y, 1 - c))


def exchange(v):
    return lax.all_to_all(v, "expert", split_axis=0, concat_axis=0, tiled=True)


def per_device(
    tokens,
    cotangent,
    order,
    lengths,
    routes,
    gate_weights,
    capacity,
    gain_attn,
    w_query,
    w_key,
    w_value,
    w_out,
    gain_ffn,
    w_gate,
    w_up,
    w_down,
):
    micro = tokens.shape[0]
    x = lax.axis_index("shard").astype(I32)
    e = lax.axis_index("expert").astype(I32)
    places = [
        jnp.stack([x, lengths[m, 0, 0], e & 1, (e >> 1) & 3, e >> 3]) for m in range(micro)
    ]
    orders = [order[m].reshape(SHARDS, TOK) for m in range(micro)]
    cap = capacity.reshape(1, EXPERTS)

    packs = run(
        "pack",
        pack_body,
        [shape((ROWS_HERE + 16, COLS), BF)] * 4,
        [places[0], w_query, w_key, w_value, gain_attn.reshape(1, -1), gain_ffn.reshape(1, -1)],
        smem=(0,),
        size=1 << 21,
    )
    packs = [packs[0]] + [from_right_pack(packs[k], k) for k in (1, 2, 3)]
    token_rows = [gather_x(tokens[m]) for m in range(micro)]
    cot_rows = [gather_x(cotangent[m]) for m in range(micro)]
    w_qkv, gains = run(
        "unpack",
        unpack_body,
        [shape((D, COLS), BF), shape((16, D), F32)],
        [places[0], *packs],
        smem=(0,),
        size=1 << 21,
    )
    weights = jnp.concatenate([w_gate, w_up, w_down], axis=0)
    weight_blocks = gather_x(weights)

    routed, attended, left, reached = [], [], [], []
    for m in range(micro):
        routed.append(
            run(
                "route",
                route_body,
                [shape((TOK, SLOTS), BF)] * 3
                + [shape((SLOTS, TOK), BF), shape((SLOTS, D), BF), shape((TOK, D), BF)],
                [places[m], orders[m], *cot_rows[m], routes[m], gate_weights[m], cap],
                smem=(0,),
                flops=2 * SLOTS * TOK * D,
                size=6 << 20,
            )
        )
        attended.append(
            run(
                "attend",
                attend_body,
                [shape((TOK, D), BF)] * 4
                + [
                    shape((TOK, D), BF),
                    shape((GT, D), BF),
                    shape((GT, COLS), BF),
                    shape((GT, QC), BF),
                    shape((GT, 128), F32),
                ],
                [places[m], orders[m], *token_rows[m], w_qkv, gains, w_out],
                smem=(0,),
                flops=4 << 30,
                size=6 << 20,
            )
        )
    grads_in = [exchange(routed[m][4]) for m in range(micro)]
    for m in range(micro):
        parts = scatter_x(attended[m][:4])
        left.append(
            run(
                "leave",
                leave_body,
                [shape((TOK, D), F32), shape((SLOTS, D), BF)],
                [*parts, attended[m][4], gains, routed[m][3]],
                flops=2 * SLOTS * TOK * D,
                size=5 << 20,
            )
        )
        reached.append(exchange(left[m][1]))

    outs, backs, sums = [], [], None
    for m in range(micro):
        result = expert_call(reached[m], grads_in[m], weight_blocks, sums)
        outs.append(result[0])
        backs.append(exchange(result[1]))
        sums = result[2] if m < micro - 1 else result[2:]
    own = sums[0]
    others = [to_right(sums[k], k) for k in (1, 2, 3)]

    sum_w = sum_o = None
    gain_sums, grad_rows = [], []
    for m in range(micro):
        last = m == micro - 1
        branch, gain_sum = run(
            "returned",
            returned_body,
            [shape((TOK, D), BF), shape((8, D), F32)],
            [backs[m], routed[m][0], left[m][0], gains, routed[m][5]],
            flops=2 * SLOTS * TOK * D,
            size=4 << 20,
        )
        gain_sums.append(gain_sum)
        ins = [places[m], orders[m], *gather_x(branch), *attended[m][5:9], w_qkv, w_out]
        out_shapes = [shape((TOK, D), BF)] * 5
        scratch = []
        if last:
            ins += [sum_w, sum_o, *gain_sums]
            out_shapes += [shape((BLOCKS * 256, 256), F32), shape((BLOCKS * 256, 256), BF)]
            scratch = [pltpu.VMEM((D, COLS), F32), pltpu.VMEM((ROWS_HERE, D), F32)]
        else:
            out_shapes += [shape((D, COLS), F32), shape((ROWS_HERE, D), F32)]
        result = run(
            "attend_back",
            functools.partial(attend_back_body, last),
            out_shapes,
            ins,
            smem=(0,),
            flops=8 << 30,
            size=12 << 20,
            scratch=scratch,
        )
        sum_w, sum_o = result[5:7]
        parts = scatter_x(result[:4])
        grad_rows.append(
            run(
                "tokens",
                tokens_body,
                [shape((TOK, D), BF)],
                [tokens[m], *parts, result[4], gains],
                size=2 << 20,
            )[0]
        )

    place = places[0]
    four = [0, 1, 2, 3]
    got = swap_core(sum_o)
    rows = BLOCKS * 64
    pieces = run(
        "split_y",
        split_y_body,
        [shape((rows, 256), F32)] + [shape((rows, 256), BF)] * 3,
        [place, sum_w, got],
        smem=(0,),
        size=4 << 20,
    )
    pieces = [pieces[0]] + [along(pieces[k], lambda z, y, c, k=k: (z, y + k, c)) for k in four[1:]]
    rows = BLOCKS * 16
    pieces = run(
        "split_z",
        split_z_body,
        [shape((rows, 256), F32)] + [shape((rows, 256), BF)] * 3,
        [place, *pieces],
        smem=(0,),
        size=1 << 20,
    )
    pieces = [pieces[0]] + [along(pieces[k], lambda z, y, c, k=k: (z + k, y, c)) for k in four[1:]]
    o_piece, *pieces = run(
        "split_x",
        split_x_body,
        [shape((32, 256), BF), shape((32, 256), F32)] + [shape((32, 256), BF)] * 3,
        [place, *pieces],
        smem=(0,),
        size=1 << 18,
    )
    piece, gain_ffn_sum = run(
        "join_x",
        join_x_body,
        [shape((96, 256), BF), shape((8, 256), F32)],
        [place, o_piece, *scatter_x(pieces)],
        smem=(0,),
        size=1 << 18,
    )
    for name, index, step in (
        ("join_z", 4, lambda z, y, c, k: (z - k, y, c)),
        ("join_y", 3, lambda z, y, c, k: (z, y - k, c)),
    ):
        pieces = [piece] + [
            along(piece, lambda z, y, c, k=k, step=step: step(z, y, c, k)) for k in four[1:]
        ]
        piece = run(
            name,
            functools.partial(join_body, index),
            [shape((4 * piece.shape[0], 256), BF)],
            [place, *pieces],
            smem=(0,),
            size=1 << 20,
        )[0]
    grad_query, grad_key, grad_value, grad_out, grad_gain = run(
        "weights",
        weights_body,
        [
            shape(w_query.shape, F32),
            shape(w_key.shape, F32),
            shape(w_value.shape, F32),
            shape(w_out.shape, F32),
            shape((ROWS_HERE, 1), F32),
        ],
        [
            place,
            piece,
            swap_core(piece),
            w_query,
            w_key,
            w_value,
            gain_attn.astype(F32).reshape(-1, 1),
        ],
        smem=(0,),
        size=6 << 20,
    )

    blocks = []
    for m in range(micro):
        returned = exchange(outs[m])
        block = run(
            "block",
            block_body,
            [shape((TOK, D), BF)],
            [returned, routed[m][1], routed[m][2], left[m][0]],
            flops=4 * SLOTS * TOK * D,
            size=5 << 20,
        )[0]
        blocks.append(
            run(
                "place",
                place_body,
                [shape((TOK, D), BF)],
                [places[m], orders[m], *gather_x(block)],
                smem=(0,),
                size=2 << 20,
            )[0]
        )

    totals = own
    for other in others:
        totals = totals + other.astype(F32)
    return (
        jnp.stack(blocks),
        jnp.stack(grad_rows),
        grad_gain.reshape(-1),
        grad_query,
        grad_key,
        grad_value,
        grad_out,
        gain_ffn_sum[0],
        totals[0:1],
        totals[1:2],
        totals[2:3],
    )


def from_right_pack(v, k):
    return from_right(v, k)


def solution(mesh):
    return jax.shard_map(
        per_device,
        mesh=mesh,
        in_specs=(
            P(None, ("expert", "shard"), None),
            P(None, ("expert", "shard"), None),
            P(None, "expert", None),
            P(None, "expert", None),
            P(None, ("expert", "shard"), None),
            P(None, ("expert", "shard"), None),
            P(),
            P("shard"),
            P("shard", None),
            P("shard", None),
            P("shard", None),
            P("shard", None),
            P("shard"),
            P("expert", None, "shard"),
            P("expert", None, "shard"),
            P("expert", None, "shard"),
        ),
        out_specs=(
            P(None, ("expert", "shard"), None),
            P(None, ("expert", "shard"), None),
            P("shard"),
            P("shard", None),
            P("shard", None),
            P("shard", None),
            P("shard", None),
            P("shard"),
            P("expert", None, "shard"),
            P("expert", None, "shard"),
            P("expert", None, "shard"),
        ),
        check_vma=False,
    )
```

```python
import functools

import jax
import jax.numpy as jnp
from jax import lax
from jax.experimental import pallas as pl
from jax.experimental.pallas import tpu as pltpu
from jax.sharding import PartitionSpec as P

D = 1024
HEADS = 16
KV_HEADS = 8
HEAD = 64
F = 512
EXPERTS = 32
TOPK = 8
CAP = 48
TOK = 128
GT = 512
SHARDS = 4
SLOTS = EXPERTS * CAP
HEADS_HERE = HEADS // SHARDS
KV_HERE = KV_HEADS // SHARDS
QC = HEADS_HERE * HEAD
KC = KV_HERE * HEAD
COLS = QC + 2 * KC
ROWS_HERE = D // SHARDS

EPS = 1e-05
MASKED = -1e30
SCALE = HEAD ** (-0.5)

BF = jnp.bfloat16
F32 = jnp.float32
I32 = jnp.int32

VMEM = pl.BlockSpec(memory_space=pltpu.VMEM)
SMEM = pl.BlockSpec(memory_space=pltpu.SMEM)
ANY = pl.BlockSpec(memory_space=pl.ANY)


def dot(a, b, ca=1, cb=0):
    return lax.dot_general(a, b, (((ca,), (cb,)), ((), ())), preferred_element_type=F32)


def shape(dims, dtype):
    return jax.ShapeDtypeStruct(dims, dtype)


MICROSECONDS = {
    "pack": 2.5,
    "route": 4.5,
    "deal": 2.3,
    "weight_stack": 2.0,
    "attend": 7.3,
    "leave": 4.3,
    "expert": 27.0,
    "returned": 3.7,
    "attend_back": 10.0,
    "weight_sums": 3.3,
    "split_y": 2.8,
    "split_z": 2.0,
    "split_x": 1.6,
    "join_x": 1.5,
    "join_z": 1.6,
    "join_y": 2.2,
    "block": 1.2,
    "place": 2.8,
    "tokens": 3.4,
    "weights": 3.9,
}


def cost(microseconds):
    return pl.CostEstimate(
        flops=1, bytes_accessed=int(3.6e6 * microseconds) + 1, transcendentals=0
    )


def run(name, body, outs, ins, smem=(), scratch=(), limit=56, after=()):
    count = len(ins)

    def whole(*refs):
        body(*refs[:count], *refs[count + len(after) :])

    ins = [*ins, *after]
    return pl.pallas_call(
        whole,
        out_shape=outs,
        in_specs=[SMEM if i in smem else VMEM for i in range(count)] + [ANY] * len(after),
        out_specs=[VMEM] * len(outs),
        scratch_shapes=list(scratch),
        compiler_params=pltpu.CompilerParams(vmem_limit_bytes=limit * 1024 * 1024),
        cost_estimate=cost(MICROSECONDS[name]),
        name=name,
    )(*ins)


def iota(dims, axis):
    return lax.broadcasted_iota(I32, dims, axis)


def x_of(place):
    return place[0] & 3


def core_of(place):
    return (place[0] >> 2) & 1


def y_of(place):
    return (place[0] >> 3) & 3


def z_of(place):
    return place[0] >> 5


def rolled_order(order_ref, m, x):
    rows = [
        order_ref[m, :, pl.ds(pl.multiple_of(((x + k) & 3) * TOK, TOK), TOK)] for k in range(SHARDS)
    ]
    return (jnp.concatenate(rows, axis=1) - TOK * x) & (GT - 1)


def given_by_dealt(order_ref, m, x, rows=GT):
    return jnp.where(iota((rows, GT), 0) == rolled_order(order_ref, m, x), 1.0, 0.0).astype(BF)


def stack(refs):
    return jnp.concatenate([r[...] for r in refs], axis=0)


def same_documents(x, first_length):
    across = ((iota((GT, GT), 1) + TOK * x) & (GT - 1)) >= first_length
    down = ((iota((GT, GT), 0) + TOK * x) & (GT - 1)) >= first_length
    return jnp.logical_not(jnp.logical_xor(across, down))


def pack_body(place, wq, wk, wv, gains, tokens, *outs):
    x = x_of(place)
    outs[4][...] = tokens[0]
    for k in range(SHARDS):
        s = (x - k) & 3
        outs[k][0:ROWS_HERE, 0:QC] = wq[:, pl.ds(pl.multiple_of(s * QC, QC), QC)]
        outs[k][0:ROWS_HERE, QC : QC + KC] = wk[:, pl.ds(pl.multiple_of(s * KC, KC), KC)]
        outs[k][0:ROWS_HERE, QC + KC : COLS] = wv[:, pl.ds(pl.multiple_of(s * KC, KC), KC)]
        outs[k][ROWS_HERE : ROWS_HERE + 16, :] = jnp.broadcast_to(gains[...], (16, 2 * ROWS_HERE))


def unpack(x, packs, w_out, gains_out):
    for k in range(SHARDS):
        s = (x + k) & 3
        w_out[pl.ds(pl.multiple_of(s * ROWS_HERE, ROWS_HERE), ROWS_HERE), :] = packs[k][
            0:ROWS_HERE, :
        ]
    rows = [p[ROWS_HERE : ROWS_HERE + 16, :].astype(F32)[0:8] for p in packs]
    for half in range(2):
        for b in range(SHARDS):
            total = jnp.zeros((8, ROWS_HERE), F32)
            for k in range(SHARDS):
                piece = rows[k][:, half * ROWS_HERE : (half + 1) * ROWS_HERE]
                total = jnp.where(((x + k) & 3) == b, piece, total)
            gains_out[half * 8 : half * 8 + 8, b * ROWS_HERE : (b + 1) * ROWS_HERE] = total


def route_body(micro, routes, cap, tokens, cotangent, *refs):
    for m in range(1, micro):
        refs[2 * m - 2][...] = tokens[m]
        refs[2 * m - 1][...] = cotangent[m]
    outs = refs[2 * micro - 2 :]
    named = iota((EXPERTS, TOK), 0)
    earlier = jnp.where(iota((TOK, TOK), 0) < iota((TOK, TOK), 1), 1.0, 0.0).astype(BF)
    one = iota((EXPERTS, EXPERTS), 0) == iota((EXPERTS, EXPERTS), 1)
    limit = jnp.sum(jnp.where(one, cap[...], 0).astype(F32), axis=1, keepdims=True)
    first = iota((EXPERTS, SLOTS), 0) * CAP
    slot = iota((EXPERTS, SLOTS), 1)
    spread = jnp.where(jnp.logical_and(slot >= first, slot < first + CAP), 1.0, 0.0).astype(BF)
    within = (iota((TOK, SLOTS), 1) % CAP).astype(F32)
    within_t = (iota((SLOTS, TOK), 0) % CAP).astype(F32)
    for m in range(micro):
        c01_ref, d01_ref = outs[2 * m : 2 * m + 2]
        hits = jnp.zeros((EXPERTS, TOK), F32)
        for k in range(TOPK):
            hit = routes[m, k : k + 1, :] == named
            hits = jnp.where(hit, 1.0, hits)
        ranks = dot(hits.astype(BF), earlier)
        kept = jnp.logical_and(hits > 0.0, ranks < limit)
        place_of = jnp.where(kept, ranks, -1.0).astype(BF)
        own = dot(place_of, spread, 0, 0) == within
        c01_ref[...] = jnp.where(own, 1.0, 0.0).astype(BF)
        own_t = dot(spread, place_of, 0, 0) == within_t
        d01_ref[...] = jnp.where(own_t, 1.0, 0.0).astype(BF)


NOTES = 16


def deal_body(m, place, order, routes, gates, c0, c1, c2, c3, out_ref):
    deal = given_by_dealt(order, m, x_of(place))[:, 0:TOK]
    out_ref[0:TOK, :] = dot(deal, stack((c0, c1, c2, c3)), 0, 0).astype(BF)
    experts = jnp.concatenate([routes[m, k : k + 1, :] for k in range(TOPK)], axis=1).astype(F32)
    weights = jnp.concatenate([gates[m, k : k + 1, :] for k in range(TOPK)], axis=1)
    high = weights.astype(BF).astype(F32)
    row = iota((NOTES, D), 0)
    notes = jnp.where(row == 0, experts, jnp.where(row == 1, high, weights - high))
    out_ref[TOK : TOK + NOTES, :] = notes.astype(BF)


def attend_body(m, place, lengths, order, t0, t1, t2, t3, wo, *refs):
    x, first_length = x_of(place), lengths[m, 0, 0]
    if m == 0:
        packs, refs = refs[:4], refs[4:]
        o0, o1, o2, o3, dealt_ref, xr_ref, qkv_ref, mixed_ref, mass_ref, w, gains = refs
        unpack(x, packs, w, gains)
    else:
        w, gains, o0, o1, o2, o3, dealt_ref, xr_ref, qkv_ref, mixed_ref, mass_ref = refs
    deal = given_by_dealt(order, m, x)
    dealt = dot(deal, stack((t0, t1, t2, t3)), 0, 0)
    dealt_ref[...] = dealt[0:TOK].astype(BF)
    scaled = dealt * lax.rsqrt(jnp.mean(dealt * dealt, axis=-1, keepdims=True) + EPS)
    xr_ref[...] = scaled.astype(BF)
    attn_in = (scaled * gains[0:1, :]).astype(BF)
    qkv = dot(attn_in, w[...]).astype(BF)
    qkv_ref[...] = qkv
    same = same_documents(x, first_length)
    heads = []
    masses = []
    for h in range(HEADS_HERE):
        g = h // (HEADS // KV_HEADS)
        q = qkv[:, h * HEAD : (h + 1) * HEAD]
        k = qkv[:, QC + g * HEAD : QC + (g + 1) * HEAD]
        v = qkv[:, QC + KC + g * HEAD : QC + KC + (g + 1) * HEAD]
        scores = jnp.where(same, dot(q, k, 1, 1) * SCALE, MASKED)
        highest = jnp.max(scores, axis=-1, keepdims=True)
        raised = jnp.exp(scores - highest)
        total = jnp.sum(raised, axis=-1, keepdims=True)
        probs = (raised * (1.0 / total)).astype(BF)
        heads.append(dot(probs, v).astype(BF))
        masses.append(jnp.broadcast_to(highest + jnp.log(total), (GT, 32)))
    mixed = jnp.concatenate(heads, axis=1)
    mixed_ref[...] = mixed
    mass_ref[...] = jnp.concatenate(masses, axis=1)
    part = dot(mixed, wo[...]).astype(BF)
    for k, out in enumerate((o0, o1, o2, o3)):
        out[...] = part[k * TOK : (k + 1) * TOK]


def leave_body(own, r1, r2, r3, dealt, gains, d01, middle_ref, rows_ref):
    middle = dealt[...].astype(F32) + (
        (own[...].astype(F32) + r1[...].astype(F32)) + (r2[...].astype(F32) + r3[...].astype(F32))
    )
    middle_ref[...] = middle
    r = lax.rsqrt(jnp.mean(middle * middle, axis=-1, keepdims=True) + EPS)
    ffn_in = (middle * r * gains[8:9, :]).astype(BF)
    rows_ref[...] = dot(d01[...], ffn_in).astype(BF)


SOURCES = 8
TILE = SOURCES * CAP


def expert_body(m, last, waits, *refs):
    refs = list(refs[waits:])
    place, cap, rows, cotangent = refs[:4]
    blocks = refs[4:9]
    refs = refs[9:]
    prev = None
    if m > 0:
        prev, refs = refs[0], refs[1:]
    out_ref, back_ref = refs[:2]
    if last:
        own_ref, sends, (wg, wu, wd, acc) = refs[2], refs[3:6], refs[6:]
    else:
        sums_ref, (wg, wu, wd, acc) = refs[2], refs[3:]
    step = pl.program_id(0)

    @pl.when(step == 0)
    def _():
        mine, right, left, first, second = blocks
        for k, ref in enumerate((mine, right, (first, second), left)):
            at = slice(k * 128, (k + 1) * 128)
            for half in range(2):
                piece = ref[half] if k != 2 else ref[half][0]
                rows_at = slice(half * (D // 2), (half + 1) * (D // 2))
                wg[rows_at, at] = piece[0]
                wu[rows_at, at] = piece[1]
                wd[rows_at, at] = piece[2]
        acc[...] = jnp.zeros(acc.shape, F32) if prev is None else prev[...]

    expert = place[0] >> 2
    notes = cotangent[:, TOK : TOK + NOTES, :].astype(F32)
    named, high, low = (notes[:, j, :] for j in range(3))
    hits = jnp.zeros((SOURCES, TOK), F32)
    weight = jnp.zeros((SOURCES, TOK), F32)
    for k in range(TOPK):
        at = slice(k * TOK, (k + 1) * TOK)
        hit = named[:, at] == expert.astype(F32)
        hits = jnp.where(hit, 1.0, hits)
        weight = jnp.where(hit, high[:, at] + low[:, at], weight)
    earlier = jnp.where(iota((TOK, TOK), 0) < iota((TOK, TOK), 1), 1.0, 0.0).astype(BF)
    ranks = dot(hits.astype(BF), earlier)
    kept = jnp.logical_and(hits > 0.0, ranks < cap[0, expert].astype(F32))
    place_of = jnp.where(kept, ranks, -1.0)
    rank = iota((CAP, TOK), 0).astype(F32)
    picks, gates_of, grads = [], [], []
    for j in range(SOURCES):
        own = place_of[j : j + 1, :] == rank
        gate = jnp.sum(jnp.where(own, weight[j : j + 1, :], 0.0), axis=1, keepdims=True)
        pick = jnp.where(own, 1.0, 0.0).astype(BF)
        picks.append(pick)
        gates_of.append(gate)
        grads.append((dot(pick, cotangent[j, 0:TOK, :]) * gate).astype(BF))
    grad = jnp.concatenate(grads, axis=0)
    row = rows[...]
    gate_of = jnp.concatenate(gates_of, axis=0)
    gate = dot(row, wg[...])
    up = dot(row, wu[...])
    sig = jax.nn.sigmoid(gate)
    silu = gate * sig
    hidden = (silu * up).astype(BF)
    weighted = (dot(hidden, wd[...], 1, 1) * gate_of).astype(BF)
    for j in range(SOURCES):
        out_ref[j] = dot(picks[j], weighted[j * CAP : (j + 1) * CAP], 0, 0).astype(BF)
    grad_hidden = dot(grad, wd[...])
    grad_gate = (grad_hidden * up * sig * (1.0 + gate * (1.0 - sig))).astype(BF)
    grad_up = (grad_hidden * silu).astype(BF)
    back_ref[...] = (dot(grad_gate, wg[...], 1, 1) + dot(grad_up, wu[...], 1, 1)).astype(BF)
    acc[0] += dot(row, grad_gate, 0, 0)
    acc[1] += dot(row, grad_up, 0, 0)
    acc[2] += dot(grad, hidden, 0, 0)

    @pl.when(step == pl.num_programs(0) - 1)
    def _():
        if last:
            for j in range(3):
                own_ref[j] = acc[j, :, 0:128]
                for k in range(1, SHARDS):
                    sends[k - 1][j] = acc[j, :, k * 128 : (k + 1) * 128].astype(BF)
        else:
            sums_ref[...] = acc[...]


def expert_call(m, micro, place, cap, rows, cotangent, blocks, prev, after=()):
    last = m == micro - 1
    tiles = SLOTS // TILE
    tile = pl.BlockSpec((TILE, D), lambda i: (i, 0))

    def fixed(dims):
        return pl.BlockSpec(dims, lambda i: (0,) * len(dims), pipeline_mode=pl.Buffered(1))

    ins = [place, cap, rows, cotangent, *blocks]
    in_specs = [
        SMEM,
        SMEM,
        tile,
        pl.BlockSpec((SOURCES, TOK + NOTES, D), lambda i: (i, 0, 0)),
    ] + [fixed(b.shape) for b in blocks]
    ins = [*after, *ins]
    in_specs = [ANY] * len(after) + in_specs
    outs = [shape((EXPERTS, TOK, D), BF), shape((SLOTS, D), BF)]
    out_specs = [pl.BlockSpec((SOURCES, TOK, D), lambda i: (i, 0, 0)), tile]
    if m > 0:
        ins.append(prev)
        in_specs.append(fixed((3, D, F)))
    if last:
        outs += [shape((3, D, 128), F32)] + [shape((3, D, 128), BF)] * 3
        out_specs += [fixed((3, D, 128))] * 4
    else:
        outs.append(shape((3, D, F), F32))
        out_specs.append(fixed((3, D, F)))
    return pl.pallas_call(
        functools.partial(expert_body, m, last, len(after)),
        grid=(tiles,),
        in_specs=in_specs,
        out_specs=out_specs,
        out_shape=outs,
        scratch_shapes=[pltpu.VMEM((D, F), BF)] * 3 + [pltpu.VMEM((3, D, F), F32)],
        compiler_params=pltpu.CompilerParams(
            vmem_limit_bytes=56 * 1024 * 1024, dimension_semantics=("arbitrary",)
        ),
        cost_estimate=cost(MICROSECONDS["expert"]),
        name="expert",
    )(*ins)


def returned_body(back, c01, middle, gains, dy, branch_ref, gain_ref):
    upstream = dot(c01[...], back[...])
    mid = middle[...]
    r = lax.rsqrt(jnp.mean(mid * mid, axis=-1, keepdims=True) + EPS)
    scaled = upstream * gains[8:9, :]
    grad = r * scaled - mid * (r * r * r) * jnp.mean(scaled * mid, axis=-1, keepdims=True)
    branch_ref[...] = (dy[0:TOK, :].astype(F32) + grad).astype(BF)
    gain_ref[...] = jnp.broadcast_to(jnp.sum(upstream * mid * r, axis=0, keepdims=True), (8, D))


def block_body(mixture, middle, out_ref):
    out_ref[...] = (middle[...] + mixture[...].astype(F32)).astype(BF)


def place_body(micro, place, order, *refs):
    for m in range(micro):
        deal = given_by_dealt(order, m, x_of(place), TOK)
        refs[-1][m] = dot(deal, stack(refs[SHARDS * m : SHARDS * (m + 1)])).astype(BF)


def attend_back_body(m, last, place, lengths, order, g0, g1, g2, g3, xr, qkv_ref, mixed, mass, w, wo, *refs):
    x, first_length = x_of(place), lengths[m, 0, 0]
    if last:
        prev_w, prev_o, gain0, gain1, *refs = refs
    o0, o1, o2, o3, given_ref, *refs = refs
    deal = given_by_dealt(order, m, x)
    branch = stack((g0, g1, g2, g3))
    given_ref[...] = dot(deal[0:TOK], branch).astype(BF)
    sum_o = dot(mixed[...], branch, 0, 0)
    grad_mixed = dot(branch, wo[...], 1, 1).astype(BF)
    qkv = qkv_ref[...]
    same = same_documents(x, first_length)
    grad_q, grad_k, grad_v = [], [], []
    for g in range(KV_HERE):
        k = qkv[:, QC + g * HEAD : QC + (g + 1) * HEAD]
        v = qkv[:, QC + KC + g * HEAD : QC + KC + (g + 1) * HEAD]
        sum_k = jnp.zeros((HEAD, GT), F32)
        sum_v = jnp.zeros((HEAD, GT), F32)
        for r in range(HEADS // KV_HEADS):
            h = g * (HEADS // KV_HEADS) + r
            q = qkv[:, h * HEAD : (h + 1) * HEAD]
            gm = grad_mixed[:, h * HEAD : (h + 1) * HEAD]
            scores = jnp.where(same, dot(q, k, 1, 1) * SCALE, MASKED)
            probs = jnp.exp(scores - mass[:, h * 32 : h * 32 + 1])
            grad_probs = dot(gm, v, 1, 1)
            sum_v += dot(gm, probs.astype(BF), 0, 0)
            weighted = probs * grad_probs
            grad_scores = weighted - probs * jnp.sum(weighted, axis=-1, keepdims=True)
            grad_scores = grad_scores.astype(BF)
            grad_q.append((dot(grad_scores, k) * SCALE).astype(BF))
            sum_k += dot(q, grad_scores, 0, 0)
        grad_k.append((sum_k * SCALE).astype(BF))
        grad_v.append(sum_v.astype(BF))
    grad_kv = jnp.concatenate(grad_k + grad_v, axis=0).astype(F32).T.astype(BF)
    grad_qkv = jnp.concatenate(grad_q + [grad_kv], axis=1)
    sum_w = dot(xr[...], grad_qkv, 0, 0)
    part = dot(grad_qkv, w[...], 1, 1).astype(BF)
    part = dot(deal, part).astype(BF)
    for k, out in enumerate((o0, o1, o2, o3)):
        out[...] = part[k * TOK : (k + 1) * TOK]
    if not last:
        sum_w_ref, sum_o_ref = refs
        sum_w_ref[...] = sum_w
        sum_o_ref[...] = sum_o
        return
    keep_ref, send_ref, all_w, all_o = refs
    c = core_of(place)
    all_w[...] = sum_w + prev_w[...]
    all_o[...] = sum_o + prev_o[...]
    gain = gain0[...] + gain1[...]
    for ref, half in ((keep_ref, c), (send_ref, 1 - c)):
        at = pl.ds(pl.multiple_of(half * 256, 256), 256)
        ref[0:D, :] = all_w[:, at].astype(ref.dtype)
        for j in range(2):
            at = pl.ds(pl.multiple_of(j * 512 + half * 256, 256), 256)
            ref[D + j * 256 : D + (j + 1) * 256, :] = all_o[:, at].astype(ref.dtype)
        tile = jnp.concatenate(
            [gain[0:1, b * 256 : (b + 1) * 256] for b in range(4)] + [jnp.zeros((12, 256), F32)], axis=0
        )
        for j in range(16):
            ref[6 * 256 + j * 16 : 6 * 256 + (j + 1) * 16, :] = tile.astype(ref.dtype)


def tokens_body(micro, tokens, gains, *refs):
    for m in range(micro):
        p0, p1, p2, p3, given = refs[5 * m : 5 * m + 5]
        upstream = (p0[...].astype(F32) + p1[...].astype(F32)) + (
            p2[...].astype(F32) + p3[...].astype(F32)
        )
        v = tokens[m].astype(F32)
        r = lax.rsqrt(jnp.mean(v * v, axis=-1, keepdims=True) + EPS)
        scaled = upstream * gains[0:1, :]
        grad = r * scaled - v * (r * r * r) * jnp.mean(scaled * v, axis=-1, keepdims=True)
        refs[-1][m] = (given[...].astype(F32) + grad).astype(BF)


def weight_sums_body(own, r1, r2, r3, *outs):
    for j in range(3):
        outs[j][0] = (own[j] + r1[j].astype(F32)) + (r2[j].astype(F32) + r3[j].astype(F32))


def weight_stack_body(a, b, c, out_ref):
    for j, ref in enumerate((a, b, c)):
        for half in range(2):
            out_ref[half, j] = ref[0, half * (D // 2) : (half + 1) * (D // 2)]


BLOCKS = 7


def split_y_body(place, keep, got, own_ref, s1, s2, s3):
    y = y_of(place)
    for b in range(BLOCKS):
        for k, ref in enumerate((own_ref, s1, s2, s3)):
            at = pl.ds(pl.multiple_of(b * 256 + ((y + k) & 3) * 64, 64), 64)
            ref[b * 64 : (b + 1) * 64, :] = (keep[at, :] + got[at, :].astype(F32)).astype(ref.dtype)


def split_z_body(place, own, r1, r2, r3, own_ref, s1, s2, s3):
    z = z_of(place)
    for b in range(BLOCKS):
        for k, ref in enumerate((own_ref, s1, s2, s3)):
            at = pl.ds(pl.multiple_of(b * 64 + ((z + k) & 3) * 16, 16), 16)
            total = (own[at, :] + r1[at, :].astype(F32)) + (
                r2[at, :].astype(F32) + r3[at, :].astype(F32)
            )
            ref[b * 16 : (b + 1) * 16, :] = total.astype(ref.dtype)


def split_x_body(place, own, r1, r2, r3, o_ref, own_ref, s1, s2, s3):
    x = x_of(place)

    def total(at):
        return (own[at, :] + r1[at, :].astype(F32)) + (r2[at, :].astype(F32) + r3[at, :].astype(F32))

    gain = total(slice(96, 112))
    row = iota((16, 256), 0)
    for k, ref in enumerate((own_ref, s1, s2, s3)):
        s = (x + k) & 3
        ref[0:16, :] = total(pl.ds(pl.multiple_of(s * 16, 16), 16)).astype(ref.dtype)
        mine = jnp.sum(jnp.where(row == s, gain, 0.0), axis=0, keepdims=True)
        ref[16:32, :] = jnp.broadcast_to(mine, (16, 256)).astype(ref.dtype)
    o_ref[...] = total(slice(64, 96)).astype(BF)


def join_x_body(place, o, own, r1, r2, r3, out_ref, gain_ref):
    x = x_of(place)
    gain = jnp.zeros((16, 256), F32)
    for k, ref in enumerate((own, r1, r2, r3)):
        s = (x - k) & 3
        out_ref[pl.ds(pl.multiple_of(s * 16, 16), 16), :] = ref[0:16, :].astype(BF)
        gain += ref[16:32, :].astype(F32)
    out_ref[64:96, :] = o[...]
    gain_ref[...] = gain[0:1]


def join_body(index_of, place, own, r1, r2, r3, out_ref):
    at = index_of(place)
    rows = own.shape[0]
    for k, ref in enumerate((own, r1, r2, r3)):
        s = (at + k) & 3
        out_ref[pl.ds(pl.multiple_of(s * rows, rows), rows), :] = ref[...]


def weights_body(place, own, got, wq, wk, wv, gain, q_ref, k_ref, v_ref, o_ref, gain_ref):
    c = core_of(place)
    scale = gain[...]
    total = jnp.zeros((ROWS_HERE, 1), F32)

    def piece(ref, b):
        return jnp.concatenate(
            [ref[j * 96 + b * 16 : j * 96 + (b + 1) * 16, :] for j in range(16)], axis=0
        ).astype(F32)

    for b in range(6):
        mine, other = piece(own, b), piece(got, b)
        left = jnp.where(c == 0, mine, other)
        right = jnp.where(c == 0, other, mine)
        if b < 4:
            q_ref[:, b * QC : (b + 1) * QC] = left * scale
            k_ref[:, b * KC : (b + 1) * KC] = right[:, 0:KC] * scale
            v_ref[:, b * KC : (b + 1) * KC] = right[:, KC : 2 * KC] * scale
            total += jnp.sum(
                left * wq[:, b * QC : (b + 1) * QC].astype(F32), axis=1, keepdims=True
            )
            total += jnp.sum(
                right[:, 0:KC] * wk[:, b * KC : (b + 1) * KC].astype(F32), axis=1, keepdims=True
            )
            total += jnp.sum(
                right[:, KC : 2 * KC] * wv[:, b * KC : (b + 1) * KC].astype(F32),
                axis=1,
                keepdims=True,
            )
        else:
            o_ref[:, (b - 4) * 512 : (b - 4) * 512 + 256] = left
            o_ref[:, (b - 4) * 512 + 256 : (b - 3) * 512] = right
    gain_ref[...] = jnp.broadcast_to(total, (ROWS_HERE, 128)).T[0:1]


def from_right(v, k):
    return lax.ppermute(v, "shard", [(i, (i - k) % SHARDS) for i in range(SHARDS)])


def to_right(v, k):
    return lax.ppermute(v, "shard", [(i, (i + k) % SHARDS) for i in range(SHARDS)])


def gather_x(v):
    return [v] + [from_right(v, k) for k in (1, 2, 3)]


def gather_ring(v):
    half = v.shape[0] // 2
    right, left = from_right(v, 1), from_right(v, 3)
    return [v, right, left, from_right(right[:half], 1), from_right(left[half:], 3)]


def hold(arrays, *others):
    count = len(arrays)
    return pl.pallas_call(
        lambda *refs: None,
        out_shape=[shape(v.shape, v.dtype) for v in arrays],
        in_specs=[ANY] * (count + len(others)),
        out_specs=[ANY] * count,
        input_output_aliases={i: i for i in range(count)},
        cost_estimate=cost(0),
        name="hold",
    )(*arrays, *others)


def scatter_x(blocks):
    return [blocks[0]] + [to_right(blocks[k], k) for k in (1, 2, 3)]


def along(v, step):
    pairs = []
    for i in range(EXPERTS):
        z, y, c = step(i // 8, (i // 2) % 4, i % 2)
        pairs.append((i, (z % 4) * 8 + (y % 4) * 2 + c % 2))
    return lax.ppermute(v, "expert", pairs)


def swap_core(v):
    return along(v, lambda z, y, c: (z, y, 1 - c))


def sum_over_experts(v):
    return lax.psum_scatter(v, "expert", scatter_dimension=0, tiled=True)


def exchange(v):
    return lax.all_to_all(v, "expert", split_axis=0, concat_axis=0, tiled=True)


def per_device(
    tokens,
    cotangent,
    order,
    lengths,
    routes,
    gate_weights,
    capacity,
    gain_attn,
    w_query,
    w_key,
    w_value,
    w_out,
    gain_ffn,
    w_gate,
    w_up,
    w_down,
):
    micro = tokens.shape[0]
    place = lax.axis_index(("expert", "shard")).astype(I32).reshape(1)
    cap = capacity.reshape(1, EXPERTS)
    experts = jnp.swapaxes(routes, 1, 2)
    gates = jnp.swapaxes(gate_weights, 1, 2)

    cot_rows = gather_x(cotangent[0])
    *packs, tokens_first = run(
        "pack",
        pack_body,
        [shape((ROWS_HERE + 16, COLS), BF)] * 4 + [shape((TOK, D), BF)],
        [
            place,
            w_query,
            w_key,
            w_value,
            jnp.concatenate([gain_attn, gain_ffn]).reshape(1, -1),
            tokens,
        ],
        smem=(0,),
    )
    pack_done = tokens_first
    waited = hold([*packs, tokens_first], *cot_rows[1:])
    packs, tokens_first = waited[:SHARDS], waited[SHARDS]
    token_rows = gather_x(tokens_first)
    packs = [packs[0]] + [from_right(packs[k], k) for k in (1, 2, 3)]
    routed = run(
        "route",
        functools.partial(route_body, micro),
        [shape((TOK, D), BF)] * (2 * micro - 2)
        + [shape((TOK, SLOTS), BF), shape((SLOTS, TOK), BF)] * micro,
        [experts, cap, tokens, cotangent],
        after=[pack_done],
    )
    later, routed = routed[: 2 * micro - 2], routed[2 * micro - 2 :]
    routed = [routed[2 * m : 2 * m + 2] for m in range(micro)]

    attended, left, reached, dealt_cot, cot_all = [], [], [], [], []
    w_qkv = gains = weights = weight_blocks = parts = None
    for m in range(micro):
        first = m == 0
        if not first:
            cot_rows = gather_x(hold([later[2 * m - 1]], *packs[1:], *token_rows[1:])[0])
            token_rows = gather_x(hold([later[2 * m - 2]], left[-1][1])[0])
        dealt_cot.append(
            run(
                "deal",
                functools.partial(deal_body, m),
                [shape((TOK + NOTES, D), BF)],
                [place, order, experts, gates, *cot_rows],
                smem=(0,),
                after=[pack_done, routed[0][0]] if first else parts[1:2],
            )[0]
        )
        cot_all.append(lax.all_gather(dealt_cot[m], "expert", axis=0))
        if first:
            weights = run(
                "weight_stack",
                weight_stack_body,
                [shape((2, 3, D // 2, 128), BF)],
                [w_gate, w_up, w_down],
                after=dealt_cot,
            )[0]
        elif m == 1:
            weight_blocks = gather_ring(hold([weights], *parts[1:])[0])
        outs = [shape((TOK, D), BF)] * 5 + [
            shape((GT, D), BF),
            shape((GT, COLS), BF),
            shape((GT, QC), BF),
            shape((GT, 128), F32),
        ]
        if first:
            outs += [shape((D, COLS), BF), shape((16, D), F32)]
        result = run(
            "attend",
            functools.partial(attend_body, m),
            outs,
            [place, lengths, order, *token_rows, w_out, *(packs if first else (w_qkv, gains))],
            smem=(0, 1),
            after=[weights] if first else [dealt_cot[m], *weight_blocks[1:3]],
        )
        if first:
            w_qkv, gains = result[9:]
        attended.append(result[:9])
        parts = scatter_x(result[:4])
        left.append(
            run(
                "leave",
                leave_body,
                [shape((TOK, D), F32), shape((SLOTS, D), BF)],
                [*parts, result[4], gains, routed[m][1]],
                after=[] if first else weight_blocks[3:],
            )
        )
        reached.append(exchange(left[m][1]))

    backs, mixtures, sums = [], [], None
    for m in range(micro):
        result = expert_call(
            m,
            micro,
            place,
            cap,
            reached[m],
            cot_all[m],
            weight_blocks,
            sums,
            after=[left[-1][1]] if m == 0 else [],
        )
        dense, back = hold(result[:2], backs[m - 1] if m else reached[-1])
        mixtures.append(sum_over_experts(dense.reshape(-1, D)))
        backs.append(exchange(back))
        sums = result[2] if m < micro - 1 else result[2:]

    def block_of(m, after):
        return run(
            "block",
            block_body,
            [shape((TOK, D), BF)],
            [mixtures[m], left[m][0]],
            after=after,
        )[0]

    sum_w = sum_o = None
    gain_sums, grad_parts = [], []
    for m in range(micro):
        last = m == micro - 1
        branch, gain_sum = run(
            "returned",
            returned_body,
            [shape((TOK, D), BF), shape((8, D), F32)],
            [backs[m], routed[m][0], left[m][0], gains, dealt_cot[m]],
            after=() if m == 0 else (sum_w, totals[0]),
        )
        branch_rows = gather_x(branch)
        if not last:
            block_rows = gather_x(block_of(0, [branch]))
            totals = run(
                "weight_sums",
                weight_sums_body,
                [shape((1, D, 128), F32)] * 3,
                scatter_x(sums),
            )
        gain_sums.append(gain_sum)
        ins = [place, lengths, order, *branch_rows, *attended[m][5:9], w_qkv, w_out]
        out_shapes = [shape((TOK, D), BF)] * 5
        scratch = []
        if last:
            ins += [sum_w, sum_o, *gain_sums]
            out_shapes += [shape((BLOCKS * 256, 256), F32), shape((BLOCKS * 256, 256), BF)]
            scratch = [pltpu.VMEM((D, COLS), F32), pltpu.VMEM((ROWS_HERE, D), F32)]
        else:
            out_shapes += [shape((D, COLS), F32), shape((ROWS_HERE, D), F32)]
        result = run(
            "attend_back",
            functools.partial(attend_back_body, m, last),
            out_shapes,
            ins,
            smem=(0, 1),
            scratch=scratch,
        )
        sum_w, sum_o = result[5:7]
        if last:
            last_parts, last_given = result[:4], result[4]
        else:
            grad_parts += [*scatter_x(result[:4]), result[4]]
    four = [0, 1, 2, 3]
    rows = BLOCKS * 64
    split_y = run(
        "split_y",
        split_y_body,
        [shape((rows, 256), F32)] + [shape((rows, 256), BF)] * 3,
        [place, sum_w, swap_core(sum_o)],
        smem=(0,),
    )
    grad_parts += [*scatter_x(hold(last_parts, split_y[0])), last_given]
    grad_tokens = run(
        "tokens",
        functools.partial(tokens_body, micro),
        [shape(tokens.shape, BF)],
        [tokens, gains, *grad_parts],
    )[0]
    pieces = [split_y[0]] + [along(split_y[k], lambda z, y, c, k=k: (z, y + k, c)) for k in four[1:]]
    rows = BLOCKS * 16
    pieces = run(
        "split_z",
        split_z_body,
        [shape((rows, 256), F32)] + [shape((rows, 256), BF)] * 3,
        [place, *pieces],
        smem=(0,),
    )
    pieces = [pieces[0]] + [along(pieces[k], lambda z, y, c, k=k: (z + k, y, c)) for k in four[1:]]
    o_piece, *pieces = run(
        "split_x",
        split_x_body,
        [shape((32, 256), BF), shape((32, 256), F32)] + [shape((32, 256), BF)] * 3,
        [place, *pieces],
        smem=(0,),
        after=[grad_tokens],
    )
    piece, gain_ffn_sum = run(
        "join_x",
        join_x_body,
        [shape((96, 256), BF), shape((1, 256), F32)],
        [place, o_piece, *scatter_x(pieces)],
        smem=(0,),
    )
    for name, index_of, step in (
        ("join_z", z_of, lambda z, y, c, k: (z - k, y, c)),
        ("join_y", y_of, lambda z, y, c, k: (z, y - k, c)),
    ):
        pieces = [piece] + [
            along(piece, lambda z, y, c, k=k, step=step: step(z, y, c, k)) for k in four[1:]
        ]
        piece = run(
            name,
            functools.partial(join_body, index_of),
            [shape((4 * piece.shape[0], 256), BF)],
            [place, *pieces],
            smem=(0,),
        )[0]
    block_rows += gather_x(block_of(1, [piece]))
    grad_query, grad_key, grad_value, grad_out, grad_gain = run(
        "weights",
        weights_body,
        [
            shape(w_query.shape, F32),
            shape(w_key.shape, F32),
            shape(w_value.shape, F32),
            shape(w_out.shape, F32),
            shape((1, ROWS_HERE), F32),
        ],
        [
            place,
            piece,
            swap_core(piece),
            w_query,
            w_key,
            w_value,
            gain_attn.astype(F32).reshape(-1, 1),
        ],
        smem=(0,),
    )

    block_out = run(
        "place",
        functools.partial(place_body, micro),
        [shape(tokens.shape, BF)],
        [place, order, *block_rows],
        smem=(0,),
    )[0]
    return (
        block_out,
        grad_tokens,
        grad_gain.reshape(-1),
        grad_query,
        grad_key,
        grad_value,
        grad_out,
        gain_ffn_sum.reshape(-1),
        *totals,
    )


def solution(mesh):
    return jax.shard_map(
        per_device,
        mesh=mesh,
        in_specs=(
            P(None, ("expert", "shard"), None),
            P(None, ("expert", "shard"), None),
            P(None, "expert", None),
            P(None, "expert", None),
            P(None, ("expert", "shard"), None),
            P(None, ("expert", "shard"), None),
            P(),
            P("shard"),
            P("shard", None),
            P("shard", None),
            P("shard", None),
            P("shard", None),
            P("shard"),
            P("expert", None, "shard"),
            P("expert", None, "shard"),
            P("expert", None, "shard"),
        ),
        out_specs=(
            P(None, ("expert", "shard"), None),
            P(None, ("expert", "shard"), None),
            P("shard"),
            P("shard", None),
            P("shard", None),
            P("shard", None),
            P("shard", None),
            P("shard"),
            P("expert", None, "shard"),
            P("expert", None, "shard"),
            P("expert", None, "shard"),
        ),
        check_vma=False,
    )
```

```python
import functools

import jax
import jax.numpy as jnp
from jax import lax
from jax.experimental import pallas as pl
from jax.experimental.pallas import tpu as pltpu
from jax.sharding import PartitionSpec as P

D = 1024
HEADS = 16
KV_HEADS = 8
HEAD = 64
F = 512
EXPERTS = 32
TOPK = 8
CAP = 48
TOK = 128
GT = 512
SHARDS = 4
SLOTS = EXPERTS * CAP
HEADS_HERE = HEADS // SHARDS
KV_HERE = KV_HEADS // SHARDS
QC = HEADS_HERE * HEAD
KC = KV_HERE * HEAD
COLS = QC + 2 * KC
ROWS_HERE = D // SHARDS

EPS = 1e-05
MASKED = -1e30
SCALE = HEAD ** (-0.5)

BF = jnp.bfloat16
F32 = jnp.float32
I32 = jnp.int32

VMEM = pl.BlockSpec(memory_space=pltpu.VMEM)
SMEM = pl.BlockSpec(memory_space=pltpu.SMEM)
ANY = pl.BlockSpec(memory_space=pl.ANY)


def dot(a, b, ca=1, cb=0):
    return lax.dot_general(a, b, (((ca,), (cb,)), ((), ())), preferred_element_type=F32)


def shape(dims, dtype):
    return jax.ShapeDtypeStruct(dims, dtype)


MICROSECONDS = {
    "pack": 2.5,
    "route": 4.5,
    "deal": 3.5,
    "weight_stack": 2.0,
    "attend": 7.3,
    "leave": 4.3,
    "expert": 27.0,
    "returned": 3.7,
    "attend_back": 11.0,
    "weight_sums": 2.0,
    "split_y": 2.8,
    "split_z": 2.0,
    "split_x": 1.6,
    "join_x": 1.5,
    "join_z": 1.6,
    "join_y": 2.2,
    "block": 4.5,
    "place": 2.8,
    "tokens": 3.4,
    "weights": 3.9,
}


def cost(microseconds):
    return pl.CostEstimate(
        flops=1, bytes_accessed=int(3.6e6 * microseconds) + 1, transcendentals=0
    )


def run(name, body, outs, ins, smem=(), scratch=(), limit=63, after=()):
    count = len(ins)

    def whole(*refs):
        body(*refs[:count], *refs[count + len(after) :])

    ins = [*ins, *after]
    return pl.pallas_call(
        whole,
        out_shape=outs,
        in_specs=[SMEM if i in smem else VMEM for i in range(count)] + [ANY] * len(after),
        out_specs=[VMEM] * len(outs),
        scratch_shapes=list(scratch),
        compiler_params=pltpu.CompilerParams(vmem_limit_bytes=limit * 1024 * 1024),
        cost_estimate=cost(MICROSECONDS[name]),
        name=name,
    )(*ins)


def iota(dims, axis):
    return lax.broadcasted_iota(I32, dims, axis)


def x_of(place):
    return place[0] & 3


def core_of(place):
    return (place[0] >> 2) & 1


def y_of(place):
    return (place[0] >> 3) & 3


def z_of(place):
    return place[0] >> 5


def rolled_order(order_ref, m, x):
    rows = [
        order_ref[m, :, pl.ds(pl.multiple_of(((x + k) & 3) * TOK, TOK), TOK)] for k in range(SHARDS)
    ]
    return (jnp.concatenate(rows, axis=1) - TOK * x) & (GT - 1)


def given_by_dealt(order_ref, m, x, rows=GT):
    return jnp.where(iota((rows, GT), 0) == rolled_order(order_ref, m, x), 1.0, 0.0).astype(BF)


def stack(refs):
    return jnp.concatenate([r[...] for r in refs], axis=0)


def same_documents(x, first_length):
    across = ((iota((GT, GT), 1) + TOK * x) & (GT - 1)) >= first_length
    down = ((iota((GT, GT), 0) + TOK * x) & (GT - 1)) >= first_length
    return jnp.logical_not(jnp.logical_xor(across, down))


def pack_body(place, wq, wk, wv, gains, tokens, *outs):
    x = x_of(place)
    outs[4][...] = tokens[0]
    for k in range(SHARDS):
        s = (x - k) & 3
        outs[k][0:ROWS_HERE, 0:QC] = wq[:, pl.ds(pl.multiple_of(s * QC, QC), QC)]
        outs[k][0:ROWS_HERE, QC : QC + KC] = wk[:, pl.ds(pl.multiple_of(s * KC, KC), KC)]
        outs[k][0:ROWS_HERE, QC + KC : COLS] = wv[:, pl.ds(pl.multiple_of(s * KC, KC), KC)]
        outs[k][ROWS_HERE : ROWS_HERE + 16, :] = jnp.broadcast_to(gains[...], (16, 2 * ROWS_HERE))


def unpack(x, packs, w_out, gains_out):
    for k in range(SHARDS):
        s = (x + k) & 3
        w_out[pl.ds(pl.multiple_of(s * ROWS_HERE, ROWS_HERE), ROWS_HERE), :] = packs[k][
            0:ROWS_HERE, :
        ]
    rows = [p[ROWS_HERE : ROWS_HERE + 16, :].astype(F32)[0:8] for p in packs]
    for half in range(2):
        for b in range(SHARDS):
            total = jnp.zeros((8, ROWS_HERE), F32)
            for k in range(SHARDS):
                piece = rows[k][:, half * ROWS_HERE : (half + 1) * ROWS_HERE]
                total = jnp.where(((x + k) & 3) == b, piece, total)
            gains_out[half * 8 : half * 8 + 8, b * ROWS_HERE : (b + 1) * ROWS_HERE] = total


def route_body(micro, routes, cap, tokens, *refs):
    for m in range(1, micro):
        refs[m - 1][...] = tokens[m]
    outs = refs[micro - 1 :]
    named = iota((EXPERTS, TOK), 0)
    earlier = jnp.where(iota((TOK, TOK), 0) < iota((TOK, TOK), 1), 1.0, 0.0).astype(BF)
    one = iota((EXPERTS, EXPERTS), 0) == iota((EXPERTS, EXPERTS), 1)
    limit = jnp.sum(jnp.where(one, cap[...], 0).astype(F32), axis=1, keepdims=True)
    first = iota((EXPERTS, SLOTS), 0) * CAP
    slot = iota((EXPERTS, SLOTS), 1)
    spread = jnp.where(jnp.logical_and(slot >= first, slot < first + CAP), 1.0, 0.0).astype(BF)
    within = (iota((TOK, SLOTS), 1) % CAP).astype(F32)
    within_t = (iota((SLOTS, TOK), 0) % CAP).astype(F32)
    for m in range(micro):
        c01_ref, d01_ref = outs[2 * m : 2 * m + 2]
        hits = jnp.zeros((EXPERTS, TOK), F32)
        for k in range(TOPK):
            hit = routes[m, k : k + 1, :] == named
            hits = jnp.where(hit, 1.0, hits)
        ranks = dot(hits.astype(BF), earlier)
        kept = jnp.logical_and(hits > 0.0, ranks < limit)
        place_of = jnp.where(kept, ranks, -1.0).astype(BF)
        own = dot(place_of, spread, 0, 0) == within
        c01_ref[...] = jnp.where(own, 1.0, 0.0).astype(BF)
        own_t = dot(spread, place_of, 0, 0) == within_t
        d01_ref[...] = jnp.where(own_t, 1.0, 0.0).astype(BF)


NOTES = 16


def deal_body(micro, place, order, routes, gates, c0, c1, c2, c3, out_ref):
    for m in range(micro):
        deal = given_by_dealt(order, m, x_of(place))[:, 0:TOK]
        rows = jnp.concatenate([c[m] for c in (c0, c1, c2, c3)], axis=0)
        out_ref[m, 0:TOK, :] = dot(deal, rows, 0, 0).astype(BF)
        experts = jnp.concatenate([routes[m, k : k + 1, :] for k in range(TOPK)], axis=1)
        weights = jnp.concatenate([gates[m, k : k + 1, :] for k in range(TOPK)], axis=1)
        high = weights.astype(BF).astype(F32)
        row = iota((NOTES, D), 0)
        notes = jnp.where(row == 1, high, weights - high)
        notes = jnp.where(row == 0, experts.astype(F32), notes)
        out_ref[m, TOK : TOK + NOTES, :] = notes.astype(BF)


def attend_body(m, place, lengths, order, t0, t1, t2, t3, wo, *refs):
    x, first_length = x_of(place), lengths[m, 0, 0]
    if m == 0:
        packs, refs = refs[:4], refs[4:]
        o0, o1, o2, o3, dealt_ref, xr_ref, qkv_ref, mixed_ref, mass_ref, w, gains = refs
        unpack(x, packs, w, gains)
    else:
        w, gains, o0, o1, o2, o3, dealt_ref, xr_ref, qkv_ref, mixed_ref, mass_ref = refs
    deal = given_by_dealt(order, m, x)
    dealt = dot(deal, stack((t0, t1, t2, t3)), 0, 0)
    dealt_ref[...] = dealt[0:TOK].astype(BF)
    scaled = dealt * lax.rsqrt(jnp.mean(dealt * dealt, axis=-1, keepdims=True) + EPS)
    xr_ref[...] = scaled.astype(BF)
    attn_in = (scaled * gains[0:1, :]).astype(BF)
    qkv = dot(attn_in, w[...]).astype(BF)
    qkv_ref[...] = qkv
    same = same_documents(x, first_length)
    heads = []
    masses = []
    for h in range(HEADS_HERE):
        g = h // (HEADS // KV_HEADS)
        q = qkv[:, h * HEAD : (h + 1) * HEAD]
        k = qkv[:, QC + g * HEAD : QC + (g + 1) * HEAD]
        v = qkv[:, QC + KC + g * HEAD : QC + KC + (g + 1) * HEAD]
        scores = jnp.where(same, dot(q, k, 1, 1) * SCALE, MASKED)
        highest = jnp.max(scores, axis=-1, keepdims=True)
        raised = jnp.exp(scores - highest)
        total = jnp.sum(raised, axis=-1, keepdims=True)
        probs = (raised * (1.0 / total)).astype(BF)
        heads.append(dot(probs, v).astype(BF))
        masses.append(jnp.broadcast_to(highest + jnp.log(total), (GT, 32)))
    mixed = jnp.concatenate(heads, axis=1)
    mixed_ref[...] = mixed
    mass_ref[...] = jnp.concatenate(masses, axis=1)
    part = dot(mixed, wo[...]).astype(BF)
    for k, out in enumerate((o0, o1, o2, o3)):
        out[...] = part[k * TOK : (k + 1) * TOK]


def leave_body(own, r1, r2, r3, dealt, gains, d01, middle_ref, rows_ref):
    middle = dealt[...].astype(F32) + (
        (own[...].astype(F32) + r1[...].astype(F32)) + (r2[...].astype(F32) + r3[...].astype(F32))
    )
    middle_ref[...] = middle
    r = lax.rsqrt(jnp.mean(middle * middle, axis=-1, keepdims=True) + EPS)
    ffn_in = (middle * r * gains[8:9, :]).astype(BF)
    rows_ref[...] = dot(d01[...], ffn_in).astype(BF)


SOURCES = 8
TILE = SOURCES * CAP


def expert_body(m, last, waits, *refs):
    refs = list(refs[waits:])
    place, cap, rows, cotangent = refs[:4]
    blocks = refs[4:9]
    refs = refs[9:]
    prev = None
    if m > 0:
        prev, refs = refs[0], refs[1:]
    out_ref, back_ref = refs[:2]
    if last:
        send_ref, (wg, wu, wd, acc) = refs[2], refs[3:]
    else:
        sums_ref, (wg, wu, wd, acc) = refs[2], refs[3:]
    step = pl.program_id(0)

    @pl.when(step == 0)
    def _():
        mine, right, left, first, second = blocks
        for k, ref in enumerate((mine, right, (first, second), left)):
            at = slice(k * 128, (k + 1) * 128)
            for half in range(2):
                piece = ref[half] if k != 2 else ref[half][0]
                rows_at = slice(half * (D // 2), (half + 1) * (D // 2))
                wg[rows_at, at] = piece[0]
                wu[rows_at, at] = piece[1]
                wd[rows_at, at] = piece[2]
        acc[...] = jnp.zeros(acc.shape, F32) if prev is None else prev[...]

    expert = place[0] >> 2
    notes = cotangent[:, 0, TOK : TOK + NOTES, :].astype(F32)
    named, high, low = (notes[:, j, :] for j in range(3))
    hits = jnp.zeros((SOURCES, TOK), F32)
    weight = jnp.zeros((SOURCES, TOK), F32)
    for k in range(TOPK):
        at = slice(k * TOK, (k + 1) * TOK)
        hit = named[:, at] == expert.astype(F32)
        hits = jnp.where(hit, 1.0, hits)
        weight = jnp.where(hit, high[:, at] + low[:, at], weight)
    earlier = jnp.where(iota((TOK, TOK), 0) < iota((TOK, TOK), 1), 1.0, 0.0).astype(BF)
    ranks = dot(hits.astype(BF), earlier)
    kept = jnp.logical_and(hits > 0.0, ranks < cap[0, expert].astype(F32))
    place_of = jnp.where(kept, ranks, -1.0)
    rank = iota((CAP, TOK), 0).astype(F32)
    picks, gates_of, grads = [], [], []
    for j in range(SOURCES):
        own = place_of[j : j + 1, :] == rank
        gate = jnp.sum(jnp.where(own, weight[j : j + 1, :], 0.0), axis=1, keepdims=True)
        pick = jnp.where(own, 1.0, 0.0).astype(BF)
        picks.append(pick)
        gates_of.append(gate)
        grads.append((dot(pick, cotangent[j, 0, 0:TOK, :]) * gate).astype(BF))
    grad = jnp.concatenate(grads, axis=0)
    row = rows[...]
    gate_of = jnp.concatenate(gates_of, axis=0)
    gate = dot(row, wg[...])
    up = dot(row, wu[...])
    sig = jax.nn.sigmoid(gate)
    silu = gate * sig
    hidden = (silu * up).astype(BF)
    weighted = (dot(hidden, wd[...], 1, 1) * gate_of).astype(BF)
    if last:
        out_ref[...] = weighted
    else:
        for j in range(SOURCES):
            out_ref[j] = dot(picks[j], weighted[j * CAP : (j + 1) * CAP], 0, 0).astype(BF)
    grad_hidden = dot(grad, wd[...])
    grad_gate = (grad_hidden * up * sig * (1.0 + gate * (1.0 - sig))).astype(BF)
    grad_up = (grad_hidden * silu).astype(BF)
    back_ref[...] = (dot(grad_gate, wg[...], 1, 1) + dot(grad_up, wu[...], 1, 1)).astype(BF)
    acc[0] += dot(row, grad_gate, 0, 0)
    acc[1] += dot(row, grad_up, 0, 0)
    acc[2] += dot(grad, hidden, 0, 0)

    @pl.when(step == pl.num_programs(0) - 1)
    def _():
        if last:
            for k in range(SHARDS):
                for j in range(3):
                    piece = acc[j, :, k * 128 : (k + 1) * 128].astype(BF)
                    send_ref[pl.ds((x_of(place) + k) & 3, 1), j] = piece[None]
        else:
            sums_ref[...] = acc[...]


def expert_call(m, micro, place, cap, rows, cotangent, blocks, prev, after=()):
    last = m == micro - 1
    tiles = SLOTS // TILE
    tile = pl.BlockSpec((TILE, D), lambda i: (i, 0))

    def fixed(dims):
        return pl.BlockSpec(dims, lambda i: (0,) * len(dims), pipeline_mode=pl.Buffered(1))

    ins = [place, cap, rows, cotangent, *blocks]
    in_specs = [
        SMEM,
        SMEM,
        tile,
        pl.BlockSpec((SOURCES, 1, TOK + NOTES, D), lambda i: (i, m, 0, 0)),
    ] + [fixed(b.shape) for b in blocks]
    ins = [*after, *ins]
    in_specs = [ANY] * len(after) + in_specs
    outs = [shape((SLOTS, D) if last else (EXPERTS, TOK, D), BF), shape((SLOTS, D), BF)]
    dense = pl.BlockSpec((SOURCES, TOK, D), lambda i: (i, 0, 0))
    out_specs = [tile if last else dense, tile]
    if m > 0:
        ins.append(prev)
        in_specs.append(fixed((3, D, F)))
    if last:
        outs.append(shape((SHARDS, 3, D, 128), BF))
        out_specs.append(fixed((SHARDS, 3, D, 128)))
    else:
        outs.append(shape((3, D, F), F32))
        out_specs.append(fixed((3, D, F)))
    return pl.pallas_call(
        functools.partial(expert_body, m, last, len(after)),
        grid=(tiles,),
        in_specs=in_specs,
        out_specs=out_specs,
        out_shape=outs,
        scratch_shapes=[pltpu.VMEM((D, F), BF)] * 3 + [pltpu.VMEM((3, D, F), F32)],
        compiler_params=pltpu.CompilerParams(
            vmem_limit_bytes=63 * 1024 * 1024, dimension_semantics=("arbitrary",)
        ),
        cost_estimate=cost(MICROSECONDS["expert"]),
        name="expert",
    )(*ins)


def returned_body(m, back, c01, middle, gains, dy, branch_ref, gain_ref):
    upstream = dot(c01[...], back[...])
    mid = middle[...]
    r = lax.rsqrt(jnp.mean(mid * mid, axis=-1, keepdims=True) + EPS)
    scaled = upstream * gains[8:9, :]
    grad = r * scaled - mid * (r * r * r) * jnp.mean(scaled * mid, axis=-1, keepdims=True)
    branch_ref[...] = (dy[m, 0:TOK, :].astype(F32) + grad).astype(BF)
    gain_ref[...] = jnp.broadcast_to(jnp.sum(upstream * mid * r, axis=0, keepdims=True), (8, D))


def block_body(micro, mixture, slots, c01, *refs):
    for m in range(micro - 1):
        refs[-1][m] = (refs[m][...] + mixture[...].astype(F32)).astype(BF)
    refs[-1][micro - 1] = (refs[micro - 1][...] + dot(c01[...], slots[...])).astype(BF)


def place_body(micro, place, order, rows, out_ref):
    given = iota((TOK, GT), 0) + TOK * x_of(place)
    for m in range(micro):
        deal = jnp.where(given == order[m], 1.0, 0.0).astype(BF)
        dealt = jnp.concatenate([rows[s, m] for s in range(SHARDS)], axis=0)
        out_ref[m] = dot(deal, dealt).astype(BF)


def attend_back_body(m, last, place, lengths, order, g0, g1, g2, g3, xr, qkv_ref, mixed, mass, w, wo, *refs):
    x, first_length = x_of(place), lengths[m, 0, 0]
    if last:
        prev_w, prev_o, gain0, gain1, *refs = refs
        before, refs = refs[:4], refs[4:]
    o0, o1, o2, o3, given_ref, *refs = refs
    deal = given_by_dealt(order, m, x)
    branch = stack((g0, g1, g2, g3))
    given_ref[...] = dot(deal[0:TOK], branch).astype(BF)
    sum_o = dot(mixed[...], branch, 0, 0)
    grad_mixed = dot(branch, wo[...], 1, 1).astype(BF)
    qkv = qkv_ref[...]
    same = same_documents(x, first_length)
    grad_q, grad_k, grad_v = [], [], []
    for g in range(KV_HERE):
        k = qkv[:, QC + g * HEAD : QC + (g + 1) * HEAD]
        v = qkv[:, QC + KC + g * HEAD : QC + KC + (g + 1) * HEAD]
        sum_k = jnp.zeros((HEAD, GT), F32)
        sum_v = jnp.zeros((HEAD, GT), F32)
        for r in range(HEADS // KV_HEADS):
            h = g * (HEADS // KV_HEADS) + r
            q = qkv[:, h * HEAD : (h + 1) * HEAD]
            gm = grad_mixed[:, h * HEAD : (h + 1) * HEAD]
            scores = jnp.where(same, dot(q, k, 1, 1) * SCALE, MASKED)
            probs = jnp.exp(scores - mass[:, h * 32 : h * 32 + 1])
            grad_probs = dot(gm, v, 1, 1)
            sum_v += dot(gm, probs.astype(BF), 0, 0)
            weighted = probs * grad_probs
            grad_scores = weighted - probs * jnp.sum(weighted, axis=-1, keepdims=True)
            grad_scores = grad_scores.astype(BF)
            grad_q.append((dot(grad_scores, k) * SCALE).astype(BF))
            sum_k += dot(q, grad_scores, 0, 0)
        grad_k.append((sum_k * SCALE).astype(BF))
        grad_v.append(sum_v.astype(BF))
    grad_kv = jnp.concatenate(grad_k + grad_v, axis=0).astype(F32).T.astype(BF)
    grad_qkv = jnp.concatenate(grad_q + [grad_kv], axis=1)
    sum_w = dot(xr[...], grad_qkv, 0, 0)
    part = dot(grad_qkv, w[...], 1, 1).astype(BF)
    part = dot(deal, part).astype(BF)
    for k, out in enumerate((o0, o1, o2, o3)):
        if last:
            out[0] = before[k][...]
            out[1] = part[k * TOK : (k + 1) * TOK]
        else:
            out[...] = part[k * TOK : (k + 1) * TOK]
    if not last:
        sum_w_ref, sum_o_ref = refs
        sum_w_ref[...] = sum_w
        sum_o_ref[...] = sum_o
        return
    keep_ref, send_ref, all_w, all_o = refs
    c = core_of(place)
    all_w[...] = sum_w + prev_w[...]
    all_o[...] = sum_o + prev_o[...]
    gain = gain0[...] + gain1[...]
    for ref, half in ((keep_ref, c), (send_ref, 1 - c)):
        at = pl.ds(pl.multiple_of(half * 256, 256), 256)
        ref[0:D, :] = all_w[:, at].astype(ref.dtype)
        for j in range(2):
            at = pl.ds(pl.multiple_of(j * 512 + half * 256, 256), 256)
            ref[D + j * 256 : D + (j + 1) * 256, :] = all_o[:, at].astype(ref.dtype)
        tile = jnp.concatenate(
            [gain[0:1, b * 256 : (b + 1) * 256] for b in range(4)] + [jnp.zeros((12, 256), F32)], axis=0
        )
        for j in range(16):
            ref[6 * 256 + j * 16 : 6 * 256 + (j + 1) * 16, :] = tile.astype(ref.dtype)


def tokens_body(micro, tokens, gains, p0, p1, p2, p3, *refs):
    for m in range(micro):
        upstream = (p0[m].astype(F32) + p1[m].astype(F32)) + (
            p2[m].astype(F32) + p3[m].astype(F32)
        )
        v = tokens[m].astype(F32)
        r = lax.rsqrt(jnp.mean(v * v, axis=-1, keepdims=True) + EPS)
        scaled = upstream * gains[0:1, :]
        grad = r * scaled - v * (r * r * r) * jnp.mean(scaled * v, axis=-1, keepdims=True)
        refs[-1][m] = (refs[m][...].astype(F32) + grad).astype(BF)


def weight_sums_body(sums, *outs):
    for j in range(3):
        outs[j][0] = sums[j].astype(F32)


def weight_stack_body(a, b, c, out_ref):
    for j, ref in enumerate((a, b, c)):
        for half in range(2):
            out_ref[half, j] = ref[0, half * (D // 2) : (half + 1) * (D // 2)]


BLOCKS = 7


def split_y_body(place, keep, got, own_ref, s1, s2, s3):
    y = y_of(place)
    for b in range(BLOCKS):
        for k, ref in enumerate((own_ref, s1, s2, s3)):
            at = pl.ds(pl.multiple_of(b * 256 + ((y + k) & 3) * 64, 64), 64)
            ref[b * 64 : (b + 1) * 64, :] = (keep[at, :] + got[at, :].astype(F32)).astype(ref.dtype)


def split_z_body(place, own, r1, r2, r3, own_ref, s1, s2, s3):
    z = z_of(place)
    for b in range(BLOCKS):
        for k, ref in enumerate((own_ref, s1, s2, s3)):
            at = pl.ds(pl.multiple_of(b * 64 + ((z + k) & 3) * 16, 16), 16)
            total = (own[at, :] + r1[at, :].astype(F32)) + (
                r2[at, :].astype(F32) + r3[at, :].astype(F32)
            )
            ref[b * 16 : (b + 1) * 16, :] = total.astype(ref.dtype)


def split_x_body(place, own, r1, r2, r3, o_ref, own_ref, s1, s2, s3):
    x = x_of(place)

    def total(at):
        return (own[at, :] + r1[at, :].astype(F32)) + (r2[at, :].astype(F32) + r3[at, :].astype(F32))

    gain = total(slice(96, 112))
    row = iota((16, 256), 0)
    for k, ref in enumerate((own_ref, s1, s2, s3)):
        s = (x + k) & 3
        ref[0:16, :] = total(pl.ds(pl.multiple_of(s * 16, 16), 16)).astype(ref.dtype)
        mine = jnp.sum(jnp.where(row == s, gain, 0.0), axis=0, keepdims=True)
        ref[16:32, :] = jnp.broadcast_to(mine, (16, 256)).astype(ref.dtype)
    o_ref[...] = total(slice(64, 96)).astype(BF)


def join_x_body(place, o, own, r1, r2, r3, out_ref, gain_ref):
    x = x_of(place)
    gain = jnp.zeros((16, 256), F32)
    for k, ref in enumerate((own, r1, r2, r3)):
        s = (x - k) & 3
        out_ref[pl.ds(pl.multiple_of(s * 16, 16), 16), :] = ref[0:16, :].astype(BF)
        gain += ref[16:32, :].astype(F32)
    out_ref[64:96, :] = o[...]
    gain_ref[...] = gain[0:1]


def join_body(index_of, place, own, r1, r2, r3, out_ref):
    at = index_of(place)
    rows = own.shape[0]
    for k, ref in enumerate((own, r1, r2, r3)):
        s = (at + k) & 3
        out_ref[pl.ds(pl.multiple_of(s * rows, rows), rows), :] = ref[...]


def weights_body(place, own, got, wq, wk, wv, gain, q_ref, k_ref, v_ref, o_ref, gain_ref):
    c = core_of(place)
    scale = gain[...]
    total = jnp.zeros((ROWS_HERE, 1), F32)

    def piece(ref, b):
        return jnp.concatenate(
            [ref[j * 96 + b * 16 : j * 96 + (b + 1) * 16, :] for j in range(16)], axis=0
        ).astype(F32)

    for b in range(6):
        mine, other = piece(own, b), piece(got, b)
        left = jnp.where(c == 0, mine, other)
        right = jnp.where(c == 0, other, mine)
        if b < 4:
            q_ref[:, b * QC : (b + 1) * QC] = left * scale
            k_ref[:, b * KC : (b + 1) * KC] = right[:, 0:KC] * scale
            v_ref[:, b * KC : (b + 1) * KC] = right[:, KC : 2 * KC] * scale
            total += jnp.sum(
                left * wq[:, b * QC : (b + 1) * QC].astype(F32), axis=1, keepdims=True
            )
            total += jnp.sum(
                right[:, 0:KC] * wk[:, b * KC : (b + 1) * KC].astype(F32), axis=1, keepdims=True
            )
            total += jnp.sum(
                right[:, KC : 2 * KC] * wv[:, b * KC : (b + 1) * KC].astype(F32),
                axis=1,
                keepdims=True,
            )
        else:
            o_ref[:, (b - 4) * 512 : (b - 4) * 512 + 256] = left
            o_ref[:, (b - 4) * 512 + 256 : (b - 3) * 512] = right
    gain_ref[...] = jnp.broadcast_to(total, (ROWS_HERE, 128)).T[0:1]


def from_right(v, k):
    return lax.ppermute(v, "shard", [(i, (i - k) % SHARDS) for i in range(SHARDS)])


def to_right(v, k):
    return lax.ppermute(v, "shard", [(i, (i + k) % SHARDS) for i in range(SHARDS)])


def gather_x(v):
    return [v] + [from_right(v, k) for k in (1, 2, 3)]


def gather_ring(v):
    half = v.shape[0] // 2
    right, left = from_right(v, 1), from_right(v, 3)
    return [v, right, left, from_right(right[:half], 1), from_right(left[half:], 3)]


def hold(arrays, *others):
    count = len(arrays)
    return pl.pallas_call(
        lambda *refs: None,
        out_shape=[shape(v.shape, v.dtype) for v in arrays],
        in_specs=[ANY] * (count + len(others)),
        out_specs=[ANY] * count,
        input_output_aliases={i: i for i in range(count)},
        cost_estimate=cost(0),
        name="hold",
    )(*arrays, *others)


def scatter_x(blocks):
    return [blocks[0]] + [to_right(blocks[k], k) for k in (1, 2, 3)]


def along(v, step):
    pairs = []
    for i in range(EXPERTS):
        z, y, c = step(i // 8, (i // 2) % 4, i % 2)
        pairs.append((i, (z % 4) * 8 + (y % 4) * 2 + c % 2))
    return lax.ppermute(v, "expert", pairs)


def swap_core(v):
    return along(v, lambda z, y, c: (z, y, 1 - c))


def sum_over_experts(v):
    return lax.psum_scatter(v, "expert", scatter_dimension=0, tiled=True)


def exchange(v):
    return lax.all_to_all(v, "expert", split_axis=0, concat_axis=0, tiled=True)


def per_device(
    tokens,
    cotangent,
    order,
    lengths,
    routes,
    gate_weights,
    capacity,
    gain_attn,
    w_query,
    w_key,
    w_value,
    w_out,
    gain_ffn,
    w_gate,
    w_up,
    w_down,
):
    micro = tokens.shape[0]
    place = lax.axis_index(("expert", "shard")).astype(I32).reshape(1)
    cap = capacity.reshape(1, EXPERTS)
    experts = jnp.swapaxes(routes, 1, 2)
    gates = jnp.swapaxes(gate_weights, 1, 2)

    cot_rows = gather_x(cotangent)
    *packs, tokens_first = run(
        "pack",
        pack_body,
        [shape((ROWS_HERE + 16, COLS), BF)] * 4 + [shape((TOK, D), BF)],
        [
            place,
            w_query,
            w_key,
            w_value,
            jnp.concatenate([gain_attn, gain_ffn]).reshape(1, -1),
            tokens,
        ],
        smem=(0,),
    )
    pack_done = tokens_first
    waited = hold([*packs, tokens_first], *cot_rows[1:])
    packs, tokens_first = waited[:SHARDS], waited[SHARDS]
    token_rows = gather_x(tokens_first)
    packs = [packs[0]] + [from_right(packs[k], k) for k in (1, 2, 3)]
    routed = run(
        "route",
        functools.partial(route_body, micro),
        [shape((TOK, D), BF)] * (micro - 1)
        + [shape((TOK, SLOTS), BF), shape((SLOTS, TOK), BF)] * micro,
        [experts, cap, tokens],
        after=[pack_done],
    )
    token_copies, routed = routed[: micro - 1], routed[micro - 1 :]
    routed = [routed[2 * m : 2 * m + 2] for m in range(micro)]

    weights = run(
        "weight_stack",
        weight_stack_body,
        [shape((2, 3, D // 2, 128), BF)],
        [w_gate, w_up, w_down],
        after=routed[0][:1],
    )[0]
    attended, left, reached = [], [], []
    w_qkv = gains = weight_blocks = None

    dealt_cot = run(
        "deal",
        functools.partial(deal_body, micro),
        [shape((micro, TOK + NOTES, D), BF)],
        [place, order, experts, gates, *cot_rows],
        smem=(0,),
        after=[pack_done, routed[0][0]],
    )[0]
    cot_all = lax.all_gather(dealt_cot, "expert", axis=0)
    for m in range(micro):
        first = m == 0
        if not first:
            token_rows = gather_x(hold([token_copies[m - 1]], left[-1][1])[0])
            weight_blocks = gather_ring(hold([weights], *token_rows[1:])[0])
        outs = [shape((TOK, D), BF)] * 5 + [
            shape((GT, D), BF),
            shape((GT, COLS), BF),
            shape((GT, QC), BF),
            shape((GT, 128), F32),
        ]
        if first:
            outs += [shape((D, COLS), BF), shape((16, D), F32)]
        result = run(
            "attend",
            functools.partial(attend_body, m),
            outs,
            [place, lengths, order, *token_rows, w_out, *(packs if first else (w_qkv, gains))],
            smem=(0, 1),
            after=[dealt_cot] if first else [],
        )
        if first:
            w_qkv, gains = result[9:]
        attended.append(result[:9])
        parts = scatter_x(result[:4])
        left.append(
            run(
                "leave",
                leave_body,
                [shape((TOK, D), F32), shape((SLOTS, D), BF)],
                [*parts, result[4], gains, routed[m][1]],
                after=[weights] if first else weight_blocks[1:3],
            )
        )
        reached.append(exchange(left[m][1]))

    backs, mixtures, sums = [], [], None
    for m in range(micro):
        result = expert_call(
            m,
            micro,
            place,
            cap,
            reached[m],
            cot_all,
            weight_blocks,
            sums,
            after=[left[-1][1]] if m == 0 else [],
        )
        if m < micro - 1:
            dense, back = hold(result[:2], reached[-1])
            mixtures.append(sum_over_experts(dense.reshape(-1, D)))
        else:
            last_out, back = result[0], hold([result[1]], backs[m - 1])[0]
        backs.append(exchange(back))
        sums = result[2]

    sum_w = sum_o = None
    gain_sums, givens = [], []
    for m in range(micro):
        last = m == micro - 1
        branch, gain_sum = run(
            "returned",
            functools.partial(returned_body, m),
            [shape((TOK, D), BF), shape((8, D), F32)],
            [backs[m], routed[m][0], left[m][0], gains, dealt_cot],
            after=() if m == 0 else (sum_w,),
        )
        branch_rows = gather_x(branch)
        if last:
            mixtures.append(exchange(hold([last_out], branch)[0]))
        else:
            sums = lax.psum_scatter(
                sums.reshape(-1, 128), "shard", scatter_dimension=0, tiled=True
            )
            totals = run(
                "weight_sums",
                weight_sums_body,
                [shape((1, D, 128), F32)] * 3,
                [sums.reshape(3, D, 128)],
            )
        gain_sums.append(gain_sum)
        ins = [place, lengths, order, *branch_rows, *attended[m][5:9], w_qkv, w_out]
        out_shapes = [shape((TOK, D), BF)] * 5
        scratch = []
        if last:
            ins += [sum_w, sum_o, *gain_sums, *parts]
            out_shapes = [shape((micro, TOK, D), BF)] * 4 + out_shapes[4:]
            out_shapes += [shape((BLOCKS * 256, 256), F32), shape((BLOCKS * 256, 256), BF)]
            scratch = [pltpu.VMEM((D, COLS), F32), pltpu.VMEM((ROWS_HERE, D), F32)]
        else:
            out_shapes += [shape((D, COLS), F32), shape((ROWS_HERE, D), F32)]
        result = run(
            "attend_back",
            functools.partial(attend_back_body, m, last),
            out_shapes,
            ins,
            smem=(0, 1),
            scratch=scratch,
        )
        sum_w, sum_o = result[5:7]
        parts = result[:4]
        givens.append(result[4])

    four = [0, 1, 2, 3]
    rows = BLOCKS * 64
    split_y = run(
        "split_y",
        split_y_body,
        [shape((rows, 256), F32)] + [shape((rows, 256), BF)] * 3,
        [place, sum_w, swap_core(sum_o)],
        smem=(0,),
    )
    pieces = [split_y[0]] + [along(split_y[k], lambda z, y, c, k=k: (z, y + k, c)) for k in four[1:]]
    rows = BLOCKS * 16
    split_z, *pieces = run(
        "split_z",
        split_z_body,
        [shape((rows, 256), F32)] + [shape((rows, 256), BF)] * 3,
        [place, *pieces],
        smem=(0,),
    )
    pieces = [split_z] + [
        along(pieces[k - 1], lambda z, y, c, k=k: (z + k, y, c)) for k in four[1:]
    ]
    blocks = run(
        "block",
        functools.partial(block_body, micro),
        [shape((micro, TOK, D), BF)],
        [*mixtures, routed[-1][0], *[left[m][0] for m in range(micro)]],
        after=[split_z],
    )[0]
    block_out = run(
        "place",
        functools.partial(place_body, micro),
        [shape(tokens.shape, BF)],
        [place, order, lax.all_gather(blocks, "shard", axis=0)],
        smem=(0,),
    )[0]
    o_piece, *pieces = run(
        "split_x",
        split_x_body,
        [shape((32, 256), BF), shape((32, 256), F32)] + [shape((32, 256), BF)] * 3,
        [place, *pieces],
        smem=(0,),
        after=[blocks],
    )
    piece, gain_ffn_sum = run(
        "join_x",
        join_x_body,
        [shape((96, 256), BF), shape((1, 256), F32)],
        [place, o_piece, *scatter_x(pieces)],
        smem=(0,),
    )
    grad_tokens = run(
        "tokens",
        functools.partial(tokens_body, micro),
        [shape(tokens.shape, BF)],
        [tokens, gains, *scatter_x(hold(parts, piece)), *givens],
    )[0]
    for name, index_of, step in (
        ("join_z", z_of, lambda z, y, c, k: (z - k, y, c)),
        ("join_y", y_of, lambda z, y, c, k: (z, y - k, c)),
    ):
        pieces = [piece] + [
            along(piece, lambda z, y, c, k=k, step=step: step(z, y, c, k)) for k in four[1:]
        ]
        piece = run(
            name,
            functools.partial(join_body, index_of),
            [shape((4 * piece.shape[0], 256), BF)],
            [place, *pieces],
            smem=(0,),
            after=[grad_tokens] if name == "join_y" else [],
        )[0]
    grad_query, grad_key, grad_value, grad_out, grad_gain = run(
        "weights",
        weights_body,
        [
            shape(w_query.shape, F32),
            shape(w_key.shape, F32),
            shape(w_value.shape, F32),
            shape(w_out.shape, F32),
            shape((1, ROWS_HERE), F32),
        ],
        [
            place,
            piece,
            swap_core(piece),
            w_query,
            w_key,
            w_value,
            gain_attn.astype(F32).reshape(-1, 1),
        ],
        smem=(0,),
    )

    return (
        block_out,
        grad_tokens,
        grad_gain.reshape(-1),
        grad_query,
        grad_key,
        grad_value,
        grad_out,
        gain_ffn_sum.reshape(-1),
        *totals,
    )


def solution(mesh):
    return jax.shard_map(
        per_device,
        mesh=mesh,
        in_specs=(
            P(None, ("expert", "shard"), None),
            P(None, ("expert", "shard"), None),
            P(None, "expert", None),
            P(None, "expert", None),
            P(None, ("expert", "shard"), None),
            P(None, ("expert", "shard"), None),
            P(),
            P("shard"),
            P("shard", None),
            P("shard", None),
            P("shard", None),
            P("shard", None),
            P("shard"),
            P("expert", None, "shard"),
            P("expert", None, "shard"),
            P("expert", None, "shard"),
        ),
        out_specs=(
            P(None, ("expert", "shard"), None),
            P(None, ("expert", "shard"), None),
            P("shard"),
            P("shard", None),
            P("shard", None),
            P("shard", None),
            P("shard", None),
            P("shard"),
            P("expert", None, "shard"),
            P("expert", None, "shard"),
            P("expert", None, "shard"),
        ),
        check_vma=False,
    )
```

```python
import functools

import jax
import jax.numpy as jnp
from jax import lax
from jax.experimental import pallas as pl
from jax.experimental.pallas import tpu as pltpu
from jax.sharding import PartitionSpec as P

D = 1024
HEADS = 16
KV_HEADS = 8
HEAD = 64
F = 512
EXPERTS = 32
TOPK = 8
CAP = 48
TOK = 128
GT = 512
SHARDS = 4
SLOTS = EXPERTS * CAP
HEADS_HERE = HEADS // SHARDS
KV_HERE = KV_HEADS // SHARDS
QC = HEADS_HERE * HEAD
KC = KV_HERE * HEAD
COLS = QC + 2 * KC
ROWS_HERE = D // SHARDS

EPS = 1e-05
MASKED = -1e30
SCALE = HEAD ** (-0.5)

BF = jnp.bfloat16
F32 = jnp.float32
I32 = jnp.int32

VMEM = pl.BlockSpec(memory_space=pltpu.VMEM)
SMEM = pl.BlockSpec(memory_space=pltpu.SMEM)
ANY = pl.BlockSpec(memory_space=pl.ANY)


def dot(a, b, ca=1, cb=0):
    return lax.dot_general(a, b, (((ca,), (cb,)), ((), ())), preferred_element_type=F32)


def shape(dims, dtype):
    return jax.ShapeDtypeStruct(dims, dtype)


MICROSECONDS = {
    "pack": 2.5,
    "route": 4.5,
    "deal": 3.5,
    "weight_stack": 2.0,
    "attend": 7.3,
    "leave": 4.3,
    "expert": 27.0,
    "returned": 3.7,
    "attend_back": 11.0,
    "weight_sums": 2.0,
    "split_y": 2.8,
    "sum_y": 2.0,
    "split_x": 2.4,
    "join_x": 1.5,
    "join_y": 2.2,
    "block": 4.5,
    "place": 2.8,
    "tokens": 3.4,
    "weights": 3.9,
}


def cost(microseconds):
    return pl.CostEstimate(
        flops=1, bytes_accessed=int(3.6e6 * microseconds) + 1, transcendentals=0
    )


def run(name, body, outs, ins, smem=(), scratch=(), limit=63, after=()):
    count = len(ins)

    def whole(*refs):
        body(*refs[:count], *refs[count + len(after) :])

    ins = [*ins, *after]
    return pl.pallas_call(
        whole,
        out_shape=outs,
        in_specs=[SMEM if i in smem else VMEM for i in range(count)] + [ANY] * len(after),
        out_specs=[VMEM] * len(outs),
        scratch_shapes=list(scratch),
        compiler_params=pltpu.CompilerParams(vmem_limit_bytes=limit * 1024 * 1024),
        cost_estimate=cost(MICROSECONDS[name]),
        name=name,
    )(*ins)


def iota(dims, axis):
    return lax.broadcasted_iota(I32, dims, axis)


def x_of(place):
    return place[0] & 3


def core_of(place):
    return (place[0] >> 2) & 1


def y_of(place):
    return (place[0] >> 3) & 3


def z_of(place):
    return place[0] >> 5


def rolled_order(order_ref, m, x):
    rows = [
        order_ref[m, :, pl.ds(pl.multiple_of(((x + k) & 3) * TOK, TOK), TOK)] for k in range(SHARDS)
    ]
    return (jnp.concatenate(rows, axis=1) - TOK * x) & (GT - 1)


def given_by_dealt(order_ref, m, x, rows=GT):
    return jnp.where(iota((rows, GT), 0) == rolled_order(order_ref, m, x), 1.0, 0.0).astype(BF)


def stack(refs):
    return jnp.concatenate([r[...] for r in refs], axis=0)


def same_documents(x, first_length):
    across = ((iota((GT, GT), 1) + TOK * x) & (GT - 1)) >= first_length
    down = ((iota((GT, GT), 0) + TOK * x) & (GT - 1)) >= first_length
    return jnp.logical_not(jnp.logical_xor(across, down))


def pack_body(place, wq, wk, wv, gains, tokens, *outs):
    x = x_of(place)
    outs[4][...] = tokens[0]
    for k in range(SHARDS):
        s = (x - k) & 3
        outs[k][0:ROWS_HERE, 0:QC] = wq[:, pl.ds(pl.multiple_of(s * QC, QC), QC)]
        outs[k][0:ROWS_HERE, QC : QC + KC] = wk[:, pl.ds(pl.multiple_of(s * KC, KC), KC)]
        outs[k][0:ROWS_HERE, QC + KC : COLS] = wv[:, pl.ds(pl.multiple_of(s * KC, KC), KC)]
        outs[k][ROWS_HERE : ROWS_HERE + 16, :] = jnp.broadcast_to(gains[...], (16, 2 * ROWS_HERE))


def unpack(x, packs, w_out, gains_out):
    for k in range(SHARDS):
        s = (x + k) & 3
        w_out[pl.ds(pl.multiple_of(s * ROWS_HERE, ROWS_HERE), ROWS_HERE), :] = packs[k][
            0:ROWS_HERE, :
        ]
    rows = [p[ROWS_HERE : ROWS_HERE + 16, :].astype(F32)[0:8] for p in packs]
    for half in range(2):
        for b in range(SHARDS):
            total = jnp.zeros((8, ROWS_HERE), F32)
            for k in range(SHARDS):
                piece = rows[k][:, half * ROWS_HERE : (half + 1) * ROWS_HERE]
                total = jnp.where(((x + k) & 3) == b, piece, total)
            gains_out[half * 8 : half * 8 + 8, b * ROWS_HERE : (b + 1) * ROWS_HERE] = total


def route_body(micro, routes, cap, tokens, *refs):
    for m in range(1, micro):
        refs[m - 1][...] = tokens[m]
    outs = refs[micro - 1 :]
    named = iota((EXPERTS, TOK), 0)
    earlier = jnp.where(iota((TOK, TOK), 0) < iota((TOK, TOK), 1), 1.0, 0.0).astype(BF)
    one = iota((EXPERTS, EXPERTS), 0) == iota((EXPERTS, EXPERTS), 1)
    limit = jnp.sum(jnp.where(one, cap[...], 0).astype(F32), axis=1, keepdims=True)
    first = iota((EXPERTS, SLOTS), 0) * CAP
    slot = iota((EXPERTS, SLOTS), 1)
    spread = jnp.where(jnp.logical_and(slot >= first, slot < first + CAP), 1.0, 0.0).astype(BF)
    within = (iota((TOK, SLOTS), 1) % CAP).astype(F32)
    within_t = (iota((SLOTS, TOK), 0) % CAP).astype(F32)
    for m in range(micro):
        c01_ref, d01_ref = outs[2 * m : 2 * m + 2]
        hits = jnp.zeros((EXPERTS, TOK), F32)
        for k in range(TOPK):
            hit = routes[m, k : k + 1, :] == named
            hits = jnp.where(hit, 1.0, hits)
        ranks = dot(hits.astype(BF), earlier)
        kept = jnp.logical_and(hits > 0.0, ranks < limit)
        place_of = jnp.where(kept, ranks, -1.0).astype(BF)
        own = dot(place_of, spread, 0, 0) == within
        c01_ref[...] = jnp.where(own, 1.0, 0.0).astype(BF)
        own_t = dot(spread, place_of, 0, 0) == within_t
        d01_ref[...] = jnp.where(own_t, 1.0, 0.0).astype(BF)


NOTES = 16


def deal_body(micro, place, order, routes, gates, c0, c1, c2, c3, out_ref):
    for m in range(micro):
        deal = given_by_dealt(order, m, x_of(place))[:, 0:TOK]
        rows = jnp.concatenate([c[m] for c in (c0, c1, c2, c3)], axis=0)
        out_ref[m, 0:TOK, :] = dot(deal, rows, 0, 0).astype(BF)
        experts = jnp.concatenate([routes[m, k : k + 1, :] for k in range(TOPK)], axis=1)
        weights = jnp.concatenate([gates[m, k : k + 1, :] for k in range(TOPK)], axis=1)
        high = weights.astype(BF).astype(F32)
        row = iota((NOTES, D), 0)
        notes = jnp.where(row == 1, high, weights - high)
        notes = jnp.where(row == 0, experts.astype(F32), notes)
        out_ref[m, TOK : TOK + NOTES, :] = notes.astype(BF)


def attend_body(m, place, lengths, order, t0, t1, t2, t3, wo, *refs):
    x, first_length = x_of(place), lengths[m, 0, 0]
    if m == 0:
        packs, refs = refs[:4], refs[4:]
        o0, o1, o2, o3, dealt_ref, xr_ref, qkv_ref, mixed_ref, mass_ref, w, gains = refs
        unpack(x, packs, w, gains)
    else:
        w, gains, o0, o1, o2, o3, dealt_ref, xr_ref, qkv_ref, mixed_ref, mass_ref = refs
    deal = given_by_dealt(order, m, x)
    dealt = dot(deal, stack((t0, t1, t2, t3)), 0, 0)
    dealt_ref[...] = dealt[0:TOK].astype(BF)
    scaled = dealt * lax.rsqrt(jnp.mean(dealt * dealt, axis=-1, keepdims=True) + EPS)
    xr_ref[...] = scaled.astype(BF)
    attn_in = (scaled * gains[0:1, :]).astype(BF)
    qkv = dot(attn_in, w[...]).astype(BF)
    qkv_ref[...] = qkv
    same = same_documents(x, first_length)
    heads = []
    masses = []
    for h in range(HEADS_HERE):
        g = h // (HEADS // KV_HEADS)
        q = qkv[:, h * HEAD : (h + 1) * HEAD]
        k = qkv[:, QC + g * HEAD : QC + (g + 1) * HEAD]
        v = qkv[:, QC + KC + g * HEAD : QC + KC + (g + 1) * HEAD]
        scores = jnp.where(same, dot(q, k, 1, 1) * SCALE, MASKED)
        highest = jnp.max(scores, axis=-1, keepdims=True)
        raised = jnp.exp(scores - highest)
        total = jnp.sum(raised, axis=-1, keepdims=True)
        probs = (raised * (1.0 / total)).astype(BF)
        heads.append(dot(probs, v).astype(BF))
        masses.append(jnp.broadcast_to(highest + jnp.log(total), (GT, 32)))
    mixed = jnp.concatenate(heads, axis=1)
    mixed_ref[...] = mixed
    mass_ref[...] = jnp.concatenate(masses, axis=1)
    part = dot(mixed, wo[...]).astype(BF)
    for k, out in enumerate((o0, o1, o2, o3)):
        out[...] = part[k * TOK : (k + 1) * TOK]


def leave_body(own, r1, r2, r3, dealt, gains, d01, middle_ref, rows_ref):
    middle = dealt[...].astype(F32) + (
        (own[...].astype(F32) + r1[...].astype(F32)) + (r2[...].astype(F32) + r3[...].astype(F32))
    )
    middle_ref[...] = middle
    r = lax.rsqrt(jnp.mean(middle * middle, axis=-1, keepdims=True) + EPS)
    ffn_in = (middle * r * gains[8:9, :]).astype(BF)
    rows_ref[...] = dot(d01[...], ffn_in).astype(BF)


SOURCES = 8
TILE = SOURCES * CAP


def expert_body(m, last, waits, *refs):
    refs = list(refs[waits:])
    place, cap, rows, cotangent = refs[:4]
    blocks = refs[4:9]
    refs = refs[9:]
    prev = None
    if m > 0:
        prev, refs = refs[0], refs[1:]
    out_ref, back_ref = refs[:2]
    if last:
        send_ref, (wg, wu, wd, acc) = refs[2], refs[3:]
    else:
        sums_ref, (wg, wu, wd, acc) = refs[2], refs[3:]
    step = pl.program_id(0)

    @pl.when(step == 0)
    def _():
        mine, right, left, first, second = blocks
        for k, ref in enumerate((mine, right, (first, second), left)):
            at = slice(k * 128, (k + 1) * 128)
            for half in range(2):
                piece = ref[half] if k != 2 else ref[half][0]
                rows_at = slice(half * (D // 2), (half + 1) * (D // 2))
                wg[rows_at, at] = piece[0]
                wu[rows_at, at] = piece[1]
                wd[rows_at, at] = piece[2]
        acc[...] = jnp.zeros(acc.shape, F32) if prev is None else prev[...]

    expert = place[0] >> 2
    notes = cotangent[:, 0, TOK : TOK + NOTES, :].astype(F32)
    named, high, low = (notes[:, j, :] for j in range(3))
    hits = jnp.zeros((SOURCES, TOK), F32)
    weight = jnp.zeros((SOURCES, TOK), F32)
    for k in range(TOPK):
        at = slice(k * TOK, (k + 1) * TOK)
        hit = named[:, at] == expert.astype(F32)
        hits = jnp.where(hit, 1.0, hits)
        weight = jnp.where(hit, high[:, at] + low[:, at], weight)
    earlier = jnp.where(iota((TOK, TOK), 0) < iota((TOK, TOK), 1), 1.0, 0.0).astype(BF)
    ranks = dot(hits.astype(BF), earlier)
    kept = jnp.logical_and(hits > 0.0, ranks < cap[0, expert].astype(F32))
    place_of = jnp.where(kept, ranks, -1.0)
    rank = iota((CAP, TOK), 0).astype(F32)
    picks, gates_of, grads = [], [], []
    for j in range(SOURCES):
        own = place_of[j : j + 1, :] == rank
        gate = jnp.sum(jnp.where(own, weight[j : j + 1, :], 0.0), axis=1, keepdims=True)
        pick = jnp.where(own, 1.0, 0.0).astype(BF)
        picks.append(pick)
        gates_of.append(gate)
        grads.append((dot(pick, cotangent[j, 0, 0:TOK, :]) * gate).astype(BF))
    grad = jnp.concatenate(grads, axis=0)
    row = rows[...]
    gate_of = jnp.concatenate(gates_of, axis=0)
    gate = dot(row, wg[...])
    up = dot(row, wu[...])
    sig = jax.nn.sigmoid(gate)
    silu = gate * sig
    hidden = (silu * up).astype(BF)
    weighted = (dot(hidden, wd[...], 1, 1) * gate_of).astype(BF)
    if last:
        out_ref[...] = weighted
    else:
        for j in range(SOURCES):
            out_ref[j] = dot(picks[j], weighted[j * CAP : (j + 1) * CAP], 0, 0).astype(BF)
    grad_hidden = dot(grad, wd[...])
    grad_gate = (grad_hidden * up * sig * (1.0 + gate * (1.0 - sig))).astype(BF)
    grad_up = (grad_hidden * silu).astype(BF)
    back_ref[...] = (dot(grad_gate, wg[...], 1, 1) + dot(grad_up, wu[...], 1, 1)).astype(BF)
    acc[0] += dot(row, grad_gate, 0, 0)
    acc[1] += dot(row, grad_up, 0, 0)
    acc[2] += dot(grad, hidden, 0, 0)

    @pl.when(step == pl.num_programs(0) - 1)
    def _():
        if last:
            for k in range(SHARDS):
                for j in range(3):
                    piece = acc[j, :, k * 128 : (k + 1) * 128].astype(BF)
                    send_ref[pl.ds((x_of(place) + k) & 3, 1), j] = piece[None]
        else:
            sums_ref[...] = acc[...]


def expert_call(m, micro, place, cap, rows, cotangent, blocks, prev, after=()):
    last = m == micro - 1
    tiles = SLOTS // TILE
    tile = pl.BlockSpec((TILE, D), lambda i: (i, 0))

    def fixed(dims):
        return pl.BlockSpec(dims, lambda i: (0,) * len(dims), pipeline_mode=pl.Buffered(1))

    ins = [place, cap, rows, cotangent, *blocks]
    in_specs = [
        SMEM,
        SMEM,
        tile,
        pl.BlockSpec((SOURCES, 1, TOK + NOTES, D), lambda i: (i, m, 0, 0)),
    ] + [fixed(b.shape) for b in blocks]
    ins = [*after, *ins]
    in_specs = [ANY] * len(after) + in_specs
    outs = [shape((SLOTS, D) if last else (EXPERTS, TOK, D), BF), shape((SLOTS, D), BF)]
    dense = pl.BlockSpec((SOURCES, TOK, D), lambda i: (i, 0, 0))
    out_specs = [tile if last else dense, tile]
    if m > 0:
        ins.append(prev)
        in_specs.append(fixed((3, D, F)))
    if last:
        outs.append(shape((SHARDS, 3, D, 128), BF))
        out_specs.append(fixed((SHARDS, 3, D, 128)))
    else:
        outs.append(shape((3, D, F), F32))
        out_specs.append(fixed((3, D, F)))
    return pl.pallas_call(
        functools.partial(expert_body, m, last, len(after)),
        grid=(tiles,),
        in_specs=in_specs,
        out_specs=out_specs,
        out_shape=outs,
        scratch_shapes=[pltpu.VMEM((D, F), BF)] * 3 + [pltpu.VMEM((3, D, F), F32)],
        compiler_params=pltpu.CompilerParams(
            vmem_limit_bytes=63 * 1024 * 1024, dimension_semantics=("arbitrary",)
        ),
        cost_estimate=cost(MICROSECONDS["expert"]),
        name="expert",
    )(*ins)


def returned_body(m, back, c01, middle, gains, dy, branch_ref, gain_ref):
    upstream = dot(c01[...], back[...])
    mid = middle[...]
    r = lax.rsqrt(jnp.mean(mid * mid, axis=-1, keepdims=True) + EPS)
    scaled = upstream * gains[8:9, :]
    grad = r * scaled - mid * (r * r * r) * jnp.mean(scaled * mid, axis=-1, keepdims=True)
    branch_ref[...] = (dy[m, 0:TOK, :].astype(F32) + grad).astype(BF)
    gain_ref[...] = jnp.broadcast_to(jnp.sum(upstream * mid * r, axis=0, keepdims=True), (8, D))


def block_body(micro, mixture, slots, c01, *refs):
    for m in range(micro - 1):
        refs[-1][m] = (refs[m][...] + mixture[...].astype(F32)).astype(BF)
    refs[-1][micro - 1] = (refs[micro - 1][...] + dot(c01[...], slots[...])).astype(BF)


def place_body(micro, place, order, rows, out_ref):
    given = iota((TOK, GT), 0) + TOK * x_of(place)
    for m in range(micro):
        deal = jnp.where(given == order[m], 1.0, 0.0).astype(BF)
        dealt = jnp.concatenate([rows[s, m] for s in range(SHARDS)], axis=0)
        out_ref[m] = dot(deal, dealt).astype(BF)


def attend_back_body(m, last, place, lengths, order, g0, g1, g2, g3, xr, qkv_ref, mixed, mass, w, wo, *refs):
    x, first_length = x_of(place), lengths[m, 0, 0]
    if last:
        prev_w, prev_o, gain0, gain1, *refs = refs
    o0, o1, o2, o3, given_ref, *refs = refs
    deal = given_by_dealt(order, m, x)
    branch = stack((g0, g1, g2, g3))
    given_ref[...] = dot(deal[0:TOK], branch).astype(BF)
    sum_o = dot(mixed[...], branch, 0, 0)
    grad_mixed = dot(branch, wo[...], 1, 1).astype(BF)
    qkv = qkv_ref[...]
    same = same_documents(x, first_length)
    grad_q, grad_k, grad_v = [], [], []
    for g in range(KV_HERE):
        k = qkv[:, QC + g * HEAD : QC + (g + 1) * HEAD]
        v = qkv[:, QC + KC + g * HEAD : QC + KC + (g + 1) * HEAD]
        sum_k = jnp.zeros((HEAD, GT), F32)
        sum_v = jnp.zeros((HEAD, GT), F32)
        for r in range(HEADS // KV_HEADS):
            h = g * (HEADS // KV_HEADS) + r
            q = qkv[:, h * HEAD : (h + 1) * HEAD]
            gm = grad_mixed[:, h * HEAD : (h + 1) * HEAD]
            scores = jnp.where(same, dot(q, k, 1, 1) * SCALE, MASKED)
            probs = jnp.exp(scores - mass[:, h * 32 : h * 32 + 1])
            grad_probs = dot(gm, v, 1, 1)
            sum_v += dot(gm, probs.astype(BF), 0, 0)
            weighted = probs * grad_probs
            grad_scores = weighted - probs * jnp.sum(weighted, axis=-1, keepdims=True)
            grad_scores = grad_scores.astype(BF)
            grad_q.append((dot(grad_scores, k) * SCALE).astype(BF))
            sum_k += dot(q, grad_scores, 0, 0)
        grad_k.append((sum_k * SCALE).astype(BF))
        grad_v.append(sum_v.astype(BF))
    grad_kv = jnp.concatenate(grad_k + grad_v, axis=0).astype(F32).T.astype(BF)
    grad_qkv = jnp.concatenate(grad_q + [grad_kv], axis=1)
    sum_w = dot(xr[...], grad_qkv, 0, 0)
    part = dot(grad_qkv, w[...], 1, 1).astype(BF)
    part = dot(deal, part).astype(BF)
    for k, out in enumerate((o0, o1, o2, o3)):
        out[...] = part[k * TOK : (k + 1) * TOK]
    if not last:
        sum_w_ref, sum_o_ref = refs
        sum_w_ref[...] = sum_w
        sum_o_ref[...] = sum_o
        return
    keep_ref, send_ref, all_w, all_o = refs
    c = core_of(place)
    all_w[...] = sum_w + prev_w[...]
    all_o[...] = sum_o + prev_o[...]
    gain = gain0[...] + gain1[...]
    for ref, half in ((keep_ref, c), (send_ref, 1 - c)):
        at = pl.ds(pl.multiple_of(half * 256, 256), 256)
        ref[0:D, :] = all_w[:, at].astype(ref.dtype)
        for j in range(2):
            at = pl.ds(pl.multiple_of(j * 512 + half * 256, 256), 256)
            ref[D + j * 256 : D + (j + 1) * 256, :] = all_o[:, at].astype(ref.dtype)
        tile = jnp.concatenate(
            [gain[0:1, b * 256 : (b + 1) * 256] for b in range(4)] + [jnp.zeros((12, 256), F32)], axis=0
        )
        for j in range(16):
            ref[6 * 256 + j * 16 : 6 * 256 + (j + 1) * 16, :] = tile.astype(ref.dtype)


def tokens_body(micro, tokens, gains, *refs):
    for m in range(micro):
        p0, p1, p2, p3, given = refs[5 * m : 5 * m + 5]
        upstream = (p0[...].astype(F32) + p1[...].astype(F32)) + (
            p2[...].astype(F32) + p3[...].astype(F32)
        )
        v = tokens[m].astype(F32)
        r = lax.rsqrt(jnp.mean(v * v, axis=-1, keepdims=True) + EPS)
        scaled = upstream * gains[0:1, :]
        grad = r * scaled - v * (r * r * r) * jnp.mean(scaled * v, axis=-1, keepdims=True)
        refs[-1][m] = (given[...].astype(F32) + grad).astype(BF)


def weight_sums_body(sums, *outs):
    for j in range(3):
        outs[j][0] = sums[j].astype(F32)


def weight_stack_body(a, b, c, out_ref):
    for j, ref in enumerate((a, b, c)):
        for half in range(2):
            out_ref[half, j] = ref[0, half * (D // 2) : (half + 1) * (D // 2)]


BLOCKS = 7


def split_y_body(place, keep, got, own_ref, s1, s2, s3):
    y = y_of(place)
    for b in range(BLOCKS):
        for k, ref in enumerate((own_ref, s1, s2, s3)):
            at = pl.ds(pl.multiple_of(b * 256 + ((y + k) & 3) * 64, 64), 64)
            ref[b * 64 : (b + 1) * 64, :] = (keep[at, :] + got[at, :].astype(F32)).astype(ref.dtype)


def sum_y_body(own, r1, r2, r3, out_ref):
    total = (own[...] + r1[...].astype(F32)) + (r2[...].astype(F32) + r3[...].astype(F32))
    out_ref[...] = total.astype(BF)


def split_x_body(place, own, r1, r2, r3, o_ref, own_ref, s1, s2, s3, held):
    x, z = x_of(place), z_of(place)
    for k, ref in enumerate((own, r1, r2, r3)):
        held[pl.ds((z - k) & 3, 1)] = ref[...][None]

    def total(at):
        return (held[0, at, :].astype(F32) + held[1, at, :].astype(F32)) + (
            held[2, at, :].astype(F32) + held[3, at, :].astype(F32)
        )

    gain = total(slice(384, 400))
    row = iota((16, 256), 0)
    for k, ref in enumerate((own_ref, s1, s2, s3)):
        s = (x + k) & 3
        ref[0:64, :] = total(pl.ds(pl.multiple_of(s * 64, 64), 64)).astype(BF)
        mine = jnp.sum(jnp.where(row == s, gain, 0.0), axis=0, keepdims=True)
        ref[64:80, :] = jnp.broadcast_to(mine, (16, 256)).astype(BF)
    o_ref[...] = total(slice(256, 384)).astype(BF)


def join_x_body(place, o, own, r1, r2, r3, out_ref, gain_ref):
    x = x_of(place)
    gain = jnp.zeros((16, 256), F32)
    for k, ref in enumerate((own, r1, r2, r3)):
        s = (x - k) & 3
        out_ref[pl.ds(pl.multiple_of(s * 64, 64), 64), :] = ref[0:64, :]
        gain += ref[64:80, :].astype(F32)
    out_ref[256:384, :] = o[...]
    gain_ref[...] = gain[0:1]


def join_y_body(place, own, r1, r2, r3, out_ref):
    rows = own.shape[0]
    for k, ref in enumerate((own, r1, r2, r3)):
        s = (y_of(place) + k) & 3
        out_ref[pl.ds(pl.multiple_of(s * rows, rows), rows), :] = ref[...]


def weights_body(place, own, got, wq, wk, wv, gain, q_ref, k_ref, v_ref, o_ref, gain_ref):
    c = core_of(place)
    scale = gain[...]
    total = jnp.zeros((ROWS_HERE, 1), F32)

    def piece(ref, b):
        return jnp.concatenate(
            [ref[j * 384 + b * 64 : j * 384 + (b + 1) * 64, :] for j in range(4)], axis=0
        ).astype(F32)

    for b in range(6):
        mine, other = piece(own, b), piece(got, b)
        left = jnp.where(c == 0, mine, other)
        right = jnp.where(c == 0, other, mine)
        if b < 4:
            q_ref[:, b * QC : (b + 1) * QC] = left * scale
            k_ref[:, b * KC : (b + 1) * KC] = right[:, 0:KC] * scale
            v_ref[:, b * KC : (b + 1) * KC] = right[:, KC : 2 * KC] * scale
            total += jnp.sum(
                left * wq[:, b * QC : (b + 1) * QC].astype(F32), axis=1, keepdims=True
            )
            total += jnp.sum(
                right[:, 0:KC] * wk[:, b * KC : (b + 1) * KC].astype(F32), axis=1, keepdims=True
            )
            total += jnp.sum(
                right[:, KC : 2 * KC] * wv[:, b * KC : (b + 1) * KC].astype(F32),
                axis=1,
                keepdims=True,
            )
        else:
            o_ref[:, (b - 4) * 512 : (b - 4) * 512 + 256] = left
            o_ref[:, (b - 4) * 512 + 256 : (b - 3) * 512] = right
    gain_ref[...] = jnp.broadcast_to(total, (ROWS_HERE, 128)).T[0:1]


def from_right(v, k):
    return lax.ppermute(v, "shard", [(i, (i - k) % SHARDS) for i in range(SHARDS)])


def to_right(v, k):
    return lax.ppermute(v, "shard", [(i, (i + k) % SHARDS) for i in range(SHARDS)])


def gather_x(v):
    return [v] + [from_right(v, k) for k in (1, 2, 3)]


def gather_ring(v):
    half = v.shape[0] // 2
    right, left = from_right(v, 1), from_right(v, 3)
    return [v, right, left, from_right(right[:half], 1), from_right(left[half:], 3)]


def hold(arrays, *others):
    count = len(arrays)
    return pl.pallas_call(
        lambda *refs: None,
        out_shape=[shape(v.shape, v.dtype) for v in arrays],
        in_specs=[ANY] * (count + len(others)),
        out_specs=[ANY] * count,
        input_output_aliases={i: i for i in range(count)},
        cost_estimate=cost(0),
        name="hold",
    )(*arrays, *others)


def scatter_x(blocks):
    return [blocks[0]] + [to_right(blocks[k], k) for k in (1, 2, 3)]


def along(v, step):
    pairs = []
    for i in range(EXPERTS):
        z, y, c = step(i // 8, (i // 2) % 4, i % 2)
        pairs.append((i, (z % 4) * 8 + (y % 4) * 2 + c % 2))
    return lax.ppermute(v, "expert", pairs)


def swap_core(v):
    return along(v, lambda z, y, c: (z, y, 1 - c))


def sum_over_experts(v):
    return lax.psum_scatter(v, "expert", scatter_dimension=0, tiled=True)


def exchange(v):
    return lax.all_to_all(v, "expert", split_axis=0, concat_axis=0, tiled=True)


def per_device(
    tokens,
    cotangent,
    order,
    lengths,
    routes,
    gate_weights,
    capacity,
    gain_attn,
    w_query,
    w_key,
    w_value,
    w_out,
    gain_ffn,
    w_gate,
    w_up,
    w_down,
):
    micro = tokens.shape[0]
    place = lax.axis_index(("expert", "shard")).astype(I32).reshape(1)
    cap = capacity.reshape(1, EXPERTS)
    experts = jnp.swapaxes(routes, 1, 2)
    gates = jnp.swapaxes(gate_weights, 1, 2)

    cot_rows = gather_x(cotangent)
    *packs, tokens_first = run(
        "pack",
        pack_body,
        [shape((ROWS_HERE + 16, COLS), BF)] * 4 + [shape((TOK, D), BF)],
        [
            place,
            w_query,
            w_key,
            w_value,
            jnp.concatenate([gain_attn, gain_ffn]).reshape(1, -1),
            tokens,
        ],
        smem=(0,),
    )
    pack_done = tokens_first
    waited = hold([*packs, tokens_first], *cot_rows[1:])
    packs, tokens_first = waited[:SHARDS], waited[SHARDS]
    token_rows = gather_x(tokens_first)
    packs = [packs[0]] + [from_right(packs[k], k) for k in (1, 2, 3)]
    routed = run(
        "route",
        functools.partial(route_body, micro),
        [shape((TOK, D), BF)] * (micro - 1)
        + [shape((TOK, SLOTS), BF), shape((SLOTS, TOK), BF)] * micro,
        [experts, cap, tokens],
        after=[pack_done],
    )
    token_copies, routed = routed[: micro - 1], routed[micro - 1 :]
    routed = [routed[2 * m : 2 * m + 2] for m in range(micro)]

    weights = run(
        "weight_stack",
        weight_stack_body,
        [shape((2, 3, D // 2, 128), BF)],
        [w_gate, w_up, w_down],
        after=routed[0][:1],
    )[0]
    attended, left, reached = [], [], []
    w_qkv = gains = weight_blocks = None

    dealt_cot = run(
        "deal",
        functools.partial(deal_body, micro),
        [shape((micro, TOK + NOTES, D), BF)],
        [place, order, experts, gates, *cot_rows],
        smem=(0,),
        after=[pack_done, routed[0][0]],
    )[0]
    cot_all = lax.all_gather(dealt_cot, "expert", axis=0)
    for m in range(micro):
        first = m == 0
        if not first:
            token_rows = later_rows
            weight_blocks = gather_ring(hold([weights], *token_rows[1:])[0])
        outs = [shape((TOK, D), BF)] * 5 + [
            shape((GT, D), BF),
            shape((GT, COLS), BF),
            shape((GT, QC), BF),
            shape((GT, 128), F32),
        ]
        if first:
            outs += [shape((D, COLS), BF), shape((16, D), F32)]
        result = run(
            "attend",
            functools.partial(attend_body, m),
            outs,
            [place, lengths, order, *token_rows, w_out, *(packs if first else (w_qkv, gains))],
            smem=(0, 1),
            after=[dealt_cot] if first else [],
        )
        if first:
            w_qkv, gains = result[9:]
        attended.append(result[:9])
        parts = scatter_x(result[:4])
        if first:
            later_rows = gather_x(hold([token_copies[m]], parts[1])[0])
        left.append(
            run(
                "leave",
                leave_body,
                [shape((TOK, D), F32), shape((SLOTS, D), BF)],
                [*parts, result[4], gains, routed[m][1]],
                after=[weights, *later_rows[1:]] if first else weight_blocks[1:3],
            )
        )
        reached.append(exchange(left[m][1]))

    backs, mixtures, sums = [], [], None
    for m in range(micro):
        result = expert_call(
            m,
            micro,
            place,
            cap,
            reached[m],
            cot_all,
            weight_blocks,
            sums,
            after=[left[-1][1]] if m == 0 else [],
        )
        if m < micro - 1:
            dense, back = hold(result[:2], reached[-1])
            mixtures.append(sum_over_experts(dense.reshape(-1, D)))
        else:
            last_out, back = result[0], hold([result[1]], backs[m - 1])[0]
        backs.append(exchange(back))
        sums = result[2]

    sum_w = sum_o = None
    gain_sums, grad_parts = [], []
    for m in range(micro):
        last = m == micro - 1
        branch, gain_sum = run(
            "returned",
            functools.partial(returned_body, m),
            [shape((TOK, D), BF), shape((8, D), F32)],
            [backs[m], routed[m][0], left[m][0], gains, dealt_cot],
            after=() if m == 0 else (sum_w, *grad_parts[1:4]),
        )
        branch_rows = gather_x(branch)
        if last:
            mixtures.append(exchange(hold([last_out], branch)[0]))
        else:
            sums = lax.psum_scatter(
                sums.reshape(-1, 128), "shard", scatter_dimension=0, tiled=True
            )
            totals = run(
                "weight_sums",
                weight_sums_body,
                [shape((1, D, 128), F32)] * 3,
                [sums.reshape(3, D, 128)],
            )
        gain_sums.append(gain_sum)
        ins = [place, lengths, order, *branch_rows, *attended[m][5:9], w_qkv, w_out]
        out_shapes = [shape((TOK, D), BF)] * 5
        scratch = []
        if last:
            ins += [sum_w, sum_o, *gain_sums]
            out_shapes += [shape((BLOCKS * 256, 256), F32), shape((BLOCKS * 256, 256), BF)]
            scratch = [pltpu.VMEM((D, COLS), F32), pltpu.VMEM((ROWS_HERE, D), F32)]
        else:
            out_shapes += [shape((D, COLS), F32), shape((ROWS_HERE, D), F32)]
        result = run(
            "attend_back",
            functools.partial(attend_back_body, m, last),
            out_shapes,
            ins,
            smem=(0, 1),
            scratch=scratch,
        )
        sum_w, sum_o = result[5:7]
        if last:
            last_parts = result[:5]
        else:
            grad_parts += [*scatter_x(result[:4]), result[4]]

    four = [0, 1, 2, 3]
    rows = BLOCKS * 64
    split_y = run(
        "split_y",
        split_y_body,
        [shape((rows, 256), F32)] + [shape((rows, 256), BF)] * 3,
        [place, sum_w, swap_core(sum_o)],
        smem=(0,),
    )
    pieces = [split_y[0]] + [along(split_y[k], lambda z, y, c, k=k: (z, y + k, c)) for k in four[1:]]
    last_parts = [*scatter_x(last_parts[:4]), last_parts[4]]
    sum_y = run(
        "sum_y", sum_y_body, [shape((rows, 256), BF)], pieces, after=last_parts[1:4]
    )[0]
    pieces = [sum_y] + [along(sum_y, lambda z, y, c, k=k: (z + k, y, c)) for k in four[1:]]
    blocks = run(
        "block",
        functools.partial(block_body, micro),
        [shape((micro, TOK, D), BF)],
        [*mixtures, routed[-1][0], *[left[m][0] for m in range(micro)]],
        after=[sum_y],
    )[0]
    block_out = run(
        "place",
        functools.partial(place_body, micro),
        [shape(tokens.shape, BF)],
        [place, order, lax.all_gather(blocks, "shard", axis=0)],
        smem=(0,),
    )[0]
    o_piece, *pieces = run(
        "split_x",
        split_x_body,
        [shape((128, 256), BF)] + [shape((80, 256), BF)] * 4,
        [place, *pieces],
        smem=(0,),
        scratch=[pltpu.VMEM((4, rows, 256), BF)],
        after=[blocks],
    )
    x_pieces = scatter_x(pieces)
    piece, gain_ffn_sum = run(
        "join_x",
        join_x_body,
        [shape((384, 256), BF), shape((1, 256), F32)],
        [place, o_piece, *x_pieces],
        smem=(0,),
    )
    grad_tokens = run(
        "tokens",
        functools.partial(tokens_body, micro),
        [shape(tokens.shape, BF)],
        [tokens, gains, *grad_parts, *last_parts],
    )[0]
    pieces = [piece] + [along(piece, lambda z, y, c, k=k: (z, y - k, c)) for k in four[1:]]
    piece = run(
        "join_y",
        join_y_body,
        [shape((1536, 256), BF)],
        [place, *pieces],
        smem=(0,),
        after=[grad_tokens, totals[0]],
    )[0]
    grad_query, grad_key, grad_value, grad_out, grad_gain = run(
        "weights",
        weights_body,
        [
            shape(w_query.shape, F32),
            shape(w_key.shape, F32),
            shape(w_value.shape, F32),
            shape(w_out.shape, F32),
            shape((1, ROWS_HERE), F32),
        ],
        [
            place,
            piece,
            swap_core(piece),
            w_query,
            w_key,
            w_value,
            gain_attn.astype(F32).reshape(-1, 1),
        ],
        smem=(0,),
        after=[block_out],
    )

    return (
        block_out,
        grad_tokens,
        grad_gain.reshape(-1),
        grad_query,
        grad_key,
        grad_value,
        grad_out,
        gain_ffn_sum.reshape(-1),
        *totals,
    )


def solution(mesh):
    return jax.shard_map(
        per_device,
        mesh=mesh,
        in_specs=(
            P(None, ("expert", "shard"), None),
            P(None, ("expert", "shard"), None),
            P(None, "expert", None),
            P(None, "expert", None),
            P(None, ("expert", "shard"), None),
            P(None, ("expert", "shard"), None),
            P(),
            P("shard"),
            P("shard", None),
            P("shard", None),
            P("shard", None),
            P("shard", None),
            P("shard"),
            P("expert", None, "shard"),
            P("expert", None, "shard"),
            P("expert", None, "shard"),
        ),
        out_specs=(
            P(None, ("expert", "shard"), None),
            P(None, ("expert", "shard"), None),
            P("shard"),
            P("shard", None),
            P("shard", None),
            P("shard", None),
            P("shard", None),
            P("shard"),
            P("expert", None, "shard"),
            P("expert", None, "shard"),
            P("expert", None, "shard"),
        ),
        check_vma=False,
    )
```

```python
import functools

import jax
import jax.numpy as jnp
from jax import lax
from jax.experimental import pallas as pl
from jax.experimental.pallas import tpu as pltpu
from jax.sharding import PartitionSpec as P

D = 1024
HEADS = 16
KV_HEADS = 8
HEAD = 64
F = 512
EXPERTS = 32
TOPK = 8
CAP = 48
TOK = 128
GT = 512
SHARDS = 4
SLOTS = EXPERTS * CAP
HEADS_HERE = HEADS // SHARDS
KV_HERE = KV_HEADS // SHARDS
QC = HEADS_HERE * HEAD
KC = KV_HERE * HEAD
COLS = QC + 2 * KC
ROWS_HERE = D // SHARDS

EPS = 1e-05
MASKED = -1e30
SCALE = HEAD ** (-0.5)

BF = jnp.bfloat16
F32 = jnp.float32
I32 = jnp.int32

VMEM = pl.BlockSpec(memory_space=pltpu.VMEM)
SMEM = pl.BlockSpec(memory_space=pltpu.SMEM)
ANY = pl.BlockSpec(memory_space=pl.ANY)


def dot(a, b, ca=1, cb=0):
    return lax.dot_general(a, b, (((ca,), (cb,)), ((), ())), preferred_element_type=F32)


def shape(dims, dtype):
    return jax.ShapeDtypeStruct(dims, dtype)


MICROSECONDS = {
    "pack": 2.5,
    "route": 4.5,
    "deal": 3.5,
    "weight_stack": 2.0,
    "attend": 7.3,
    "leave": 4.3,
    "expert": 27.0,
    "returned": 3.7,
    "attend_back": 11.0,
    "weight_sums": 2.0,
    "split_y": 2.8,
    "sum_y": 2.0,
    "split_x": 2.4,
    "join_x": 1.5,
    "join_y": 2.2,
    "block": 4.5,
    "tokens": 3.4,
    "finish": 5.5,
}


def cost(microseconds):
    return pl.CostEstimate(
        flops=1, bytes_accessed=int(3.6e6 * microseconds) + 1, transcendentals=0
    )


def run(name, body, outs, ins, smem=(), scratch=(), limit=63, after=()):
    count = len(ins)

    def whole(*refs):
        body(*refs[:count], *refs[count + len(after) :])

    ins = [*ins, *after]
    return pl.pallas_call(
        whole,
        out_shape=outs,
        in_specs=[SMEM if i in smem else VMEM for i in range(count)] + [ANY] * len(after),
        out_specs=[VMEM] * len(outs),
        scratch_shapes=list(scratch),
        compiler_params=pltpu.CompilerParams(vmem_limit_bytes=limit * 1024 * 1024),
        cost_estimate=cost(MICROSECONDS[name]),
        name=name,
    )(*ins)


def iota(dims, axis):
    return lax.broadcasted_iota(I32, dims, axis)


def x_of(place):
    return place[0] & 3


def core_of(place):
    return (place[0] >> 2) & 1


def y_of(place):
    return (place[0] >> 3) & 3


def z_of(place):
    return place[0] >> 5


def rolled_order(order_ref, m, x):
    rows = [
        order_ref[m, :, pl.ds(pl.multiple_of(((x + k) & 3) * TOK, TOK), TOK)] for k in range(SHARDS)
    ]
    return (jnp.concatenate(rows, axis=1) - TOK * x) & (GT - 1)


def given_by_dealt(order_ref, m, x, rows=GT):
    return jnp.where(iota((rows, GT), 0) == rolled_order(order_ref, m, x), 1.0, 0.0).astype(BF)


def stack(refs):
    return jnp.concatenate([r[...] for r in refs], axis=0)


def same_documents(x, first_length):
    across = ((iota((GT, GT), 1) + TOK * x) & (GT - 1)) >= first_length
    down = ((iota((GT, GT), 0) + TOK * x) & (GT - 1)) >= first_length
    return jnp.logical_not(jnp.logical_xor(across, down))


def pack_body(place, wq, wk, wv, gains, tokens, *outs):
    x = x_of(place)
    outs[4][...] = tokens[0]
    for k in range(SHARDS):
        s = (x - k) & 3
        outs[k][0:ROWS_HERE, 0:QC] = wq[:, pl.ds(pl.multiple_of(s * QC, QC), QC)]
        outs[k][0:ROWS_HERE, QC : QC + KC] = wk[:, pl.ds(pl.multiple_of(s * KC, KC), KC)]
        outs[k][0:ROWS_HERE, QC + KC : COLS] = wv[:, pl.ds(pl.multiple_of(s * KC, KC), KC)]
        outs[k][ROWS_HERE : ROWS_HERE + 16, :] = jnp.broadcast_to(gains[...], (16, 2 * ROWS_HERE))


def unpack(x, packs, w_out, gains_out):
    for k in range(SHARDS):
        s = (x + k) & 3
        w_out[pl.ds(pl.multiple_of(s * ROWS_HERE, ROWS_HERE), ROWS_HERE), :] = packs[k][
            0:ROWS_HERE, :
        ]
    rows = [p[ROWS_HERE : ROWS_HERE + 16, :].astype(F32)[0:8] for p in packs]
    for half in range(2):
        for b in range(SHARDS):
            total = jnp.zeros((8, ROWS_HERE), F32)
            for k in range(SHARDS):
                piece = rows[k][:, half * ROWS_HERE : (half + 1) * ROWS_HERE]
                total = jnp.where(((x + k) & 3) == b, piece, total)
            gains_out[half * 8 : half * 8 + 8, b * ROWS_HERE : (b + 1) * ROWS_HERE] = total


def route_body(micro, routes, cap, tokens, *refs):
    for m in range(1, micro):
        refs[m - 1][...] = tokens[m]
    outs = refs[micro - 1 :]
    named = iota((EXPERTS, TOK), 0)
    earlier = jnp.where(iota((TOK, TOK), 0) < iota((TOK, TOK), 1), 1.0, 0.0).astype(BF)
    one = iota((EXPERTS, EXPERTS), 0) == iota((EXPERTS, EXPERTS), 1)
    limit = jnp.sum(jnp.where(one, cap[...], 0).astype(F32), axis=1, keepdims=True)
    first = iota((EXPERTS, SLOTS), 0) * CAP
    slot = iota((EXPERTS, SLOTS), 1)
    spread = jnp.where(jnp.logical_and(slot >= first, slot < first + CAP), 1.0, 0.0).astype(BF)
    within = (iota((TOK, SLOTS), 1) % CAP).astype(F32)
    within_t = (iota((SLOTS, TOK), 0) % CAP).astype(F32)
    for m in range(micro):
        c01_ref, d01_ref = outs[2 * m : 2 * m + 2]
        hits = jnp.zeros((EXPERTS, TOK), F32)
        for k in range(TOPK):
            hit = routes[m, k : k + 1, :] == named
            hits = jnp.where(hit, 1.0, hits)
        ranks = dot(hits.astype(BF), earlier)
        kept = jnp.logical_and(hits > 0.0, ranks < limit)
        place_of = jnp.where(kept, ranks, -1.0).astype(BF)
        own = dot(place_of, spread, 0, 0) == within
        c01_ref[...] = jnp.where(own, 1.0, 0.0).astype(BF)
        own_t = dot(spread, place_of, 0, 0) == within_t
        d01_ref[...] = jnp.where(own_t, 1.0, 0.0).astype(BF)


NOTES = 16


def deal_body(micro, place, order, routes, gates, c0, c1, c2, c3, out_ref):
    for m in range(micro):
        deal = given_by_dealt(order, m, x_of(place))[:, 0:TOK]
        rows = jnp.concatenate([c[m] for c in (c0, c1, c2, c3)], axis=0)
        out_ref[m, 0:TOK, :] = dot(deal, rows, 0, 0).astype(BF)
        experts = jnp.concatenate([routes[m, k : k + 1, :] for k in range(TOPK)], axis=1)
        weights = jnp.concatenate([gates[m, k : k + 1, :] for k in range(TOPK)], axis=1)
        high = weights.astype(BF).astype(F32)
        row = iota((NOTES, D), 0)
        notes = jnp.where(row == 1, high, weights - high)
        notes = jnp.where(row == 0, experts.astype(F32), notes)
        out_ref[m, TOK : TOK + NOTES, :] = notes.astype(BF)


def attend_body(m, place, lengths, order, t0, t1, t2, t3, wo, *refs):
    x, first_length = x_of(place), lengths[m, 0, 0]
    if m == 0:
        packs, refs = refs[:4], refs[4:]
        o0, o1, o2, o3, dealt_ref, xr_ref, qkv_ref, mixed_ref, mass_ref, w, gains = refs
        unpack(x, packs, w, gains)
    else:
        w, gains, o0, o1, o2, o3, dealt_ref, xr_ref, qkv_ref, mixed_ref, mass_ref = refs
    deal = given_by_dealt(order, m, x)
    dealt = dot(deal, stack((t0, t1, t2, t3)), 0, 0)
    dealt_ref[...] = dealt[0:TOK].astype(BF)
    scaled = dealt * lax.rsqrt(jnp.mean(dealt * dealt, axis=-1, keepdims=True) + EPS)
    xr_ref[...] = scaled.astype(BF)
    attn_in = (scaled * gains[0:1, :]).astype(BF)
    qkv = dot(attn_in, w[...]).astype(BF)
    qkv_ref[...] = qkv
    same = same_documents(x, first_length)
    heads = []
    masses = []
    for h in range(HEADS_HERE):
        g = h // (HEADS // KV_HEADS)
        q = qkv[:, h * HEAD : (h + 1) * HEAD]
        k = qkv[:, QC + g * HEAD : QC + (g + 1) * HEAD]
        v = qkv[:, QC + KC + g * HEAD : QC + KC + (g + 1) * HEAD]
        scores = jnp.where(same, dot(q, k, 1, 1) * SCALE, MASKED)
        highest = jnp.max(scores, axis=-1, keepdims=True)
        raised = jnp.exp(scores - highest)
        total = jnp.sum(raised, axis=-1, keepdims=True)
        probs = (raised * (1.0 / total)).astype(BF)
        heads.append(dot(probs, v).astype(BF))
        masses.append(jnp.broadcast_to(highest + jnp.log(total), (GT, 32)))
    mixed = jnp.concatenate(heads, axis=1)
    mixed_ref[...] = mixed
    mass_ref[...] = jnp.concatenate(masses, axis=1)
    part = dot(mixed, wo[...]).astype(BF)
    for k, out in enumerate((o0, o1, o2, o3)):
        out[...] = part[k * TOK : (k + 1) * TOK]


def leave_body(own, r1, r2, r3, dealt, gains, d01, middle_ref, rows_ref):
    middle = dealt[...].astype(F32) + (
        (own[...].astype(F32) + r1[...].astype(F32)) + (r2[...].astype(F32) + r3[...].astype(F32))
    )
    middle_ref[...] = middle
    r = lax.rsqrt(jnp.mean(middle * middle, axis=-1, keepdims=True) + EPS)
    ffn_in = (middle * r * gains[8:9, :]).astype(BF)
    rows_ref[...] = dot(d01[...], ffn_in).astype(BF)


SOURCES = 8
TILE = SOURCES * CAP


def expert_body(m, last, waits, *refs):
    refs = list(refs[waits:])
    place, cap, rows, cotangent = refs[:4]
    blocks = refs[4:9]
    refs = refs[9:]
    prev = None
    if m > 0:
        prev, refs = refs[0], refs[1:]
    out_ref, back_ref = refs[:2]
    if last:
        send_ref, (wg, wu, wd, acc) = refs[2], refs[3:]
    else:
        sums_ref, (wg, wu, wd, acc) = refs[2], refs[3:]
    step = pl.program_id(0)

    @pl.when(step == 0)
    def _():
        mine, right, left, first, second = blocks
        for k, ref in enumerate((mine, right, (first, second), left)):
            at = slice(k * 128, (k + 1) * 128)
            for half in range(2):
                piece = ref[half] if k != 2 else ref[half][0]
                rows_at = slice(half * (D // 2), (half + 1) * (D // 2))
                wg[rows_at, at] = piece[0]
                wu[rows_at, at] = piece[1]
                wd[rows_at, at] = piece[2]
        acc[...] = jnp.zeros(acc.shape, F32) if prev is None else prev[...]

    expert = place[0] >> 2
    notes = cotangent[:, 0, TOK : TOK + NOTES, :].astype(F32)
    named, high, low = (notes[:, j, :] for j in range(3))
    hits = jnp.zeros((SOURCES, TOK), F32)
    weight = jnp.zeros((SOURCES, TOK), F32)
    for k in range(TOPK):
        at = slice(k * TOK, (k + 1) * TOK)
        hit = named[:, at] == expert.astype(F32)
        hits = jnp.where(hit, 1.0, hits)
        weight = jnp.where(hit, high[:, at] + low[:, at], weight)
    earlier = jnp.where(iota((TOK, TOK), 0) < iota((TOK, TOK), 1), 1.0, 0.0).astype(BF)
    ranks = dot(hits.astype(BF), earlier)
    kept = jnp.logical_and(hits > 0.0, ranks < cap[0, expert].astype(F32))
    place_of = jnp.where(kept, ranks, -1.0)
    rank = iota((CAP, TOK), 0).astype(F32)
    picks, gates_of, grads = [], [], []
    for j in range(SOURCES):
        own = place_of[j : j + 1, :] == rank
        gate = jnp.sum(jnp.where(own, weight[j : j + 1, :], 0.0), axis=1, keepdims=True)
        pick = jnp.where(own, 1.0, 0.0).astype(BF)
        picks.append(pick)
        gates_of.append(gate)
        grads.append((dot(pick, cotangent[j, 0, 0:TOK, :]) * gate).astype(BF))
    grad = jnp.concatenate(grads, axis=0)
    row = rows[...]
    gate_of = jnp.concatenate(gates_of, axis=0)
    gate = dot(row, wg[...])
    up = dot(row, wu[...])
    sig = jax.nn.sigmoid(gate)
    silu = gate * sig
    hidden = (silu * up).astype(BF)
    weighted = (dot(hidden, wd[...], 1, 1) * gate_of).astype(BF)
    if last:
        out_ref[...] = weighted
    else:
        for j in range(SOURCES):
            out_ref[j] = dot(picks[j], weighted[j * CAP : (j + 1) * CAP], 0, 0).astype(BF)
    grad_hidden = dot(grad, wd[...])
    grad_gate = (grad_hidden * up * sig * (1.0 + gate * (1.0 - sig))).astype(BF)
    grad_up = (grad_hidden * silu).astype(BF)
    back_ref[...] = (dot(grad_gate, wg[...], 1, 1) + dot(grad_up, wu[...], 1, 1)).astype(BF)
    acc[0] += dot(row, grad_gate, 0, 0)
    acc[1] += dot(row, grad_up, 0, 0)
    acc[2] += dot(grad, hidden, 0, 0)

    @pl.when(step == pl.num_programs(0) - 1)
    def _():
        if last:
            for k in range(SHARDS):
                for j in range(3):
                    piece = acc[j, :, k * 128 : (k + 1) * 128].astype(BF)
                    send_ref[pl.ds((x_of(place) + k) & 3, 1), j] = piece[None]
        else:
            sums_ref[...] = acc[...]


def expert_call(m, micro, place, cap, rows, cotangent, blocks, prev, after=()):
    last = m == micro - 1
    tiles = SLOTS // TILE
    tile = pl.BlockSpec((TILE, D), lambda i: (i, 0))

    def fixed(dims):
        return pl.BlockSpec(dims, lambda i: (0,) * len(dims), pipeline_mode=pl.Buffered(1))

    ins = [place, cap, rows, cotangent, *blocks]
    in_specs = [
        SMEM,
        SMEM,
        tile,
        pl.BlockSpec((SOURCES, 1, TOK + NOTES, D), lambda i: (i, m, 0, 0)),
    ] + [fixed(b.shape) for b in blocks]
    ins = [*after, *ins]
    in_specs = [ANY] * len(after) + in_specs
    outs = [shape((SLOTS, D) if last else (EXPERTS, TOK, D), BF), shape((SLOTS, D), BF)]
    dense = pl.BlockSpec((SOURCES, TOK, D), lambda i: (i, 0, 0))
    out_specs = [tile if last else dense, tile]
    if m > 0:
        ins.append(prev)
        in_specs.append(fixed((3, D, F)))
    if last:
        outs.append(shape((SHARDS, 3, D, 128), BF))
        out_specs.append(fixed((SHARDS, 3, D, 128)))
    else:
        outs.append(shape((3, D, F), F32))
        out_specs.append(fixed((3, D, F)))
    return pl.pallas_call(
        functools.partial(expert_body, m, last, len(after)),
        grid=(tiles,),
        in_specs=in_specs,
        out_specs=out_specs,
        out_shape=outs,
        scratch_shapes=[pltpu.VMEM((D, F), BF)] * 3 + [pltpu.VMEM((3, D, F), F32)],
        compiler_params=pltpu.CompilerParams(
            vmem_limit_bytes=63 * 1024 * 1024, dimension_semantics=("arbitrary",)
        ),
        cost_estimate=cost(MICROSECONDS["expert"]),
        name="expert",
    )(*ins)


def returned_body(m, back, c01, middle, gains, dy, branch_ref, gain_ref):
    upstream = dot(c01[...], back[...])
    mid = middle[...]
    r = lax.rsqrt(jnp.mean(mid * mid, axis=-1, keepdims=True) + EPS)
    scaled = upstream * gains[8:9, :]
    grad = r * scaled - mid * (r * r * r) * jnp.mean(scaled * mid, axis=-1, keepdims=True)
    branch_ref[...] = (dy[m, 0:TOK, :].astype(F32) + grad).astype(BF)
    gain_ref[...] = jnp.broadcast_to(jnp.sum(upstream * mid * r, axis=0, keepdims=True), (8, D))


def block_body(micro, mixture, slots, c01, *refs):
    for m in range(micro - 1):
        refs[-1][m] = (refs[m][...] + mixture[...].astype(F32)).astype(BF)
    refs[-1][micro - 1] = (refs[micro - 1][...] + dot(c01[...], slots[...])).astype(BF)


def place_body(micro, place, order, rows, out_ref):
    given = iota((TOK, GT), 0) + TOK * x_of(place)
    for m in range(micro):
        deal = jnp.where(given == order[m], 1.0, 0.0).astype(BF)
        dealt = jnp.concatenate([rows[s, m] for s in range(SHARDS)], axis=0)
        out_ref[m] = dot(deal, dealt).astype(BF)


def attend_back_body(m, last, place, lengths, order, g0, g1, g2, g3, xr, qkv_ref, mixed, mass, w, wo, *refs):
    x, first_length = x_of(place), lengths[m, 0, 0]
    if last:
        prev_w, prev_o, gain0, gain1, *refs = refs
    o0, o1, o2, o3, given_ref, *refs = refs
    deal = given_by_dealt(order, m, x)
    branch = stack((g0, g1, g2, g3))
    given_ref[...] = dot(deal[0:TOK], branch).astype(BF)
    sum_o = dot(mixed[...], branch, 0, 0)
    grad_mixed = dot(branch, wo[...], 1, 1).astype(BF)
    qkv = qkv_ref[...]
    same = same_documents(x, first_length)
    grad_q, grad_k, grad_v = [], [], []
    for g in range(KV_HERE):
        k = qkv[:, QC + g * HEAD : QC + (g + 1) * HEAD]
        v = qkv[:, QC + KC + g * HEAD : QC + KC + (g + 1) * HEAD]
        sum_k = jnp.zeros((HEAD, GT), F32)
        sum_v = jnp.zeros((HEAD, GT), F32)
        for r in range(HEADS // KV_HEADS):
            h = g * (HEADS // KV_HEADS) + r
            q = qkv[:, h * HEAD : (h + 1) * HEAD]
            gm = grad_mixed[:, h * HEAD : (h + 1) * HEAD]
            scores = jnp.where(same, dot(q, k, 1, 1) * SCALE, MASKED)
            probs = jnp.exp(scores - mass[:, h * 32 : h * 32 + 1])
            grad_probs = dot(gm, v, 1, 1)
            sum_v += dot(gm, probs.astype(BF), 0, 0)
            weighted = probs * grad_probs
            grad_scores = weighted - probs * jnp.sum(weighted, axis=-1, keepdims=True)
            grad_scores = grad_scores.astype(BF)
            grad_q.append((dot(grad_scores, k) * SCALE).astype(BF))
            sum_k += dot(q, grad_scores, 0, 0)
        grad_k.append((sum_k * SCALE).astype(BF))
        grad_v.append(sum_v.astype(BF))
    grad_kv = jnp.concatenate(grad_k + grad_v, axis=0).astype(F32).T.astype(BF)
    grad_qkv = jnp.concatenate(grad_q + [grad_kv], axis=1)
    sum_w = dot(xr[...], grad_qkv, 0, 0)
    part = dot(grad_qkv, w[...], 1, 1).astype(BF)
    part = dot(deal, part).astype(BF)
    for k, out in enumerate((o0, o1, o2, o3)):
        out[...] = part[k * TOK : (k + 1) * TOK]
    if not last:
        sum_w_ref, sum_o_ref = refs
        sum_w_ref[...] = sum_w
        sum_o_ref[...] = sum_o
        return
    keep_ref, send_ref, all_w, all_o = refs
    c = core_of(place)
    all_w[...] = sum_w + prev_w[...]
    all_o[...] = sum_o + prev_o[...]
    gain = gain0[...] + gain1[...]
    for ref, half in ((keep_ref, c), (send_ref, 1 - c)):
        at = pl.ds(pl.multiple_of(half * 256, 256), 256)
        ref[0:D, :] = all_w[:, at].astype(ref.dtype)
        for j in range(2):
            at = pl.ds(pl.multiple_of(j * 512 + half * 256, 256), 256)
            ref[D + j * 256 : D + (j + 1) * 256, :] = all_o[:, at].astype(ref.dtype)
        tile = jnp.concatenate(
            [gain[0:1, b * 256 : (b + 1) * 256] for b in range(4)] + [jnp.zeros((12, 256), F32)], axis=0
        )
        for j in range(16):
            ref[6 * 256 + j * 16 : 6 * 256 + (j + 1) * 16, :] = tile.astype(ref.dtype)


def tokens_body(micro, tokens, gains, *refs):
    for m in range(micro):
        p0, p1, p2, p3, given = refs[5 * m : 5 * m + 5]
        upstream = (p0[...].astype(F32) + p1[...].astype(F32)) + (
            p2[...].astype(F32) + p3[...].astype(F32)
        )
        v = tokens[m].astype(F32)
        r = lax.rsqrt(jnp.mean(v * v, axis=-1, keepdims=True) + EPS)
        scaled = upstream * gains[0:1, :]
        grad = r * scaled - v * (r * r * r) * jnp.mean(scaled * v, axis=-1, keepdims=True)
        refs[-1][m] = (given[...].astype(F32) + grad).astype(BF)


def weight_sums_body(sums, *outs):
    for j in range(3):
        outs[j][0] = sums[j].astype(F32)


def weight_stack_body(a, b, c, out_ref):
    for j, ref in enumerate((a, b, c)):
        for half in range(2):
            out_ref[half, j] = ref[0, half * (D // 2) : (half + 1) * (D // 2)]


BLOCKS = 7


def split_y_body(place, keep, got, own_ref, s1, s2, s3):
    y = y_of(place)
    for b in range(BLOCKS):
        for k, ref in enumerate((own_ref, s1, s2, s3)):
            at = pl.ds(pl.multiple_of(b * 256 + ((y + k) & 3) * 64, 64), 64)
            ref[b * 64 : (b + 1) * 64, :] = (keep[at, :] + got[at, :].astype(F32)).astype(ref.dtype)


def sum_y_body(own, r1, r2, r3, out_ref):
    total = (own[...] + r1[...].astype(F32)) + (r2[...].astype(F32) + r3[...].astype(F32))
    out_ref[...] = total.astype(BF)


def split_x_body(place, own, r1, r2, r3, o_ref, own_ref, s1, s2, s3, held):
    x, z = x_of(place), z_of(place)
    for k, ref in enumerate((own, r1, r2, r3)):
        held[pl.ds((z - k) & 3, 1)] = ref[...][None]

    def total(at):
        return (held[0, at, :].astype(F32) + held[1, at, :].astype(F32)) + (
            held[2, at, :].astype(F32) + held[3, at, :].astype(F32)
        )

    gain = total(slice(384, 400))
    row = iota((16, 256), 0)
    for k, ref in enumerate((own_ref, s1, s2, s3)):
        s = (x + k) & 3
        ref[0:64, :] = total(pl.ds(pl.multiple_of(s * 64, 64), 64)).astype(BF)
        mine = jnp.sum(jnp.where(row == s, gain, 0.0), axis=0, keepdims=True)
        ref[64:80, :] = jnp.broadcast_to(mine, (16, 256)).astype(BF)
    o_ref[...] = total(slice(256, 384)).astype(BF)


def join_x_body(place, o, own, r1, r2, r3, out_ref, gain_ref):
    x = x_of(place)
    gain = jnp.zeros((16, 256), F32)
    for k, ref in enumerate((own, r1, r2, r3)):
        s = (x - k) & 3
        out_ref[pl.ds(pl.multiple_of(s * 64, 64), 64), :] = ref[0:64, :]
        gain += ref[64:80, :].astype(F32)
    out_ref[256:384, :] = o[...]
    gain_ref[...] = gain[0:1]


def join_y_body(place, own, r1, r2, r3, out_ref):
    rows = own.shape[0]
    for k, ref in enumerate((own, r1, r2, r3)):
        s = (y_of(place) + k) & 3
        out_ref[pl.ds(pl.multiple_of(s * rows, rows), rows), :] = ref[...]


def weights_body(place, own, got, wq, wk, wv, gain, q_ref, k_ref, v_ref, o_ref, gain_ref):
    c = core_of(place)
    scale = gain[...]
    total = jnp.zeros((ROWS_HERE, 1), F32)

    def piece(ref, b):
        return jnp.concatenate(
            [ref[j * 384 + b * 64 : j * 384 + (b + 1) * 64, :] for j in range(4)], axis=0
        ).astype(F32)

    for b in range(6):
        mine, other = piece(own, b), piece(got, b)
        left = jnp.where(c == 0, mine, other)
        right = jnp.where(c == 0, other, mine)
        if b < 4:
            q_ref[:, b * QC : (b + 1) * QC] = left * scale
            k_ref[:, b * KC : (b + 1) * KC] = right[:, 0:KC] * scale
            v_ref[:, b * KC : (b + 1) * KC] = right[:, KC : 2 * KC] * scale
            total += jnp.sum(
                left * wq[:, b * QC : (b + 1) * QC].astype(F32), axis=1, keepdims=True
            )
            total += jnp.sum(
                right[:, 0:KC] * wk[:, b * KC : (b + 1) * KC].astype(F32), axis=1, keepdims=True
            )
            total += jnp.sum(
                right[:, KC : 2 * KC] * wv[:, b * KC : (b + 1) * KC].astype(F32),
                axis=1,
                keepdims=True,
            )
        else:
            o_ref[:, (b - 4) * 512 : (b - 4) * 512 + 256] = left
            o_ref[:, (b - 4) * 512 + 256 : (b - 3) * 512] = right
    gain_ref[...] = jnp.broadcast_to(total, (ROWS_HERE, 128)).T[0:1]


def finish_body(micro, place, order, block_rows, own, got, wq, wk, wv, gain, block_ref, *outs):
    weights_body(place, own, got, wq, wk, wv, gain, *outs)
    place_body(micro, place, order, block_rows, block_ref)


def from_right(v, k):
    return lax.ppermute(v, "shard", [(i, (i - k) % SHARDS) for i in range(SHARDS)])


def to_right(v, k):
    return lax.ppermute(v, "shard", [(i, (i + k) % SHARDS) for i in range(SHARDS)])


def gather_x(v):
    return [v] + [from_right(v, k) for k in (1, 2, 3)]


def gather_ring(v):
    half = v.shape[0] // 2
    right, left = from_right(v, 1), from_right(v, 3)
    return [v, right, left, from_right(right[:half], 1), from_right(left[half:], 3)]


def hold(arrays, *others):
    count = len(arrays)
    return pl.pallas_call(
        lambda *refs: None,
        out_shape=[shape(v.shape, v.dtype) for v in arrays],
        in_specs=[ANY] * (count + len(others)),
        out_specs=[ANY] * count,
        input_output_aliases={i: i for i in range(count)},
        cost_estimate=cost(0),
        name="hold",
    )(*arrays, *others)


def scatter_x(blocks):
    return [blocks[0]] + [to_right(blocks[k], k) for k in (1, 2, 3)]


def along(v, step):
    pairs = []
    for i in range(EXPERTS):
        z, y, c = step(i // 8, (i // 2) % 4, i % 2)
        pairs.append((i, (z % 4) * 8 + (y % 4) * 2 + c % 2))
    return lax.ppermute(v, "expert", pairs)


def swap_core(v):
    return along(v, lambda z, y, c: (z, y, 1 - c))


def sum_over_experts(v):
    return lax.psum_scatter(v, "expert", scatter_dimension=0, tiled=True)


def exchange(v):
    return lax.all_to_all(v, "expert", split_axis=0, concat_axis=0, tiled=True)


def per_device(
    tokens,
    cotangent,
    order,
    lengths,
    routes,
    gate_weights,
    capacity,
    gain_attn,
    w_query,
    w_key,
    w_value,
    w_out,
    gain_ffn,
    w_gate,
    w_up,
    w_down,
):
    micro = tokens.shape[0]
    place = lax.axis_index(("expert", "shard")).astype(I32).reshape(1)
    cap = capacity.reshape(1, EXPERTS)
    experts = jnp.swapaxes(routes, 1, 2)
    gates = jnp.swapaxes(gate_weights, 1, 2)

    cot_rows = gather_x(cotangent)
    *packs, tokens_first = run(
        "pack",
        pack_body,
        [shape((ROWS_HERE + 16, COLS), BF)] * 4 + [shape((TOK, D), BF)],
        [
            place,
            w_query,
            w_key,
            w_value,
            jnp.concatenate([gain_attn, gain_ffn]).reshape(1, -1),
            tokens,
        ],
        smem=(0,),
    )
    pack_done = tokens_first
    waited = hold([*packs, tokens_first], *cot_rows[1:])
    packs, tokens_first = waited[:SHARDS], waited[SHARDS]
    token_rows = gather_x(tokens_first)
    packs = [packs[0]] + [from_right(packs[k], k) for k in (1, 2, 3)]
    routed = run(
        "route",
        functools.partial(route_body, micro),
        [shape((TOK, D), BF)] * (micro - 1)
        + [shape((TOK, SLOTS), BF), shape((SLOTS, TOK), BF)] * micro,
        [experts, cap, tokens],
        after=[pack_done],
    )
    token_copies, routed = routed[: micro - 1], routed[micro - 1 :]
    routed = [routed[2 * m : 2 * m + 2] for m in range(micro)]

    weights = run(
        "weight_stack",
        weight_stack_body,
        [shape((2, 3, D // 2, 128), BF)],
        [w_gate, w_up, w_down],
        after=routed[0][:1],
    )[0]
    attended, left, reached = [], [], []
    w_qkv = gains = weight_blocks = None

    dealt_cot = run(
        "deal",
        functools.partial(deal_body, micro),
        [shape((micro, TOK + NOTES, D), BF)],
        [place, order, experts, gates, *cot_rows],
        smem=(0,),
        after=[pack_done, routed[0][0]],
    )[0]
    cot_all = lax.all_gather(dealt_cot, "expert", axis=0)
    for m in range(micro):
        first = m == 0
        if not first:
            token_rows = later_rows
            weight_blocks = gather_ring(hold([weights], *token_rows[1:])[0])
        outs = [shape((TOK, D), BF)] * 5 + [
            shape((GT, D), BF),
            shape((GT, COLS), BF),
            shape((GT, QC), BF),
            shape((GT, 128), F32),
        ]
        if first:
            outs += [shape((D, COLS), BF), shape((16, D), F32)]
        result = run(
            "attend",
            functools.partial(attend_body, m),
            outs,
            [place, lengths, order, *token_rows, w_out, *(packs if first else (w_qkv, gains))],
            smem=(0, 1),
            after=[dealt_cot] if first else [],
        )
        if first:
            w_qkv, gains = result[9:]
        attended.append(result[:9])
        parts = scatter_x(result[:4])
        if first:
            later_rows = gather_x(hold([token_copies[m]], parts[1])[0])
        left.append(
            run(
                "leave",
                leave_body,
                [shape((TOK, D), F32), shape((SLOTS, D), BF)],
                [*parts, result[4], gains, routed[m][1]],
                after=[weights, *later_rows[1:]] if first else weight_blocks[1:3],
            )
        )
        reached.append(exchange(left[m][1]))

    backs, mixtures, sums = [], [], None
    for m in range(micro):
        result = expert_call(
            m,
            micro,
            place,
            cap,
            reached[m],
            cot_all,
            weight_blocks,
            sums,
            after=[left[-1][1]] if m == 0 else [],
        )
        if m < micro - 1:
            dense, back = hold(result[:2], reached[-1])
            mixtures.append(sum_over_experts(dense.reshape(-1, D)))
        else:
            last_out, back = result[0], hold([result[1]], backs[m - 1])[0]
        backs.append(exchange(back))
        sums = result[2]

    sum_w = sum_o = None
    gain_sums, grad_parts = [], []
    for m in range(micro):
        last = m == micro - 1
        branch, gain_sum = run(
            "returned",
            functools.partial(returned_body, m),
            [shape((TOK, D), BF), shape((8, D), F32)],
            [backs[m], routed[m][0], left[m][0], gains, dealt_cot],
            after=() if m == 0 else (sum_w, *grad_parts[1:4]),
        )
        branch_rows = gather_x(branch)
        if last:
            mixtures.append(exchange(hold([last_out], branch)[0]))
        else:
            sums = lax.psum_scatter(
                sums.reshape(-1, 128), "shard", scatter_dimension=0, tiled=True
            )
            totals = run(
                "weight_sums",
                weight_sums_body,
                [shape((1, D, 128), F32)] * 3,
                [sums.reshape(3, D, 128)],
            )
        gain_sums.append(gain_sum)
        ins = [place, lengths, order, *branch_rows, *attended[m][5:9], w_qkv, w_out]
        out_shapes = [shape((TOK, D), BF)] * 5
        scratch = []
        if last:
            ins += [sum_w, sum_o, *gain_sums]
            out_shapes += [shape((BLOCKS * 256, 256), F32), shape((BLOCKS * 256, 256), BF)]
            scratch = [pltpu.VMEM((D, COLS), F32), pltpu.VMEM((ROWS_HERE, D), F32)]
        else:
            out_shapes += [shape((D, COLS), F32), shape((ROWS_HERE, D), F32)]
        result = run(
            "attend_back",
            functools.partial(attend_back_body, m, last),
            out_shapes,
            ins,
            smem=(0, 1),
            scratch=scratch,
        )
        sum_w, sum_o = result[5:7]
        if last:
            last_parts = result[:5]
        else:
            grad_parts += [*scatter_x(result[:4]), result[4]]

    four = [0, 1, 2, 3]
    rows = BLOCKS * 64
    split_y = run(
        "split_y",
        split_y_body,
        [shape((rows, 256), F32)] + [shape((rows, 256), BF)] * 3,
        [place, sum_w, swap_core(sum_o)],
        smem=(0,),
    )
    pieces = [split_y[0]] + [along(split_y[k], lambda z, y, c, k=k: (z, y + k, c)) for k in four[1:]]
    last_parts = [*scatter_x(last_parts[:4]), last_parts[4]]
    sum_y = run(
        "sum_y", sum_y_body, [shape((rows, 256), BF)], pieces, after=last_parts[1:4]
    )[0]
    pieces = [sum_y] + [along(sum_y, lambda z, y, c, k=k: (z + k, y, c)) for k in four[1:]]
    blocks = run(
        "block",
        functools.partial(block_body, micro),
        [shape((micro, TOK, D), BF)],
        [*mixtures, routed[-1][0], *[left[m][0] for m in range(micro)]],
        after=[sum_y],
    )[0]
    block_rows = lax.all_gather(blocks, "shard", axis=0)
    o_piece, *pieces = run(
        "split_x",
        split_x_body,
        [shape((128, 256), BF)] + [shape((80, 256), BF)] * 4,
        [place, *pieces],
        smem=(0,),
        scratch=[pltpu.VMEM((4, rows, 256), BF)],
        after=[blocks],
    )
    x_pieces = scatter_x(pieces)
    piece, gain_ffn_sum = run(
        "join_x",
        join_x_body,
        [shape((384, 256), BF), shape((1, 256), F32)],
        [place, o_piece, *x_pieces],
        smem=(0,),
        after=totals[:1],
    )
    grad_tokens = run(
        "tokens",
        functools.partial(tokens_body, micro),
        [shape(tokens.shape, BF)],
        [tokens, gains, *grad_parts, *last_parts],
    )[0]
    pieces = [piece] + [along(piece, lambda z, y, c, k=k: (z, y - k, c)) for k in four[1:]]
    piece = run(
        "join_y",
        join_y_body,
        [shape((1536, 256), BF)],
        [place, *pieces],
        smem=(0,),
        after=[grad_tokens],
    )[0]
    block_out, grad_query, grad_key, grad_value, grad_out, grad_gain = run(
        "finish",
        functools.partial(finish_body, micro),
        [
            shape(tokens.shape, BF),
            shape(w_query.shape, F32),
            shape(w_key.shape, F32),
            shape(w_value.shape, F32),
            shape(w_out.shape, F32),
            shape((1, ROWS_HERE), F32),
        ],
        [
            place,
            order,
            block_rows,
            piece,
            swap_core(piece),
            w_query,
            w_key,
            w_value,
            gain_attn.astype(F32).reshape(-1, 1),
        ],
        smem=(0,),
    )

    return (
        block_out,
        grad_tokens,
        grad_gain.reshape(-1),
        grad_query,
        grad_key,
        grad_value,
        grad_out,
        gain_ffn_sum.reshape(-1),
        *totals,
    )


def solution(mesh):
    return jax.shard_map(
        per_device,
        mesh=mesh,
        in_specs=(
            P(None, ("expert", "shard"), None),
            P(None, ("expert", "shard"), None),
            P(None, "expert", None),
            P(None, "expert", None),
            P(None, ("expert", "shard"), None),
            P(None, ("expert", "shard"), None),
            P(),
            P("shard"),
            P("shard", None),
            P("shard", None),
            P("shard", None),
            P("shard", None),
            P("shard"),
            P("expert", None, "shard"),
            P("expert", None, "shard"),
            P("expert", None, "shard"),
        ),
        out_specs=(
            P(None, ("expert", "shard"), None),
            P(None, ("expert", "shard"), None),
            P("shard"),
            P("shard", None),
            P("shard", None),
            P("shard", None),
            P("shard", None),
            P("shard"),
            P("expert", None, "shard"),
            P("expert", None, "shard"),
            P("expert", None, "shard"),
        ),
        check_vma=False,
    )
```

```python
import functools

import jax
import jax.numpy as jnp
from jax import lax
from jax.experimental import pallas as pl
from jax.experimental.pallas import tpu as pltpu
from jax.sharding import PartitionSpec as P

D = 1024
HEADS = 16
KV_HEADS = 8
HEAD = 64
F = 512
EXPERTS = 32
TOPK = 8
CAP = 48
TOK = 128
GT = 512
SHARDS = 4
SLOTS = EXPERTS * CAP
HEADS_HERE = HEADS // SHARDS
KV_HERE = KV_HEADS // SHARDS
QC = HEADS_HERE * HEAD
KC = KV_HERE * HEAD
COLS = QC + 2 * KC
ROWS_HERE = D // SHARDS

EPS = 1e-05
MASKED = -1e30
SCALE = HEAD ** (-0.5)

BF = jnp.bfloat16
F32 = jnp.float32
I32 = jnp.int32

VMEM = pl.BlockSpec(memory_space=pltpu.VMEM)
SMEM = pl.BlockSpec(memory_space=pltpu.SMEM)
ANY = pl.BlockSpec(memory_space=pl.ANY)


def dot(a, b, ca=1, cb=0):
    return lax.dot_general(a, b, (((ca,), (cb,)), ((), ())), preferred_element_type=F32)


def shape(dims, dtype):
    return jax.ShapeDtypeStruct(dims, dtype)


MICROSECONDS = {
    "pack": 2.5,
    "route": 4.5,
    "deal": 3.5,
    "weight_stack": 2.0,
    "attend": 7.3,
    "leave": 4.3,
    "expert": 27.0,
    "returned": 3.7,
    "attend_back": 11.0,
    "weight_sums": 2.0,
    "split_y": 2.8,
    "sum_y": 2.0,
    "split_x": 2.4,
    "join_x": 1.5,
    "join_y": 2.2,
    "block": 4.5,
    "tokens": 3.4,
    "finish": 5.5,
}


def cost(microseconds):
    return pl.CostEstimate(
        flops=1, bytes_accessed=int(3.6e6 * microseconds) + 1, transcendentals=0
    )


def run(name, body, outs, ins, smem=(), scratch=(), limit=63, after=()):
    count = len(ins)

    def whole(*refs):
        body(*refs[:count], *refs[count + len(after) :])

    ins = [*ins, *after]
    return pl.pallas_call(
        whole,
        out_shape=outs,
        in_specs=[SMEM if i in smem else VMEM for i in range(count)] + [ANY] * len(after),
        out_specs=[VMEM] * len(outs),
        scratch_shapes=list(scratch),
        compiler_params=pltpu.CompilerParams(vmem_limit_bytes=limit * 1024 * 1024),
        cost_estimate=cost(MICROSECONDS[name]),
        name=name,
    )(*ins)


def iota(dims, axis):
    return lax.broadcasted_iota(I32, dims, axis)


def x_of(place):
    return place[0] & 3


def core_of(place):
    return (place[0] >> 2) & 1


def y_of(place):
    return (place[0] >> 3) & 3


def z_of(place):
    return place[0] >> 5


def rolled_order(order_ref, m, x):
    rows = [
        order_ref[m, :, pl.ds(pl.multiple_of(((x + k) & 3) * TOK, TOK), TOK)] for k in range(SHARDS)
    ]
    return (jnp.concatenate(rows, axis=1) - TOK * x) & (GT - 1)


def given_by_dealt(order_ref, m, x, rows=GT):
    return jnp.where(iota((rows, GT), 0) == rolled_order(order_ref, m, x), 1.0, 0.0).astype(BF)


def stack(refs):
    return jnp.concatenate([r[...] for r in refs], axis=0)


def same_documents(x, first_length):
    across = ((iota((GT, GT), 1) + TOK * x) & (GT - 1)) >= first_length
    down = ((iota((GT, GT), 0) + TOK * x) & (GT - 1)) >= first_length
    return jnp.logical_not(jnp.logical_xor(across, down))


def pack_body(place, wq, wk, wv, gains, tokens, *outs):
    x = x_of(place)
    outs[4][...] = tokens[0]
    for k in range(SHARDS):
        s = (x - k) & 3
        outs[k][0:ROWS_HERE, 0:QC] = wq[:, pl.ds(pl.multiple_of(s * QC, QC), QC)]
        outs[k][0:ROWS_HERE, QC : QC + KC] = wk[:, pl.ds(pl.multiple_of(s * KC, KC), KC)]
        outs[k][0:ROWS_HERE, QC + KC : COLS] = wv[:, pl.ds(pl.multiple_of(s * KC, KC), KC)]
        outs[k][ROWS_HERE : ROWS_HERE + 16, :] = jnp.broadcast_to(gains[...], (16, 2 * ROWS_HERE))


def unpack(x, packs, w_out, gains_out):
    for k in range(SHARDS):
        s = (x + k) & 3
        w_out[pl.ds(pl.multiple_of(s * ROWS_HERE, ROWS_HERE), ROWS_HERE), :] = packs[k][
            0:ROWS_HERE, :
        ]
    rows = [p[ROWS_HERE : ROWS_HERE + 16, :].astype(F32)[0:8] for p in packs]
    for half in range(2):
        for b in range(SHARDS):
            total = jnp.zeros((8, ROWS_HERE), F32)
            for k in range(SHARDS):
                piece = rows[k][:, half * ROWS_HERE : (half + 1) * ROWS_HERE]
                total = jnp.where(((x + k) & 3) == b, piece, total)
            gains_out[half * 8 : half * 8 + 8, b * ROWS_HERE : (b + 1) * ROWS_HERE] = total


def route_body(micro, routes, cap, tokens, *refs):
    for m in range(1, micro):
        refs[m - 1][...] = tokens[m]
    outs = refs[micro - 1 :]
    named = iota((EXPERTS, TOK), 0)
    earlier = jnp.where(iota((TOK, TOK), 0) < iota((TOK, TOK), 1), 1.0, 0.0).astype(BF)
    one = iota((EXPERTS, EXPERTS), 0) == iota((EXPERTS, EXPERTS), 1)
    limit = jnp.sum(jnp.where(one, cap[...], 0).astype(F32), axis=1, keepdims=True)
    first = iota((EXPERTS, SLOTS), 0) * CAP
    slot = iota((EXPERTS, SLOTS), 1)
    spread = jnp.where(jnp.logical_and(slot >= first, slot < first + CAP), 1.0, 0.0).astype(BF)
    within = (iota((TOK, SLOTS), 1) % CAP).astype(F32)
    within_t = (iota((SLOTS, TOK), 0) % CAP).astype(F32)
    for m in range(micro):
        c01_ref, d01_ref = outs[2 * m : 2 * m + 2]
        hits = jnp.zeros((EXPERTS, TOK), F32)
        for k in range(TOPK):
            hit = routes[m, k : k + 1, :] == named
            hits = jnp.where(hit, 1.0, hits)
        ranks = dot(hits.astype(BF), earlier)
        kept = jnp.logical_and(hits > 0.0, ranks < limit)
        place_of = jnp.where(kept, ranks, -1.0).astype(BF)
        own = dot(place_of, spread, 0, 0) == within
        c01_ref[...] = jnp.where(own, 1.0, 0.0).astype(BF)
        own_t = dot(spread, place_of, 0, 0) == within_t
        d01_ref[...] = jnp.where(own_t, 1.0, 0.0).astype(BF)


NOTES = 16


def deal_body(micro, place, order, routes, gates, c0, c1, c2, c3, out_ref):
    for m in range(micro):
        deal = given_by_dealt(order, m, x_of(place))[:, 0:TOK]
        rows = jnp.concatenate([c[m] for c in (c0, c1, c2, c3)], axis=0)
        out_ref[m, 0:TOK, :] = dot(deal, rows, 0, 0).astype(BF)
        experts = jnp.concatenate([routes[m, k : k + 1, :] for k in range(TOPK)], axis=1)
        weights = jnp.concatenate([gates[m, k : k + 1, :] for k in range(TOPK)], axis=1)
        high = weights.astype(BF).astype(F32)
        row = iota((NOTES, D), 0)
        notes = jnp.where(row == 1, high, weights - high)
        notes = jnp.where(row == 0, experts.astype(F32), notes)
        out_ref[m, TOK : TOK + NOTES, :] = notes.astype(BF)


def attend_body(m, place, lengths, order, t0, t1, t2, t3, wo, *refs):
    x, first_length = x_of(place), lengths[m, 0, 0]
    if m == 0:
        packs, refs = refs[:4], refs[4:]
        o0, o1, o2, o3, dealt_ref, xr_ref, qkv_ref, mixed_ref, mass_ref, w, gains = refs
        unpack(x, packs, w, gains)
    else:
        w, gains, o0, o1, o2, o3, dealt_ref, xr_ref, qkv_ref, mixed_ref, mass_ref = refs
    deal = given_by_dealt(order, m, x)
    dealt = dot(deal, stack((t0, t1, t2, t3)), 0, 0)
    dealt_ref[...] = dealt[0:TOK].astype(BF)
    scaled = dealt * lax.rsqrt(jnp.mean(dealt * dealt, axis=-1, keepdims=True) + EPS)
    xr_ref[...] = scaled.astype(BF)
    attn_in = (scaled * gains[0:1, :]).astype(BF)
    qkv = dot(attn_in, w[...]).astype(BF)
    qkv_ref[...] = qkv
    same = same_documents(x, first_length)
    heads = []
    masses = []
    for h in range(HEADS_HERE):
        g = h // (HEADS // KV_HEADS)
        q = qkv[:, h * HEAD : (h + 1) * HEAD]
        k = qkv[:, QC + g * HEAD : QC + (g + 1) * HEAD]
        v = qkv[:, QC + KC + g * HEAD : QC + KC + (g + 1) * HEAD]
        scores = jnp.where(same, dot(q, k, 1, 1) * SCALE, MASKED)
        highest = jnp.max(scores, axis=-1, keepdims=True)
        raised = jnp.exp(scores - highest)
        total = jnp.sum(raised, axis=-1, keepdims=True)
        probs = (raised * (1.0 / total)).astype(BF)
        heads.append(dot(probs, v).astype(BF))
        masses.append(jnp.broadcast_to(highest + jnp.log(total), (GT, 32)))
    mixed = jnp.concatenate(heads, axis=1)
    mixed_ref[...] = mixed
    mass_ref[...] = jnp.concatenate(masses, axis=1)
    part = dot(mixed, wo[...]).astype(BF)
    for k, out in enumerate((o0, o1, o2, o3)):
        out[...] = part[k * TOK : (k + 1) * TOK]


def leave_body(own, r1, r2, r3, dealt, gains, d01, middle_ref, rows_ref):
    middle = dealt[...].astype(F32) + (
        (own[...].astype(F32) + r1[...].astype(F32)) + (r2[...].astype(F32) + r3[...].astype(F32))
    )
    middle_ref[...] = middle
    r = lax.rsqrt(jnp.mean(middle * middle, axis=-1, keepdims=True) + EPS)
    ffn_in = (middle * r * gains[8:9, :]).astype(BF)
    rows_ref[...] = dot(d01[...], ffn_in).astype(BF)


SOURCES = 8
TILE = SOURCES * CAP


def expert_body(m, last, waits, *refs):
    refs = list(refs[waits:])
    place, cap, rows, cotangent = refs[:4]
    blocks = refs[4:9]
    refs = refs[9:]
    prev = None
    if m > 0:
        prev, refs = refs[0], refs[1:]
    out_ref, back_ref = refs[:2]
    if last:
        send_ref, (wg, wu, wd, acc) = refs[2], refs[3:]
    else:
        sums_ref, (wg, wu, wd, acc) = refs[2], refs[3:]
    step = pl.program_id(0)

    @pl.when(step == 0)
    def _():
        mine, right, left, first, second = blocks
        for k, ref in enumerate((mine, right, (first, second), left)):
            at = slice(k * 128, (k + 1) * 128)
            for half in range(2):
                piece = ref[half] if k != 2 else ref[half][0]
                rows_at = slice(half * (D // 2), (half + 1) * (D // 2))
                wg[rows_at, at] = piece[0]
                wu[rows_at, at] = piece[1]
                wd[rows_at, at] = piece[2]
        acc[...] = jnp.zeros(acc.shape, F32) if prev is None else prev[...]

    expert = place[0] >> 2
    notes = cotangent[:, 0, TOK : TOK + NOTES, :].astype(F32)
    named, high, low = (notes[:, j, :] for j in range(3))
    hits = jnp.zeros((SOURCES, TOK), F32)
    weight = jnp.zeros((SOURCES, TOK), F32)
    for k in range(TOPK):
        at = slice(k * TOK, (k + 1) * TOK)
        hit = named[:, at] == expert.astype(F32)
        hits = jnp.where(hit, 1.0, hits)
        weight = jnp.where(hit, high[:, at] + low[:, at], weight)
    earlier = jnp.where(iota((TOK, TOK), 0) < iota((TOK, TOK), 1), 1.0, 0.0).astype(BF)
    ranks = dot(hits.astype(BF), earlier)
    kept = jnp.logical_and(hits > 0.0, ranks < cap[0, expert].astype(F32))
    place_of = jnp.where(kept, ranks, -1.0)
    rank = iota((CAP, TOK), 0).astype(F32)
    picks, gates_of, grads = [], [], []
    for j in range(SOURCES):
        own = place_of[j : j + 1, :] == rank
        gate = jnp.sum(jnp.where(own, weight[j : j + 1, :], 0.0), axis=1, keepdims=True)
        pick = jnp.where(own, 1.0, 0.0).astype(BF)
        picks.append(pick)
        gates_of.append(gate)
        grads.append((dot(pick, cotangent[j, 0, 0:TOK, :]) * gate).astype(BF))
    grad = jnp.concatenate(grads, axis=0)
    row = rows[...]
    gate_of = jnp.concatenate(gates_of, axis=0)
    gate = dot(row, wg[...])
    up = dot(row, wu[...])
    sig = jax.nn.sigmoid(gate)
    silu = gate * sig
    hidden = (silu * up).astype(BF)
    weighted = (dot(hidden, wd[...], 1, 1) * gate_of).astype(BF)
    if last:
        out_ref[...] = weighted
    else:
        for j in range(SOURCES):
            out_ref[j] = dot(picks[j], weighted[j * CAP : (j + 1) * CAP], 0, 0).astype(BF)
    grad_hidden = dot(grad, wd[...])
    grad_gate = (grad_hidden * up * sig * (1.0 + gate * (1.0 - sig))).astype(BF)
    grad_up = (grad_hidden * silu).astype(BF)
    back_ref[...] = (dot(grad_gate, wg[...], 1, 1) + dot(grad_up, wu[...], 1, 1)).astype(BF)
    acc[0] += dot(row, grad_gate, 0, 0)
    acc[1] += dot(row, grad_up, 0, 0)
    acc[2] += dot(grad, hidden, 0, 0)

    @pl.when(step == pl.num_programs(0) - 1)
    def _():
        if last:
            for k in range(SHARDS):
                for j in range(3):
                    piece = acc[j, :, k * 128 : (k + 1) * 128].astype(BF)
                    send_ref[pl.ds((x_of(place) + k) & 3, 1), j] = piece[None]
        else:
            sums_ref[...] = acc[...]


def expert_call(m, micro, place, cap, rows, cotangent, blocks, prev, after=()):
    last = m == micro - 1
    tiles = SLOTS // TILE
    tile = pl.BlockSpec((TILE, D), lambda i: (i, 0))

    def fixed(dims):
        return pl.BlockSpec(dims, lambda i: (0,) * len(dims), pipeline_mode=pl.Buffered(1))

    ins = [place, cap, rows, cotangent, *blocks]
    in_specs = [
        SMEM,
        SMEM,
        tile,
        pl.BlockSpec((SOURCES, 1, TOK + NOTES, D), lambda i: (i, m, 0, 0)),
    ] + [fixed(b.shape) for b in blocks]
    ins = [*after, *ins]
    in_specs = [ANY] * len(after) + in_specs
    outs = [shape((SLOTS, D) if last else (EXPERTS, TOK, D), BF), shape((SLOTS, D), BF)]
    dense = pl.BlockSpec((SOURCES, TOK, D), lambda i: (i, 0, 0))
    out_specs = [tile if last else dense, tile]
    if m > 0:
        ins.append(prev)
        in_specs.append(fixed((3, D, F)))
    if last:
        outs.append(shape((SHARDS, 3, D, 128), BF))
        out_specs.append(fixed((SHARDS, 3, D, 128)))
    else:
        outs.append(shape((3, D, F), F32))
        out_specs.append(fixed((3, D, F)))
    return pl.pallas_call(
        functools.partial(expert_body, m, last, len(after)),
        grid=(tiles,),
        in_specs=in_specs,
        out_specs=out_specs,
        out_shape=outs,
        scratch_shapes=[pltpu.VMEM((D, F), BF)] * 3 + [pltpu.VMEM((3, D, F), F32)],
        compiler_params=pltpu.CompilerParams(
            vmem_limit_bytes=63 * 1024 * 1024, dimension_semantics=("arbitrary",)
        ),
        cost_estimate=cost(MICROSECONDS["expert"]),
        name="expert",
    )(*ins)


def returned_body(m, back, c01, middle, gains, dy, branch_ref, gain_ref):
    upstream = dot(c01[...], back[...])
    mid = middle[...]
    r = lax.rsqrt(jnp.mean(mid * mid, axis=-1, keepdims=True) + EPS)
    scaled = upstream * gains[8:9, :]
    grad = r * scaled - mid * (r * r * r) * jnp.mean(scaled * mid, axis=-1, keepdims=True)
    branch_ref[...] = (dy[m, 0:TOK, :].astype(F32) + grad).astype(BF)
    gain_ref[...] = jnp.broadcast_to(jnp.sum(upstream * mid * r, axis=0, keepdims=True), (8, D))


def block_body(micro, mixture, slots, c01, *refs):
    for m in range(micro - 1):
        refs[-1][m] = (refs[m][...] + mixture[...].astype(F32)).astype(BF)
    refs[-1][micro - 1] = (refs[micro - 1][...] + dot(c01[...], slots[...])).astype(BF)


def place_body(micro, place, order, rows, out_ref):
    given = iota((TOK, GT), 0) + TOK * x_of(place)
    for m in range(micro):
        deal = jnp.where(given == order[m], 1.0, 0.0).astype(BF)
        dealt = jnp.concatenate([rows[s, m] for s in range(SHARDS)], axis=0)
        out_ref[m] = dot(deal, dealt).astype(BF)


def attend_back_body(m, last, place, lengths, order, g0, g1, g2, g3, xr, qkv_ref, mixed, mass, w, wo, *refs):
    x, first_length = x_of(place), lengths[m, 0, 0]
    if last:
        prev_w, prev_o, gain0, gain1, *refs = refs
    o0, o1, o2, o3, given_ref, *refs = refs
    deal = given_by_dealt(order, m, x)
    branch = stack((g0, g1, g2, g3))
    given_ref[...] = dot(deal[0:TOK], branch).astype(BF)
    sum_o = dot(mixed[...], branch, 0, 0)
    grad_mixed = dot(branch, wo[...], 1, 1).astype(BF)
    qkv = qkv_ref[...]
    same = same_documents(x, first_length)
    grad_q, grad_k, grad_v = [], [], []
    for g in range(KV_HERE):
        k = qkv[:, QC + g * HEAD : QC + (g + 1) * HEAD]
        v = qkv[:, QC + KC + g * HEAD : QC + KC + (g + 1) * HEAD]
        sum_k = jnp.zeros((HEAD, GT), F32)
        sum_v = jnp.zeros((HEAD, GT), F32)
        for r in range(HEADS // KV_HEADS):
            h = g * (HEADS // KV_HEADS) + r
            q = qkv[:, h * HEAD : (h + 1) * HEAD]
            gm = grad_mixed[:, h * HEAD : (h + 1) * HEAD]
            scores = jnp.where(same, dot(q, k, 1, 1) * SCALE, MASKED)
            probs = jnp.exp(scores - mass[:, h * 32 : h * 32 + 1])
            grad_probs = dot(gm, v, 1, 1)
            sum_v += dot(gm, probs.astype(BF), 0, 0)
            weighted = probs * grad_probs
            grad_scores = weighted - probs * jnp.sum(weighted, axis=-1, keepdims=True)
            grad_scores = grad_scores.astype(BF)
            grad_q.append((dot(grad_scores, k) * SCALE).astype(BF))
            sum_k += dot(q, grad_scores, 0, 0)
        grad_k.append((sum_k * SCALE).astype(BF))
        grad_v.append(sum_v.astype(BF))
    grad_kv = jnp.concatenate(grad_k + grad_v, axis=0).astype(F32).T.astype(BF)
    grad_qkv = jnp.concatenate(grad_q + [grad_kv], axis=1)
    sum_w = dot(xr[...], grad_qkv, 0, 0)
    part = dot(grad_qkv, w[...], 1, 1).astype(BF)
    part = dot(deal, part).astype(BF)
    for k, out in enumerate((o0, o1, o2, o3)):
        out[...] = part[k * TOK : (k + 1) * TOK]
    if not last:
        sum_w_ref, sum_o_ref = refs
        sum_w_ref[...] = sum_w
        sum_o_ref[...] = sum_o
        return
    keep_ref, send_ref, all_w, all_o = refs
    c = core_of(place)
    all_w[...] = sum_w + prev_w[...]
    all_o[...] = sum_o + prev_o[...]
    gain = gain0[...] + gain1[...]
    for ref, half in ((keep_ref, c), (send_ref, 1 - c)):
        at = pl.ds(pl.multiple_of(half * 256, 256), 256)
        ref[0:D, :] = all_w[:, at].astype(ref.dtype)
        for j in range(2):
            at = pl.ds(pl.multiple_of(j * 512 + half * 256, 256), 256)
            ref[D + j * 256 : D + (j + 1) * 256, :] = all_o[:, at].astype(ref.dtype)
        tile = jnp.concatenate(
            [gain[0:1, b * 256 : (b + 1) * 256] for b in range(4)] + [jnp.zeros((12, 256), F32)], axis=0
        )
        for j in range(16):
            ref[6 * 256 + j * 16 : 6 * 256 + (j + 1) * 16, :] = tile.astype(ref.dtype)


def tokens_body(micro, tokens, gains, *refs):
    for m in range(micro):
        p0, p1, p2, p3, given = refs[5 * m : 5 * m + 5]
        upstream = (p0[...].astype(F32) + p1[...].astype(F32)) + (
            p2[...].astype(F32) + p3[...].astype(F32)
        )
        v = tokens[m].astype(F32)
        r = lax.rsqrt(jnp.mean(v * v, axis=-1, keepdims=True) + EPS)
        scaled = upstream * gains[0:1, :]
        grad = r * scaled - v * (r * r * r) * jnp.mean(scaled * v, axis=-1, keepdims=True)
        refs[-1][m] = (given[...].astype(F32) + grad).astype(BF)


def weight_sums_body(sums, *outs):
    for j in range(3):
        outs[j][0] = sums[j].astype(F32)


def weight_stack_body(a, b, c, out_ref):
    for j, ref in enumerate((a, b, c)):
        for half in range(2):
            out_ref[half, j] = ref[0, half * (D // 2) : (half + 1) * (D // 2)]


BLOCKS = 7


def split_y_body(place, keep, got, own_ref, s1, s2, s3):
    y = y_of(place)
    for b in range(BLOCKS):
        for k, ref in enumerate((own_ref, s1, s2, s3)):
            at = pl.ds(pl.multiple_of(b * 256 + ((y + k) & 3) * 64, 64), 64)
            ref[b * 64 : (b + 1) * 64, :] = (keep[at, :] + got[at, :].astype(F32)).astype(ref.dtype)


def sum_y_body(own, r1, r2, r3, out_ref):
    total = (own[...] + r1[...].astype(F32)) + (r2[...].astype(F32) + r3[...].astype(F32))
    out_ref[...] = total.astype(BF)


def split_x_body(place, own, r1, r2, r3, o_ref, own_ref, s1, s2, s3, held):
    x, z = x_of(place), z_of(place)
    for k, ref in enumerate((own, r1, r2, r3)):
        held[pl.ds((z - k) & 3, 1)] = ref[...][None]

    def total(at):
        return (held[0, at, :].astype(F32) + held[1, at, :].astype(F32)) + (
            held[2, at, :].astype(F32) + held[3, at, :].astype(F32)
        )

    gain = total(slice(384, 400))
    row = iota((16, 256), 0)
    for k, ref in enumerate((own_ref, s1, s2, s3)):
        s = (x + k) & 3
        ref[0:64, :] = total(pl.ds(pl.multiple_of(s * 64, 64), 64)).astype(BF)
        mine = jnp.sum(jnp.where(row == s, gain, 0.0), axis=0, keepdims=True)
        ref[64:80, :] = jnp.broadcast_to(mine, (16, 256)).astype(BF)
    o_ref[...] = total(slice(256, 384)).astype(BF)


def join_x_body(place, o, own, r1, r2, r3, out_ref):
    x = x_of(place)
    gain = jnp.zeros((16, 256), F32)
    for k, ref in enumerate((own, r1, r2, r3)):
        s = (x - k) & 3
        out_ref[pl.ds(pl.multiple_of(s * 64, 64), 64), :] = ref[0:64, :]
        gain += ref[64:80, :].astype(F32)
    out_ref[256:384, :] = o[...]
    high = gain.astype(BF).astype(F32)
    halves = jnp.where(iota((16, 256), 0) < 8, high, gain - high)
    out_ref[384:400, :] = halves.astype(BF)


def join_y_body(place, own, r1, r2, r3, out_ref):
    rows = own.shape[0]
    for k, ref in enumerate((own, r1, r2, r3)):
        s = (y_of(place) + k) & 3
        out_ref[pl.ds(pl.multiple_of(s * rows, rows), rows), :] = ref[...]


def weights_body(
    place, own, got, wq, wk, wv, gain, q_ref, k_ref, v_ref, o_ref, gain_ref, gain_ffn_ref
):
    c = core_of(place)
    halves = jnp.where(c == 0, own[384:400, :].astype(F32), got[384:400, :].astype(F32))
    gain_ffn_ref[...] = halves[0:1] + halves[8:9]
    scale = gain[...]
    total = jnp.zeros((ROWS_HERE, 1), F32)

    def piece(ref, b):
        return jnp.concatenate(
            [ref[j * 400 + b * 64 : j * 400 + (b + 1) * 64, :] for j in range(4)], axis=0
        ).astype(F32)

    for b in range(6):
        mine, other = piece(own, b), piece(got, b)
        left = jnp.where(c == 0, mine, other)
        right = jnp.where(c == 0, other, mine)
        if b < 4:
            q_ref[:, b * QC : (b + 1) * QC] = left * scale
            k_ref[:, b * KC : (b + 1) * KC] = right[:, 0:KC] * scale
            v_ref[:, b * KC : (b + 1) * KC] = right[:, KC : 2 * KC] * scale
            total += jnp.sum(
                left * wq[:, b * QC : (b + 1) * QC].astype(F32), axis=1, keepdims=True
            )
            total += jnp.sum(
                right[:, 0:KC] * wk[:, b * KC : (b + 1) * KC].astype(F32), axis=1, keepdims=True
            )
            total += jnp.sum(
                right[:, KC : 2 * KC] * wv[:, b * KC : (b + 1) * KC].astype(F32),
                axis=1,
                keepdims=True,
            )
        else:
            o_ref[:, (b - 4) * 512 : (b - 4) * 512 + 256] = left
            o_ref[:, (b - 4) * 512 + 256 : (b - 3) * 512] = right
    gain_ref[...] = jnp.broadcast_to(total, (ROWS_HERE, 128)).T[0:1]


def finish_body(micro, place, order, block_rows, own, got, wq, wk, wv, gain, block_ref, *outs):
    weights_body(place, own, got, wq, wk, wv, gain, *outs)
    place_body(micro, place, order, block_rows, block_ref)


def from_right(v, k):
    return lax.ppermute(v, "shard", [(i, (i - k) % SHARDS) for i in range(SHARDS)])


def to_right(v, k):
    return lax.ppermute(v, "shard", [(i, (i + k) % SHARDS) for i in range(SHARDS)])


def gather_x(v):
    return [v] + [from_right(v, k) for k in (1, 2, 3)]


def gather_ring(v):
    half = v.shape[0] // 2
    right, left = from_right(v, 1), from_right(v, 3)
    return [v, right, left, from_right(right[:half], 1), from_right(left[half:], 3)]


def hold(arrays, *others):
    count = len(arrays)
    return pl.pallas_call(
        lambda *refs: None,
        out_shape=[shape(v.shape, v.dtype) for v in arrays],
        in_specs=[ANY] * (count + len(others)),
        out_specs=[ANY] * count,
        input_output_aliases={i: i for i in range(count)},
        cost_estimate=cost(0),
        name="hold",
    )(*arrays, *others)


def scatter_x(blocks):
    return [blocks[0]] + [to_right(blocks[k], k) for k in (1, 2, 3)]


def along(v, step):
    pairs = []
    for i in range(EXPERTS):
        z, y, c = step(i // 8, (i // 2) % 4, i % 2)
        pairs.append((i, (z % 4) * 8 + (y % 4) * 2 + c % 2))
    return lax.ppermute(v, "expert", pairs)


def swap_core(v):
    return along(v, lambda z, y, c: (z, y, 1 - c))


def sum_over_experts(v):
    return lax.psum_scatter(v, "expert", scatter_dimension=0, tiled=True)


def exchange(v):
    return lax.all_to_all(v, "expert", split_axis=0, concat_axis=0, tiled=True)


def per_device(
    tokens,
    cotangent,
    order,
    lengths,
    routes,
    gate_weights,
    capacity,
    gain_attn,
    w_query,
    w_key,
    w_value,
    w_out,
    gain_ffn,
    w_gate,
    w_up,
    w_down,
):
    micro = tokens.shape[0]
    place = lax.axis_index(("expert", "shard")).astype(I32).reshape(1)
    cap = capacity.reshape(1, EXPERTS)
    experts = jnp.swapaxes(routes, 1, 2)
    gates = jnp.swapaxes(gate_weights, 1, 2)

    cot_rows = gather_x(cotangent)
    *packs, tokens_first = run(
        "pack",
        pack_body,
        [shape((ROWS_HERE + 16, COLS), BF)] * 4 + [shape((TOK, D), BF)],
        [
            place,
            w_query,
            w_key,
            w_value,
            jnp.concatenate([gain_attn, gain_ffn]).reshape(1, -1),
            tokens,
        ],
        smem=(0,),
    )
    pack_done = tokens_first
    waited = hold([*packs, tokens_first], *cot_rows[1:])
    packs, tokens_first = waited[:SHARDS], waited[SHARDS]
    token_rows = gather_x(tokens_first)
    packs = [packs[0]] + [from_right(packs[k], k) for k in (1, 2, 3)]
    routed = run(
        "route",
        functools.partial(route_body, micro),
        [shape((TOK, D), BF)] * (micro - 1)
        + [shape((TOK, SLOTS), BF), shape((SLOTS, TOK), BF)] * micro,
        [experts, cap, tokens],
        after=[pack_done],
    )
    token_copies, routed = routed[: micro - 1], routed[micro - 1 :]
    routed = [routed[2 * m : 2 * m + 2] for m in range(micro)]

    weights = run(
        "weight_stack",
        weight_stack_body,
        [shape((2, 3, D // 2, 128), BF)],
        [w_gate, w_up, w_down],
        after=routed[0][:1],
    )[0]
    attended, left, reached = [], [], []
    w_qkv = gains = weight_blocks = None

    dealt_cot = run(
        "deal",
        functools.partial(deal_body, micro),
        [shape((micro, TOK + NOTES, D), BF)],
        [place, order, experts, gates, *cot_rows],
        smem=(0,),
        after=[pack_done, routed[0][0]],
    )[0]
    cot_all = lax.all_gather(dealt_cot, "expert", axis=0)
    for m in range(micro):
        first = m == 0
        if not first:
            token_rows = later_rows
            weight_blocks = gather_ring(hold([weights], *token_rows[1:])[0])
        outs = [shape((TOK, D), BF)] * 5 + [
            shape((GT, D), BF),
            shape((GT, COLS), BF),
            shape((GT, QC), BF),
            shape((GT, 128), F32),
        ]
        if first:
            outs += [shape((D, COLS), BF), shape((16, D), F32)]
        result = run(
            "attend",
            functools.partial(attend_body, m),
            outs,
            [place, lengths, order, *token_rows, w_out, *(packs if first else (w_qkv, gains))],
            smem=(0, 1),
            after=[dealt_cot] if first else [],
        )
        if first:
            w_qkv, gains = result[9:]
        attended.append(result[:9])
        parts = scatter_x(result[:4])
        if first:
            later_rows = gather_x(hold([token_copies[m]], parts[1])[0])
        left.append(
            run(
                "leave",
                leave_body,
                [shape((TOK, D), F32), shape((SLOTS, D), BF)],
                [*parts, result[4], gains, routed[m][1]],
                after=[weights, *later_rows[1:]] if first else weight_blocks[1:3],
            )
        )
        reached.append(exchange(left[m][1]))

    backs, mixtures, sums = [], [], None
    for m in range(micro):
        result = expert_call(
            m,
            micro,
            place,
            cap,
            reached[m],
            cot_all,
            weight_blocks,
            sums,
            after=[left[-1][1]] if m == 0 else [],
        )
        if m < micro - 1:
            dense, back = hold(result[:2], reached[-1])
            mixtures.append(sum_over_experts(dense.reshape(-1, D)))
        else:
            last_out, back = result[0], hold([result[1]], backs[m - 1])[0]
        backs.append(exchange(back))
        sums = result[2]

    sum_w = sum_o = None
    gain_sums, grad_parts = [], []
    for m in range(micro):
        last = m == micro - 1
        branch, gain_sum = run(
            "returned",
            functools.partial(returned_body, m),
            [shape((TOK, D), BF), shape((8, D), F32)],
            [backs[m], routed[m][0], left[m][0], gains, dealt_cot],
            after=() if m == 0 else (sum_w, *grad_parts[1:4]),
        )
        branch_rows = gather_x(branch)
        if last:
            mixtures.append(exchange(hold([last_out], branch)[0]))
        else:
            sums = lax.psum_scatter(
                sums.reshape(-1, 128), "shard", scatter_dimension=0, tiled=True
            )
            totals = run(
                "weight_sums",
                weight_sums_body,
                [shape((1, D, 128), F32)] * 3,
                [sums.reshape(3, D, 128)],
            )
        gain_sums.append(gain_sum)
        ins = [place, lengths, order, *branch_rows, *attended[m][5:9], w_qkv, w_out]
        out_shapes = [shape((TOK, D), BF)] * 5
        scratch = []
        if last:
            ins += [sum_w, sum_o, *gain_sums]
            out_shapes += [shape((BLOCKS * 256, 256), F32), shape((BLOCKS * 256, 256), BF)]
            scratch = [pltpu.VMEM((D, COLS), F32), pltpu.VMEM((ROWS_HERE, D), F32)]
        else:
            out_shapes += [shape((D, COLS), F32), shape((ROWS_HERE, D), F32)]
        result = run(
            "attend_back",
            functools.partial(attend_back_body, m, last),
            out_shapes,
            ins,
            smem=(0, 1),
            scratch=scratch,
        )
        sum_w, sum_o = result[5:7]
        if last:
            last_parts = result[:5]
        else:
            grad_parts += [*scatter_x(result[:4]), result[4]]

    four = [0, 1, 2, 3]
    rows = BLOCKS * 64
    split_y = run(
        "split_y",
        split_y_body,
        [shape((rows, 256), F32)] + [shape((rows, 256), BF)] * 3,
        [place, sum_w, swap_core(sum_o)],
        smem=(0,),
    )
    pieces = [split_y[0]] + [along(split_y[k], lambda z, y, c, k=k: (z, y + k, c)) for k in four[1:]]
    last_parts = [*scatter_x(last_parts[:4]), last_parts[4]]
    sum_y = run(
        "sum_y", sum_y_body, [shape((rows, 256), BF)], pieces, after=last_parts[1:4]
    )[0]
    pieces = [sum_y] + [along(sum_y, lambda z, y, c, k=k: (z + k, y, c)) for k in four[1:]]
    blocks = run(
        "block",
        functools.partial(block_body, micro),
        [shape((micro, TOK, D), BF)],
        [*mixtures, routed[-1][0], *[left[m][0] for m in range(micro)]],
        after=[sum_y],
    )[0]
    block_rows = lax.all_gather(blocks, "shard", axis=0)
    o_piece, *pieces = run(
        "split_x",
        split_x_body,
        [shape((128, 256), BF)] + [shape((80, 256), BF)] * 4,
        [place, *pieces],
        smem=(0,),
        scratch=[pltpu.VMEM((4, rows, 256), BF)],
        after=[blocks],
    )
    x_pieces = scatter_x(pieces)
    piece = run(
        "join_x",
        join_x_body,
        [shape((400, 256), BF)],
        [place, o_piece, *x_pieces],
        smem=(0,),
        after=totals[:1],
    )[0]
    grad_tokens = run(
        "tokens",
        functools.partial(tokens_body, micro),
        [shape(tokens.shape, BF)],
        [tokens, gains, *grad_parts, *last_parts],
    )[0]
    pieces = [piece] + [along(piece, lambda z, y, c, k=k: (z, y - k, c)) for k in four[1:]]
    piece = run(
        "join_y",
        join_y_body,
        [shape((1600, 256), BF)],
        [place, *pieces],
        smem=(0,),
        after=[grad_tokens],
    )[0]
    block_out, grad_query, grad_key, grad_value, grad_out, grad_gain, gain_ffn_sum = run(
        "finish",
        functools.partial(finish_body, micro),
        [
            shape(tokens.shape, BF),
            shape(w_query.shape, F32),
            shape(w_key.shape, F32),
            shape(w_value.shape, F32),
            shape(w_out.shape, F32),
            shape((1, ROWS_HERE), F32),
            shape((1, ROWS_HERE), F32),
        ],
        [
            place,
            order,
            block_rows,
            piece,
            swap_core(piece),
            w_query,
            w_key,
            w_value,
            gain_attn.astype(F32).reshape(-1, 1),
        ],
        smem=(0,),
    )

    return (
        block_out,
        grad_tokens,
        grad_gain.reshape(-1),
        grad_query,
        grad_key,
        grad_value,
        grad_out,
        gain_ffn_sum.reshape(-1),
        *totals,
    )


def solution(mesh):
    return jax.shard_map(
        per_device,
        mesh=mesh,
        in_specs=(
            P(None, ("expert", "shard"), None),
            P(None, ("expert", "shard"), None),
            P(None, "expert", None),
            P(None, "expert", None),
            P(None, ("expert", "shard"), None),
            P(None, ("expert", "shard"), None),
            P(),
            P("shard"),
            P("shard", None),
            P("shard", None),
            P("shard", None),
            P("shard", None),
            P("shard"),
            P("expert", None, "shard"),
            P("expert", None, "shard"),
            P("expert", None, "shard"),
        ),
        out_specs=(
            P(None, ("expert", "shard"), None),
            P(None, ("expert", "shard"), None),
            P("shard"),
            P("shard", None),
            P("shard", None),
            P("shard", None),
            P("shard", None),
            P("shard"),
            P("expert", None, "shard"),
            P("expert", None, "shard"),
            P("expert", None, "shard"),
        ),
        check_vma=False,
    )
```
